32 devices in a mesh: wide: 8 (over z, y), narrow: 4 (over x, core).
Axes of the slice: x: 2, y: 2, z: 4, core: 2. Of those that a mesh axis runs over, the one named last changes fastest.
Arguments:
- inputs: bfloat16 [8192, 2048], P(('wide', 'narrow')), may hold values from -6 to 6
- out_grad: bfloat16 [8192, 2048], P(('wide', 'narrow')), may hold values from -6 to 6
- seq_lengths: int32 [10], replicated, may hold values from 1 to 2048, 8192 in all
- decay_rate: float32 [16], replicated, may hold values from 0.00012207031 to 0.05
- attn_in: float32 [2048, 8192], P(('wide', 'narrow')), may hold values from -0.125 to 0.125
- attn_out: float32 [2048, 2048], P(('wide', 'narrow')), may hold values from -0.125 to 0.125
- sglu_in: float32 [2, 2048, 5632], P(None, 'wide', 'narrow'), may hold values from -0.125 to 0.125
- sglu_out: float32 [5632, 2048], P('narrow', 'wide'), may hold values from -0.078125 to 0.078125
- mom_attn_in: float32 [2048, 8192], P(('wide', 'narrow')), may hold values from -512 to 512
- mom_attn_out: float32 [2048, 2048], P(('wide', 'narrow')), may hold values from -512 to 512
- mom_sglu_in: float32 [2, 2048, 5632], P(None, 'wide', 'narrow'), may hold values from -512 to 512
- mom_sglu_out: float32 [5632, 2048], P('narrow', 'wide'), may hold values from -512 to 512
- avg_attn_in: float32 [2048, 8192], P(('wide', 'narrow')), may hold values from -0.125 to 0.125
- avg_attn_out: float32 [2048, 2048], P(('wide', 'narrow')), may hold values from -0.125 to 0.125
- avg_sglu_in: float32 [2, 2048, 5632], P(None, 'wide', 'narrow'), may hold values from -0.125 to 0.125
- avg_sglu_out: float32 [5632, 2048], P('narrow', 'wide'), may hold values from -0.078125 to 0.078125
Outputs:
- output: float32 [8192, 2048], P(('wide', 'narrow'))
- input_grad: float32 [8192, 2048], P(('wide', 'narrow'))
- new_mom_attn_in: float32 [2048, 8192], P(('wide', 'narrow'))
- new_mom_attn_out: float32 [2048, 2048], P(('wide', 'narrow'))
- new_mom_sglu_in: float32 [2, 2048, 5632], P(None, 'wide', 'narrow')
- new_mom_sglu_out: float32 [5632, 2048], P('narrow', 'wide')
- new_attn_in: float32 [2048, 8192], P(('wide', 'narrow'))
- new_attn_out: float32 [2048, 2048], P(('wide', 'narrow'))
- new_sglu_in: float32 [2, 2048, 5632], P(None, 'wide', 'narrow')
- new_sglu_out: float32 [5632, 2048], P('narrow', 'wide')
- new_avg_attn_in: float32 [2048, 8192], P(('wide', 'narrow'))
- new_avg_attn_out: float32 [2048, 2048], P(('wide', 'narrow'))
- new_avg_sglu_in: float32 [2, 2048, 5632], P(None, 'wide', 'narrow')
- new_avg_sglu_out: float32 [5632, 2048], P('narrow', 'wide')
The draws below stay inside these ranges and needn't reach their ends.
Inputs may be any that keep to these rules, and one draw needn't show every extreme that they name: `seq_lengths`: the lengths sum to 8192; the largest is exactly 2048.
All inputs are finite; a program needn't handle non-finite values.
Results may differ from the reference program's by a relative error of at most 0.012.
Values may be sent and summed in bfloat16 or wider, within the bound.
No kernel may reach another device: no remote copies, remote signals or barrier semaphores. Data moves between devices by JAX's collectives and lax.ppermute only.
A program may use at most 384 MiB of HBM per device.

```python
import math
import jax
import jax.numpy as jnp
import numpy as np
from jax import lax

D = 2048
H = 16
HD = 128
FF = 5632
BLOCK = 256
TOK_DEV = 256
NSEQ = 10
TOKENS = 8192
LONGEST = 2048
N_WIDE = 8
N_NARROW = 4


def level_of(key, shape, shards, least, largest):
    def one(axis_at, parts):
        draws = jax.random.uniform(jax.random.fold_in(jax.random.fold_in(key, 6), axis_at), (parts,), jnp.float32, least / len(shards), largest / len(shards))
        return jnp.repeat(jnp.exp(draws), shape[axis_at] // parts).reshape((-1,) + (1,) * (len(shape) - axis_at - 1))

    gain = one(*shards[0])
    for cut in shards[1:]:
        gain = gain * one(*cut)
    return gain


def split_up(amount, total, limit, lean):
    weights = [(1 << 20) // math.isqrt(standing ** lean) + 1 for standing in range(2, amount + 1)]
    spare, holding = total - limit - (amount - 1), [1] * (amount - 1)
    while spare > 0:
        movable = [i for i in range(amount - 1) if holding[i] < limit]
        mass, left = sum([weights[i] for i in movable]), spare
        for i in movable:
            addition = min(limit - holding[i], max(1, left * weights[i] // mass), spare)
            holding[i] = holding[i] + addition
            spare = spare - addition
    return np.array([limit] + holding)


def uneven(key, number_of, total, most, skew):
    if number_of == 2:
        one = jax.random.randint(key, (), max(1, total - most), min(most, total - 1) + 1)
        return jnp.stack([one, total - one])
    sizes = jnp.asarray(split_up(number_of, total, most, skew), jnp.int32)
    couples = (number_of - 1) // 2
    donor, receiver = sizes[1:1 + 2 * couples:2], sizes[2:2 + 2 * couples:2]
    margin = jnp.minimum(donor - 1, most - receiver)
    moved = jax.random.randint(jax.random.fold_in(key, 1), (couples,), 0, 1 << 20) % (margin + 1)
    sizes = sizes.at[1:1 + 2 * couples:2].set(donor - moved).at[2:2 + 2 * couples:2].set(receiver + moved)
    return sizes[jax.random.permutation(jax.random.fold_in(key, 2), number_of)]


def gaussian(rng, shape, deviation, reach, split=(), kind=jnp.bfloat16):
    array = jax.random.normal(rng, shape, jnp.float32) * deviation
    if len(split) > 0:
        array = level_of(rng, shape, split, -0.22, 0.18) * array
    return jnp.clip(array, min=-reach, max=reach).astype(kind)


def setup_inputs(seed: int = 0) -> dict:
    key_list = jax.random.split(jax.random.key(seed), 17)
    return {
        "inputs": gaussian(key_list[0], (TOKENS, D), 1.0, 6.0, ((0, 32),)),
        "out_grad": gaussian(key_list[1], (TOKENS, D), 1.0, 6.0, ((0, 32),)),
        "seq_lengths": uneven(key_list[2], NSEQ, TOKENS, LONGEST, 2).astype(jnp.int32),
        "decay_rate": jnp.clip(jnp.exp(jax.random.uniform(key_list[3], (H,), jnp.float32, math.log(0.00012207031), math.log(0.05))), 0.00012207031, 0.05),
        "attn_in": gaussian(key_list[4], (D, 4 * D), D ** -0.5, 0.125, ((0, 32),), jnp.float32),
        "attn_out": gaussian(key_list[5], (D, D), D ** -0.5, 0.125, ((0, 32),), jnp.float32),
        "sglu_in": gaussian(key_list[6], (2, D, FF), D ** -0.5, 0.125, ((1, 8), (2, 4)), jnp.float32),
        "sglu_out": gaussian(key_list[7], (FF, D), FF ** -0.5, 0.078125, ((0, 4), (1, 8)), jnp.float32),
        "mom_attn_in": gaussian(key_list[8], (D, 4 * D), ((TOK_DEV * N_WIDE * N_NARROW) ** 0.5), 512.0, ((0, 32),), jnp.float32),
        "mom_attn_out": gaussian(key_list[9], (D, D), ((TOK_DEV * N_WIDE * N_NARROW) ** 0.5), 512.0, ((0, 32),), jnp.float32),
        "mom_sglu_in": gaussian(key_list[10], (2, D, FF), ((TOK_DEV * N_WIDE * N_NARROW) ** 0.5), 512.0, ((1, 8), (2, 4)), jnp.float32),
        "mom_sglu_out": gaussian(key_list[11], (FF, D), ((TOK_DEV * N_WIDE * N_NARROW) ** 0.5), 512.0, ((0, 4), (1, 8)), jnp.float32),
        "avg_attn_in": gaussian(key_list[12], (D, 4 * D), D ** -0.5, 0.125, ((0, 32),), jnp.float32),
        "avg_attn_out": gaussian(key_list[13], (D, D), D ** -0.5, 0.125, ((0, 32),), jnp.float32),
        "avg_sglu_in": gaussian(key_list[14], (2, D, FF), D ** -0.5, 0.125, ((1, 8), (2, 4)), jnp.float32),
        "avg_sglu_out": gaussian(key_list[15], (FF, D), FF ** -0.5, 0.078125, ((0, 4), (1, 8)), jnp.float32),
    }


@jax.custom_vjp
def low(v):
    return lax.optimization_barrier(v.astype(jnp.bfloat16)).astype(jnp.float32)

@jax.custom_vjp
def low_back(v):
    return v

def low_keep(v):
    return (low(v), None)

def low_pass(kept, grad):
    return (grad,)

def back_keep(v):
    return (v, None)

def back_low(kept, grad):
    return (low(grad),)
low.defvjp(low_keep, low_pass)
low_back.defvjp(back_keep, back_low)
EPS = 1e-06
MU = 0.9
BETA = 0.8
HIGH = lax.Precision.HIGHEST

def srms(v):
    return v * lax.rsqrt(lax.optimization_barrier(jnp.mean(v * v, axis=-1, keepdims=True)) + EPS)

def matmul(left, right):
    return jnp.dot(left, right, precision=HIGH, preferred_element_type=jnp.float32)

def block_parts(seg_block, prev_seg, rate):
    length = seg_block.shape[0]
    index = jnp.arange(length).astype(jnp.float32)
    spread = index[:, None] - index[None, :]
    allowed = (spread >= 0) & (seg_block[:, None] == seg_block[None, :])
    mask = jnp.where(allowed[None], jnp.exp(-rate[:, None, None] * jnp.maximum(spread, 0.0)[None]), 0.0)
    enter = jnp.exp(-rate[None, :] * index[:, None]) * (seg_block == prev_seg).astype(jnp.float32)[:, None]
    last = seg_block[length - 1]
    leave = jnp.exp(-rate[None, :] * (length - index)[:, None]) * (seg_block == last).astype(jnp.float32)[:, None]
    carry = jnp.exp(-rate * length) * (prev_seg == last).astype(jnp.float32)
    return (mask, enter, leave, carry)

def forward(xf, w_in, w_out, w_pair, w_third, seg_ids, prev_ids, rate):
    norm1 = low(srms(xf))
    pre = low_back(matmul(norm1, low(w_in)))
    query = low(jax.nn.silu(pre[:, :D]))
    key = low(jax.nn.silu(pre[:, D:2 * D]))
    value = low(pre[:, 2 * D:3 * D])
    gate = pre[:, 3 * D:]
    blocks = TOKENS // BLOCK
    query_b = query.reshape(blocks, BLOCK, H, HD)
    key_b = key.reshape(blocks, BLOCK, H, HD)
    value_b = value.reshape(blocks, BLOCK, H, HD)
    seg_b = seg_ids.reshape(blocks, BLOCK)

    def step(state, pieces):
        qb, kb, vb, sb, pb = pieces
        mask, enter, leave, carry = block_parts(sb, pb, rate)
        scores = low_back(jnp.einsum('thd,shd->hts', qb, kb, precision=HIGH))
        weights = low(scores * mask)
        intra = jnp.einsum('hts,shd->thd', weights, vb, precision=HIGH)
        inter = jnp.einsum('thd,hde->the', qb * enter[:, :, None], state, precision=HIGH)
        new_state = carry[:, None, None] * state + jnp.einsum('thd,the->hde', kb * leave[:, :, None], vb, precision=HIGH)
        return (new_state, intra + inter)
    start_state = jnp.zeros((H, HD, HD), jnp.float32)
    _, outs = lax.scan(jax.checkpoint(step), start_state, (query_b, key_b, value_b, seg_b, prev_ids))
    attn = low_back(outs.reshape(TOKENS, D))
    mixed = low(srms(attn) * gate)
    mid = xf + low_back(matmul(mixed, low(w_out)))
    norm2 = low(srms(mid))
    first = low_back(matmul(norm2, low(w_pair[0])))
    second = low_back(matmul(norm2, low(w_pair[1])))
    product = low(first * second)
    return mid + low_back(matmul(product, low(w_third)))

def renew(weight, moment, average, grad, fan):
    step = 0.4 / math.sqrt(fan * TOKENS)
    moment_new = MU * moment + grad
    weight_new = weight - step * (grad + MU * moment_new)
    average_new = BETA * average + (1.0 - BETA) * weight_new
    return (moment_new, weight_new, average_new)

def reference(inputs, out_grad, seq_lengths, decay_rate, attn_in, attn_out, sglu_in, sglu_out, mom_attn_in, mom_attn_out, mom_sglu_in, mom_sglu_out, avg_attn_in, avg_attn_out, avg_sglu_in, avg_sglu_out):
    places = jnp.arange(TOKENS).astype(jnp.int32)
    ends = jnp.cumsum(seq_lengths).astype(jnp.int32)
    seg_ids = lax.optimization_barrier(jnp.sum((places[:, None] >= ends[None, :]).astype(jnp.int32), axis=1)).astype(jnp.int32)
    shifted = jnp.concatenate([jnp.full((1,), -1, jnp.int32), seg_ids[:-1]])
    prev_ids = shifted.reshape(TOKENS // BLOCK, BLOCK)[:, 0]
    xf = inputs.astype(jnp.float32)

    def run(xv, w_in, w_out, w_pair, w_third):
        return forward(xv, w_in, w_out, w_pair, w_third, seg_ids, prev_ids, decay_rate)
    output, pull = jax.vjp(run, xf, attn_in, attn_out, sglu_in, sglu_out)
    grad_x, grad_in, grad_out, grad_pair, grad_third = pull(out_grad.astype(jnp.float32))
    m_in, w_in_new, a_in = renew(attn_in, mom_attn_in, avg_attn_in, grad_in, D)
    m_out, w_out_new, a_out = renew(attn_out, mom_attn_out, avg_attn_out, grad_out, D)
    m_pair, w_pair_new, a_pair = renew(sglu_in, mom_sglu_in, avg_sglu_in, grad_pair, D)
    m_third, w_third_new, a_third = renew(sglu_out, mom_sglu_out, avg_sglu_out, grad_third, FF)
    return (output, grad_x, m_in, m_out, m_pair, m_third, w_in_new, w_out_new, w_pair_new, w_third_new, a_in, a_out, a_pair, a_third)
```

```python
import math

import jax
import jax.numpy as jnp
from jax import lax
from jax.sharding import Mesh
from jax.sharding import PartitionSpec as P

BLOCK = 256
EPS = 1e-06
MU = 0.9
BETA = 0.8
HIGH = lax.Precision.HIGHEST
BF = jnp.bfloat16
F32 = jnp.float32
SWAP = [(0, 1), (1, 0)]
XORS = (0, 2, 4, 6, 1, 3, 5, 7)


def dot(a, b, dims=((1,), (0,))):
    return lax.dot_general(a, b, (dims, ((), ())), preferred_element_type=F32)


def inverse_rms(v):
    return lax.rsqrt(jnp.mean(v * v, axis=-1, keepdims=True) + EPS)


def srms_back(v, grad):
    r = inverse_rms(v)
    return r * grad - v * (r * r * r) * jnp.mean(grad * v, axis=-1, keepdims=True)


def renew(weight, moment, average, grad, fan, tokens):
    step = 0.4 / math.sqrt(fan * tokens)
    moment_new = MU * moment + grad
    weight_new = weight - step * (grad + MU * moment_new)
    average_new = BETA * average + (1.0 - BETA) * weight_new
    return (moment_new, weight_new, average_new)


class Square:
    def __init__(self):
        self.tp = ("y", "x", "c")
        self.fs = ("z",)
        self.size = 8
        self.groups = 4

    def begin(self):
        self.z = lax.axis_index("z")
        self.y = lax.axis_index("y")
        self.c = lax.axis_index("c")
        self.p = lax.axis_index(self.tp)
        self.q = self.p // 2
        self.group = self.z
        self.slot_ids = self.p ^ jnp.array(XORS, jnp.int32)
        self.head_ids = 8 * self.c + 4 * jnp.arange(2) + self.q

    def turn(self, v):
        wide = v.shape[1] // 4
        return jnp.concatenate(
            [
                lax.dynamic_slice_in_dim(v, ((self.z - k) % 4) * wide, wide, axis=1)
                for k in range(4)
            ],
            axis=1,
        )

    def rows_all(self, a):
        half = a.shape[0] // 2
        ax = lax.ppermute(a, "x", SWAP)
        ay = lax.ppermute(a, "y", SWAP)
        d0 = lax.ppermute(ay[:half], "x", SWAP)
        d1 = lax.ppermute(ax[half:], "y", SWAP)
        chip = [a, ax, ay, jnp.concatenate([d0, d1])]
        other = [lax.ppermute(v, "c", SWAP) for v in chip]
        return jnp.concatenate(chip + other)

    def rows_sum(self, part, kind=BF):
        rows = part.shape[0] // 8
        half = rows // 2
        keep, give = part[: 4 * rows], part[4 * rows :]
        got = lax.ppermute(give.astype(kind), "c", SWAP)
        total = keep.astype(F32) + got.astype(F32)
        s0, s2, s4, s6 = [total[i * rows : (i + 1) * rows] for i in range(4)]
        s6 = s6.astype(kind)
        u = lax.ppermute(s6[:half], "x", SWAP)
        v = lax.ppermute(s6[half:], "y", SWAP)
        s4 = jnp.concatenate([s4[:half] + u.astype(F32), s4[half:]]).astype(kind)
        s2 = jnp.concatenate([s2[:half], s2[half:] + v.astype(F32)]).astype(kind)
        return (
            s0
            + lax.ppermute(s2, "x", SWAP).astype(F32)
            + lax.ppermute(s4, "y", SWAP).astype(F32)
        )

    def planes_all(self, a):
        up = lambda v, s: lax.ppermute(v, "z", [(i, i + 1) for i in range(s, 3)])
        down = lambda v, s: lax.ppermute(v, "z", [(3 - i, 2 - i) for i in range(s, 3)])
        up1, down1 = up(a, 0), down(a, 0)
        up2, down2 = up(up1, 1), down(down1, 1)
        up3, down3 = up(up2, 2), down(down2, 2)
        return [
            a,
            jnp.where(self.z >= 1, up1, down3),
            jnp.where(self.z >= 2, up2, down2),
            jnp.where(self.z >= 3, up3, down1),
        ]

    def planes_sum(self, g):
        up = lambda v, s: lax.ppermute(v.astype(BF), "z", [(i, i + 1) for i in range(s)])
        down = lambda v, s: lax.ppermute(v.astype(BF), "z", [(3 - i, 2 - i) for i in range(s)])
        f = lambda v: v.astype(F32)
        u, d = up(g[1], 1), down(g[3], 1)
        u, d = up(f(g[2]) + f(u), 2), down(f(g[2]) + f(d), 2)
        u, d = up(f(g[3]) + f(u), 3), down(f(g[1]) + f(d), 3)
        return f(g[0]) + f(u) + f(d)

    def by_plane(self, slots):
        stack = jnp.stack(slots)
        return jnp.take(stack, (self.z - jnp.arange(4)) % 4, axis=0)

    def attn_in(self, w):
        rows = w.shape[0]
        view = w.reshape(rows, 4, 2, 2, 4, 128).transpose(4, 2, 0, 1, 3, 5)
        mine = lax.all_to_all(view.reshape(8, rows, 1024), self.tp, 0, 0, tiled=True)
        return jnp.concatenate(self.planes_all(mine.reshape(8 * rows, 1024)))

    def attn_in_back(self, g):
        rows = g.shape[0] // 4
        total = self.planes_sum([g[k * rows : (k + 1) * rows] for k in range(4)])
        view = total.astype(BF).reshape(8, rows // 8, 1024)
        mine = lax.all_to_all(view, self.tp, 0, 0, tiled=True)
        mine = mine.reshape(4, 2, rows // 8, 4, 2, 128).transpose(2, 3, 1, 4, 0, 5)
        return mine.reshape(rows // 8, 8192).astype(F32)

    def attn_out(self, w):
        planes = self.by_plane(self.planes_all(w))
        mine = lax.dynamic_slice_in_dim(planes, 2 * self.c, 2)
        give = lax.dynamic_slice_in_dim(planes, 2 * (1 - self.c), 2)
        got = lax.ppermute(give, "c", SWAP)
        first = self.c == 0
        pair = jnp.stack([jnp.where(first, mine, got), jnp.where(first, got, mine)], axis=1)
        return pair.reshape(4 * w.shape[0], w.shape[1])

    def attn_out_back(self, g):
        rows = g.shape[0] // 4
        halves = g.astype(BF).reshape(2, 2, rows, g.shape[1])
        first = self.c == 0
        keep = jnp.where(first, halves[:, 0], halves[:, 1])
        give = jnp.where(first, halves[:, 1], halves[:, 0])
        got = lax.ppermute(give, "c", SWAP)
        planes = jnp.concatenate([jnp.where(first, keep, got), jnp.where(first, got, keep)])
        slots = self.by_plane([planes[k] for k in range(4)])
        return self.planes_sum([slots[k] for k in range(4)])

    def sglu(self, pair, third):
        n = pair.shape[2] // 2
        first = self.y == 0

        def join(a, axis, cut):
            mine = jnp.where(first, cut(a, 0), cut(a, 1))
            give = jnp.where(first, cut(a, 1), cut(a, 0))
            got = lax.ppermute(give, "y", SWAP)
            return jnp.concatenate(
                [jnp.where(first, mine, got), jnp.where(first, got, mine)], axis=axis
            )

        both = join(pair, 1, lambda a, i: a[:, :, i * n : (i + 1) * n])
        back = join(third, 1, lambda a, i: a[i * n : (i + 1) * n])
        return both, back

    def sglu_all(self, both, back):
        return (
            jnp.concatenate(self.planes_all(both), axis=1),
            jnp.concatenate(self.planes_all(back), axis=1),
        )

    def pair_back(self, g):
        n = g.shape[1] // 4
        total = self.planes_sum([g[:, k * n : (k + 1) * n] for k in range(4)]).astype(BF)
        first = self.y == 0
        a, b = total[:, : n // 2], total[:, n // 2 :]
        mine, give = jnp.where(first, a, b), jnp.where(first, b, a)
        got = lax.ppermute(give, "y", SWAP)
        return jnp.concatenate(
            [jnp.where(first, mine, got), jnp.where(first, got, mine)], axis=2
        ).astype(F32)

    def third_back(self, g):
        n = g.shape[1] // 4
        total = self.planes_sum([g[:, k * n : (k + 1) * n] for k in range(4)]).astype(BF)
        first = self.y == 0
        a, b = total[:, : n // 2], total[:, n // 2 :]
        mine, give = jnp.where(first, a, b), jnp.where(first, b, a)
        got = lax.ppermute(give, "y", SWAP)
        return jnp.concatenate(
            [jnp.where(first, mine, got), jnp.where(first, got, mine)], axis=0
        ).astype(F32)


class Plain:
    def __init__(self, wide, narrow):
        self.tp = ("narrow",)
        self.fs = ("wide",)
        self.size = narrow
        self.groups = wide

    def begin(self):
        self.p = lax.axis_index("narrow")
        self.group = lax.axis_index("wide")
        self.slot_ids = jnp.arange(self.size, dtype=jnp.int32)

    def turn(self, v):
        return v

    def rows_all(self, a):
        return lax.all_gather(a, "narrow", axis=0, tiled=True)

    def rows_sum(self, part, kind=BF):
        return lax.psum_scatter(
            part.astype(kind), "narrow", scatter_dimension=0, tiled=True
        ).astype(F32)

    def attn_in(self, w):
        rows, cols = w.shape
        each = cols // 4 // self.size
        view = w.reshape(rows, 4, self.size, each).transpose(2, 0, 1, 3)
        view = view.reshape(self.size, rows, 4 * each)
        mine = lax.all_to_all(view, "narrow", 0, 0, tiled=True)
        mine = mine.reshape(self.size * rows, 4 * each)
        return lax.all_gather(mine, "wide", axis=0, tiled=True)

    def attn_in_back(self, g):
        cols = g.shape[1]
        total = lax.psum_scatter(g.astype(BF), "wide", scatter_dimension=0, tiled=True)
        rows = total.shape[0] // self.size
        view = total.reshape(self.size, rows, cols)
        mine = lax.all_to_all(view, "narrow", 0, 0, tiled=True)
        mine = mine.reshape(self.size, rows, 4, cols // 4).transpose(1, 2, 0, 3)
        return mine.reshape(rows, cols * self.size).astype(F32)

    def attn_out(self, w):
        whole = lax.all_gather(w, ("wide", "narrow"), axis=0, tiled=True)
        each = whole.shape[0] // self.size
        return lax.dynamic_slice_in_dim(whole, self.p * each, each)

    def attn_out_back(self, g):
        each = g.shape[0]
        whole = jnp.zeros((each * self.size, g.shape[1]), BF)
        whole = lax.dynamic_update_slice_in_dim(whole, g.astype(BF), self.p * each, 0)
        return lax.psum_scatter(
            whole, ("wide", "narrow"), scatter_dimension=0, tiled=True
        ).astype(F32)

    def sglu(self, pair, third):
        return pair, third

    def sglu_all(self, both, back):
        return (
            lax.all_gather(both, "wide", axis=1, tiled=True),
            lax.all_gather(back, "wide", axis=1, tiled=True),
        )

    def pair_back(self, g):
        return lax.psum_scatter(g.astype(BF), "wide", scatter_dimension=1, tiled=True).astype(F32)

    third_back = pair_back


def per_device(
    plan,
    inputs,
    out_grad,
    seq_lengths,
    decay_rate,
    attn_in,
    attn_out,
    sglu_in,
    sglu_out,
    mom_attn_in,
    mom_attn_out,
    mom_sglu_in,
    mom_sglu_out,
    avg_attn_in,
    avg_attn_out,
    avg_sglu_in,
    avg_sglu_out,
):
    plan.begin()
    rows, width = inputs.shape
    heads = decay_rate.shape[0]
    hd = width // heads
    size = plan.size
    own = heads // size
    cols = own * hd
    group_rows = size * rows
    tokens = group_rows * plan.groups
    fan_third = sglu_out.shape[0] * lax.axis_size(plan.narrow)

    ends = jnp.cumsum(seq_lengths)

    def seg_at(place):
        mark = jnp.sum((place[..., None] >= ends).astype(jnp.int32), axis=-1)
        return jnp.where(place < 0, -1, mark)

    first_block = plan.group * size
    blocks = first_block + plan.slot_ids
    seg = seg_at(blocks[:, None] * rows + jnp.arange(rows, dtype=jnp.int32)[None, :])
    prev = seg_at(blocks * rows - 1)
    last = seg[:, rows - 1]
    head_ids = plan.head_ids if hasattr(plan, "head_ids") else own * plan.p + jnp.arange(own)
    rate = jnp.take(decay_rate, head_ids)

    w_out = plan.attn_out(attn_out.astype(BF))
    w_in = plan.attn_in(attn_in.astype(BF))
    both, back = plan.sglu(sglu_in.astype(BF), sglu_out.astype(BF))
    w_in, both, back = lax.optimization_barrier((w_in, both, back))
    w_pair, w_third = plan.sglu_all(both, back)

    xf = inputs.astype(F32)
    norm1 = plan.rows_all(plan.turn((xf * inverse_rms(xf)).astype(BF)))
    pre = dot(norm1, w_in)
    pre_query, pre_key = pre[:, :cols], pre[:, cols : 2 * cols]
    gate = pre[:, 3 * cols :]

    def split(v):
        return v.astype(BF).reshape(size, rows, own, hd).transpose(0, 2, 1, 3)

    query = split(jax.nn.silu(pre_query))
    key = split(jax.nn.silu(pre_key))
    value = split(pre[:, 2 * cols : 3 * cols])

    index = jnp.arange(rows).astype(F32)
    spread = index[:, None] - index[None, :]
    fade = jnp.exp(-rate[:, None, None] * jnp.maximum(spread, 0.0)[None])
    allowed = (spread >= 0)[None] & (seg[:, :, None] == seg[:, None, :])
    mask = jnp.where(allowed[:, None], fade[None], 0.0)
    enter = jnp.where(
        (seg == prev[:, None])[:, None], jnp.exp(-rate[:, None] * index[None])[None], 0.0
    )[..., None]
    leave = jnp.where(
        (seg == last[:, None])[:, None], jnp.exp(-rate[:, None] * (rows - index)[None])[None], 0.0
    )[..., None]

    def reach(gap, same):
        return jnp.where(
            same & (gap >= 0), jnp.exp(-rate[:, None, None] * (rows * jnp.maximum(gap, 0))), 0.0
        )

    inner = reach(
        (blocks[:, None] - blocks[None, :] - 1).astype(F32)[None],
        (prev[:, None] == last[None, :])[None],
    )
    border = seg_at((first_block + size) * rows - 1)
    out_reach = reach(
        (first_block + size - 1 - blocks).astype(F32)[None, None], (last == border)[None, None]
    )[:, 0]
    entry = seg_at(first_block * rows - 1)
    in_reach = reach((blocks - first_block).astype(F32)[None, None], (prev == entry)[None, None])[
        :, 0
    ]
    longest = tokens // 4
    hops = min(-(-longest // group_rows), plan.groups - 1)

    def hop_factor(j, ahead):
        if ahead:
            here, there = border, seg_at((first_block + j * size) * rows - 1)
        else:
            here, there = entry, seg_at((first_block - (j - 1) * size) * rows - 1)
        return jnp.where(here == there, jnp.exp(-rate * ((j - 1) * group_rows)), 0.0)

    def bring(total, ahead):
        n = plan.groups
        got = jnp.zeros_like(total)
        for j in range(1, hops + 1):
            pairs = [(i + j, i) if ahead else (i, i + j) for i in range(n - j)]
            part = lax.ppermute(total, plan.fs, pairs)
            got = got + hop_factor(j, ahead)[:, None, None] * part
        return got

    term = jnp.einsum(
        "bhtd,bhte->bhde", key.astype(F32) * leave, value.astype(F32), precision=HIGH
    )
    leaving = jnp.einsum("hb,bhde->hde", out_reach, term, precision=HIGH)
    entering = bring(leaving, False)
    state = jnp.einsum("hbc,chde->bhde", inner, term, precision=HIGH) + (
        in_reach.T[:, :, None, None] * entering[None]
    )
    scores = jnp.einsum("bhtd,bhsd->bhts", query, key, preferred_element_type=F32)
    weights = (scores * mask).astype(BF)
    attn = jnp.einsum("bhts,bhsd->bhtd", weights, value, preferred_element_type=F32) + jnp.einsum(
        "bhtd,bhde->bhte", query.astype(F32) * enter, state, precision=HIGH
    )
    attn = attn.transpose(0, 2, 1, 3).reshape(group_rows, cols)
    branch = plan.rows_sum(dot((attn * gate).astype(BF), w_out))
    square = plan.rows_sum(jnp.sum(attn * attn, axis=1), F32)
    r_attn = lax.rsqrt(square / width + EPS)[:, None]
    mid = xf + r_attn * branch
    r_mid = inverse_rms(mid)
    norm2 = plan.rows_all(plan.turn((mid * r_mid).astype(BF)))
    grad_rows = plan.rows_all(plan.turn(out_grad))

    first = dot(norm2, w_pair[0])
    second = dot(norm2, w_pair[1])
    product = (first * second).astype(BF)
    grad_prod = dot(grad_rows, w_third, ((1,), (1,)))
    grad_first = (grad_prod * second).astype(BF)
    grad_second = (grad_prod * first).astype(BF)
    grad_norm2 = plan.rows_sum(
        dot(grad_first, w_pair[0], ((1,), (1,))) + dot(grad_second, w_pair[1], ((1,), (1,)))
    )
    grad_third = dot(product, grad_rows, ((0,), (0,))).astype(BF)
    grad_pair = jnp.stack(
        [dot(norm2, grad_first, ((0,), (0,))), dot(norm2, grad_second, ((0,), (0,)))]
    ).astype(BF)
    sum_third = plan.third_back(grad_third)
    sum_pair = plan.pair_back(grad_pair)
    output = mid + plan.turn(plan.rows_sum(dot(product, w_third)))

    grad_mid = out_grad.astype(F32) + srms_back(mid, plan.turn(grad_norm2))
    grad_branch = grad_mid.astype(BF)
    inward = jnp.mean(grad_branch.astype(F32) * branch, axis=1, keepdims=True)
    grad_branch = plan.rows_all(grad_branch)
    scales = plan.rows_all(jnp.concatenate([r_attn, r_attn * r_attn * r_attn * inward], axis=1))
    r_rows, pull_rows = scales[:, :1], scales[:, 1:]
    grad_mixed = dot(grad_branch, w_out, ((1,), (1,)))
    normed = r_rows * attn
    mixed = (normed * gate).astype(BF)
    grad_wout = dot(mixed, grad_branch, ((0,), (0,)))
    grad_gate = grad_mixed * normed
    grad_attn = split(r_rows * (grad_mixed * gate) - attn * pull_rows)
    d_term = jnp.einsum(
        "bhtd,bhte->bhde", query.astype(F32) * enter, grad_attn.astype(F32), precision=HIGH
    )
    d_leaving = jnp.einsum("hb,bhde->hde", in_reach, d_term, precision=HIGH)
    d_entering = bring(d_leaving, True)
    later = jnp.einsum("hcb,chde->bhde", inner, d_term, precision=HIGH) + (
        out_reach.T[:, :, None, None] * d_entering[None]
    )
    grad_w = jnp.einsum("bhte,bhse->bhts", grad_attn, value, preferred_element_type=F32)
    grad_s = (grad_w * mask).astype(BF)
    grad_query = jnp.einsum(
        "bhts,bhsd->bhtd", grad_s, key, preferred_element_type=F32
    ) + enter * jnp.einsum("bhte,bhde->bhtd", grad_attn.astype(F32), state, precision=HIGH)
    grad_key = jnp.einsum(
        "bhts,bhtd->bhsd", grad_s, query, preferred_element_type=F32
    ) + leave * jnp.einsum("bhse,bhde->bhsd", value.astype(F32), later, precision=HIGH)
    grad_value = jnp.einsum(
        "bhts,bhte->bhse", weights, grad_attn, preferred_element_type=F32
    ) + leave * jnp.einsum("bhsd,bhde->bhse", key.astype(F32), later, precision=HIGH)

    def merge(v):
        return v.transpose(0, 2, 1, 3).reshape(group_rows, cols)

    sig_query = jax.nn.sigmoid(pre_query)
    sig_key = jax.nn.sigmoid(pre_key)
    slope_query = sig_query * (1.0 + pre_query * (1.0 - sig_query))
    slope_key = sig_key * (1.0 + pre_key * (1.0 - sig_key))
    grad_pre = jnp.concatenate(
        [
            merge(grad_query) * slope_query,
            merge(grad_key) * slope_key,
            merge(grad_value),
            grad_gate,
        ],
        axis=1,
    ).astype(BF)
    grad_win = dot(norm1, grad_pre, ((0,), (0,))).astype(BF)
    grad_norm1 = plan.turn(plan.rows_sum(dot(grad_pre, w_in, ((1,), (1,)))))
    sum_out = plan.attn_out_back(grad_wout)
    sum_in = plan.attn_in_back(grad_win)
    input_grad = grad_mid + srms_back(xf, grad_norm1)

    m_in, w_in_new, a_in = renew(attn_in, mom_attn_in, avg_attn_in, sum_in, width, tokens)
    m_out, w_out_new, a_out = renew(attn_out, mom_attn_out, avg_attn_out, sum_out, width, tokens)
    m_pair, w_pair_new, a_pair = renew(sglu_in, mom_sglu_in, avg_sglu_in, sum_pair, width, tokens)
    m_third, w_third_new, a_third = renew(
        sglu_out, mom_sglu_out, avg_sglu_out, sum_third, fan_third, tokens
    )
    return (
        output,
        input_grad,
        m_in,
        m_out,
        m_pair,
        m_third,
        w_in_new,
        w_out_new,
        w_pair_new,
        w_third_new,
        a_in,
        a_out,
        a_pair,
        a_third,
    )


def solution(mesh):
    wide, narrow = mesh.shape["wide"], mesh.shape["narrow"]
    if (wide, narrow) == (8, 4):
        mesh = Mesh(mesh.devices.reshape(4, 2, 2, 2), ("z", "y", "x", "c"))
        plan, w, n = Square(), ("z", "y"), ("x", "c")
    else:
        plan, w, n = Plain(wide, narrow), ("wide",), ("narrow",)
    plan.narrow = n
    by_rows = P(w + n, None)
    pair, third = P(None, w, n), P(n, w)
    weights = (by_rows, by_rows, pair, third)

    def run(*args):
        return per_device(plan, *args)

    return jax.shard_map(
        run,
        mesh=mesh,
        in_specs=(by_rows, by_rows, P(), P()) + weights * 3,
        out_specs=(by_rows, by_rows) + weights * 3,
        check_vma=False,
    )
```

```python
import math

import jax
import jax.numpy as jnp
from jax import lax
from jax.experimental import pallas as pl
from jax.experimental.layout import Layout, with_layout_constraint
from jax.experimental.pallas import tpu as pltpu
from jax.sharding import Mesh
from jax.sharding import PartitionSpec as P

BLOCK = 256
EPS = 1e-06
MU = 0.9
BETA = 0.8
HIGH = lax.Precision.HIGHEST
BF = jnp.bfloat16
F32 = jnp.float32
SWAP = [(0, 1), (1, 0)]
XORS = (0, 2, 4, 6, 1, 3, 5, 7)


def dot(a, b, dims=((1,), (0,))):
    return lax.dot_general(a, b, (dims, ((), ())), preferred_element_type=F32)


def inverse_rms(v):
    return lax.rsqrt(jnp.mean(v * v, axis=-1, keepdims=True) + EPS)


def srms_back(v, grad):
    r = inverse_rms(v)
    return r * grad - v * (r * r * r) * jnp.mean(grad * v, axis=-1, keepdims=True)


def renew(weight, moment, average, grad, fan, tokens):
    step = 0.4 / math.sqrt(fan * tokens)
    moment_new = MU * moment + grad
    weight_new = weight - step * (grad + MU * moment_new)
    average_new = BETA * average + (1.0 - BETA) * weight_new
    return (moment_new, weight_new, average_new)


ROWS = 256
HALF = 4
HD = 128
VMEM = 56 * 1024 * 1024
EXTRA = 128


def pin(v):
    return with_layout_constraint(v, Layout(major_to_minor=tuple(range(v.ndim))))


class Clock:
    def __init__(self):
        self.token = jnp.zeros((8, 128), F32)

    def now(self, *values):
        out = [lax.optimization_barrier((v, self.token))[0] for v in values]
        return out if len(out) > 1 else out[0]

    def end(self, *done):
        self.token = lax.optimization_barrier((self.token,) + done)[0]


def block_spec(shape):
    return pl.BlockSpec(shape, lambda i: (i,) + (0,) * (len(shape) - 1))


def whole_spec(a):
    return pl.BlockSpec(a.shape, lambda i: (0,) * a.ndim)


def scalar_spec():
    return pl.BlockSpec(memory_space=pltpu.SMEM)


def call(kernel, steps, ins, outs, flops):
    moved = sum(a.size * a.dtype.itemsize for a, _ in ins)
    moved += sum(math.prod(s) * jnp.dtype(d).itemsize for s, d, _ in outs)
    return pl.pallas_call(
        kernel,
        grid=(steps,),
        in_specs=[s for _, s in ins],
        out_specs=[b if isinstance(b, pl.BlockSpec) else block_spec(b) for _, _, b in outs],
        out_shape=[jax.ShapeDtypeStruct(s, d) for s, d, _ in outs],
        compiler_params=pltpu.CompilerParams(
            vmem_limit_bytes=VMEM, dimension_semantics=("arbitrary",)
        ),
        cost_estimate=pl.CostEstimate(
            flops=int(flops), bytes_accessed=int(moved), transcendentals=0
        ),
    )(*[a for a, _ in ins])


NT = ((1,), (1,))
TN = ((0,), (0,))


def fades(rate, seg_c, prev, last):
    t = lax.broadcasted_iota(jnp.int32, (ROWS, 1), 0).astype(F32)
    enter = jnp.where(seg_c == prev, jnp.exp(-rate * t), 0.0)
    leave = jnp.where(seg_c == last, jnp.exp(-rate * (ROWS - t)), 0.0)
    return enter, leave


def mask_of(rate, seg_c, seg_r):
    t = lax.broadcasted_iota(jnp.int32, (ROWS, ROWS), 0)
    s = lax.broadcasted_iota(jnp.int32, (ROWS, ROWS), 1)
    spread = (t - s).astype(F32)
    allowed = (t >= s) & (seg_c == seg_r)
    return jnp.where(allowed, jnp.exp(-rate * jnp.maximum(spread, 0.0)), 0.0)


def project(n1, w_in, seg_c, prev, last, rate):
    own = rate.shape[0]
    cols = own * HD
    parts = len(w_in)
    deep = n1.shape[1] // parts

    def kernel(*refs):
        x_ref, w_refs = refs[0], refs[1 : 1 + parts]
        seg_ref, prev_ref, last_ref, rate_ref = refs[1 + parts : 5 + parts]
        raw_ref, gate_ref, qkv_ref, term_ref = refs[5 + parts :]
        i = pl.program_id(0)
        pre = dot(x_ref[:, :deep], w_refs[0][...])
        for k in range(1, parts):
            pre = pre + dot(x_ref[:, k * deep : (k + 1) * deep], w_refs[k][...])
        pq, pk, pv = pre[:, :cols], pre[:, cols : 2 * cols], pre[:, 2 * cols : 3 * cols]
        raw_ref[...] = pre[:, : 2 * cols]
        gate_ref[...] = pre[:, 3 * cols :]
        key = (pk * jax.nn.sigmoid(pk)).astype(BF)
        value = pv.astype(BF)
        qkv_ref[:, :cols] = (pq * jax.nn.sigmoid(pq)).astype(BF)
        qkv_ref[:, cols : 2 * cols] = key
        qkv_ref[:, 2 * cols :] = value
        for j in range(own):
            _, leave = fades(rate_ref[j], seg_ref[0], prev_ref[i], last_ref[i])
            at = slice(j * HD, (j + 1) * HD)
            scaled = (key[:, at].astype(F32) * leave).astype(BF)
            term_ref[0, j] = dot(scaled, value[:, at], TN)

    n = n1.shape[0] // ROWS
    some = pl.BlockSpec((deep, 4 * cols), lambda i: (0, 0))
    ins = [(n1, block_spec((ROWS, n1.shape[1])))] + [(w, some) for w in w_in]
    ins += [(seg_c, block_spec((1, ROWS, 1)))] + [(a, scalar_spec()) for a in (prev, last, rate)]
    outs = [
        ((n * ROWS, 2 * cols), F32, (ROWS, 2 * cols)),
        ((n * ROWS, cols), F32, (ROWS, cols)),
        ((n * ROWS, 3 * cols), BF, (ROWS, 3 * cols)),
        ((n, own, HD, HD), F32, (1, own, HD, HD)),
    ]
    return call(kernel, n, ins, outs, 2 * n1.size * 4 * cols)


def attend(qkv, gate, state, w_out, seg_c, seg_r, prev, last, rate):
    own = rate.shape[0]
    cols = own * HD

    def kernel(
        qkv_ref, gate_ref, state_ref, w_ref, sc_ref, sr_ref, prev_ref, last_ref, rate_ref,
        attn_ref, branch_ref,
    ):
        i = pl.program_id(0)
        for j in range(own):
            at = slice(j * HD, (j + 1) * HD)
            q = qkv_ref[:, j * HD : (j + 1) * HD]
            k = qkv_ref[:, cols + j * HD : cols + (j + 1) * HD]
            v = qkv_ref[:, 2 * cols + j * HD : 2 * cols + (j + 1) * HD]
            enter, _ = fades(rate_ref[j], sc_ref[0], prev_ref[i], last_ref[i])
            weights = (dot(q, k, NT) * mask_of(rate_ref[j], sc_ref[0], sr_ref[0])).astype(BF)
            attn_ref[:, at] = dot(weights, v) + enter * dot(q, state_ref[0, j].astype(BF))
        attn = attn_ref[...]
        branch_ref[:, :width] = dot((attn * gate_ref[...]).astype(BF), w_ref[...]).astype(BF)
        rest = jnp.sum(attn * attn, axis=1, keepdims=True)
        lane = lax.broadcasted_iota(jnp.int32, (ROWS, EXTRA), 1)
        strip = jnp.zeros((ROWS, EXTRA), F32)
        for n in range(3):
            top = rest.astype(BF).astype(F32)
            strip = jnp.where(lane == n, top, strip)
            rest = rest - top
        branch_ref[:, width:] = strip.astype(BF)

    n = qkv.shape[0] // ROWS
    width = w_out.shape[1]
    ins = [
        (qkv, block_spec((ROWS, 3 * cols))),
        (gate, block_spec((ROWS, cols))),
        (state, block_spec((1, own, HD, HD))),
        (w_out, whole_spec(w_out)),
        (seg_c, block_spec((1, ROWS, 1))),
        (seg_r, block_spec((1, 1, ROWS))),
    ] + [(a, scalar_spec()) for a in (prev, last, rate)]
    outs = [
        ((n * ROWS, cols), F32, (ROWS, cols)),
        ((n * ROWS, width + EXTRA), BF, (ROWS, width + EXTRA)),
    ]
    return call(kernel, n, ins, outs, 2 * n * ROWS * cols * (width + 2 * ROWS))


def sglu_rows(n2, g, w_pair, w_third):
    parts = len(w_pair)
    _, hidden, deep = w_pair[0].shape
    block = 2 * ROWS

    def kernel(*refs):
        x_ref, g_ref = refs[:2]
        both, three = (refs[2 + k * parts : 2 + (k + 1) * parts] for k in range(2))
        prod_ref, prod_t, gf_t, gs_t, back_ref = refs[2 + 2 * parts :]
        first = second = grad = None
        for k in range(parts):
            at = slice(k * deep, (k + 1) * deep)
            x, gk = x_ref[:, at], g_ref[:, at]
            a, b, c = dot(x, both[k][0], NT), dot(x, both[k][1], NT), dot(gk, three[k][...], NT)
            first = a if first is None else first + a
            second = b if second is None else second + b
            grad = c if grad is None else grad + c
        prod = (first * second).astype(BF)
        gf = (grad * second).astype(BF)
        gs = (grad * first).astype(BF)
        prod_ref[...] = prod
        prod_t[...] = prod.T
        gf_t[...] = gf.T
        gs_t[...] = gs.T
        for k in range(parts):
            at = slice(k * deep, (k + 1) * deep)
            back_ref[:, at] = (dot(gf, both[k][0]) + dot(gs, both[k][1])).astype(BF)

    n = n2.shape[0] // block
    width = n2.shape[1]
    ins = [(n2, block_spec((block, width))), (g, block_spec((block, width)))]
    ins += [(w, whole_spec(w)) for w in w_pair + w_third]
    outs = [((n * block, hidden), BF, (block, hidden))]
    turned = pl.BlockSpec((hidden, block), lambda i: (0, i))
    outs += [((hidden, n * block), BF, turned)] * 3
    outs += [((n * block, width), BF, (block, width))]
    return call(kernel, n, ins, outs, 10 * n2.size * hidden)


def sglu_last(product, w_third):
    parts = len(w_third)
    deep = w_third[0].shape[1]
    block = 2 * ROWS

    def kernel(*refs):
        for k in range(parts):
            refs[-1][:, k * deep : (k + 1) * deep] = dot(refs[0][...], refs[1 + k][...]).astype(BF)

    n, width = product.shape[0] // block, parts * deep
    ins = [(product, block_spec((block, product.shape[1])))]
    ins += [(w, whole_spec(w)) for w in w_third]
    return call(
        kernel, n, ins, [((n * block, width), BF, (block, width))], 2 * product.size * width
    )[0]


def attend_back_rows(gb, w_out, attn, gate, qkv, seg_c, prev, last, rate):
    own = rate.shape[0]
    cols = own * HD
    width = w_out.shape[1]

    def kernel(
        gb_ref, w_ref, attn_ref, gate_ref, qkv_ref, sc_ref, prev_ref, last_ref, rate_ref,
        ga_ref, gg_ref, mixed_ref, term_ref,
    ):
        i = pl.program_id(0)
        extra = gb_ref[:, width : width + 8].astype(F32)
        r = extra[:, 0:1] + extra[:, 1:2] + extra[:, 2:3]
        pull = extra[:, 3:4] + extra[:, 4:5] + extra[:, 5:6]
        gm = dot(gb_ref[:, :width], w_ref[...], NT)
        attn, gate = attn_ref[...], gate_ref[...]
        normed = r * attn
        gg_ref[...] = (gm * normed).astype(BF)
        mixed_ref[...] = (normed * gate).astype(BF)
        ga = (r * (gm * gate) - attn * pull).astype(BF)
        ga_ref[...] = ga
        for j in range(own):
            enter, _ = fades(rate_ref[j], sc_ref[0], prev_ref[i], last_ref[i])
            q = qkv_ref[:, j * HD : (j + 1) * HD].astype(F32)
            term_ref[0, j] = dot((q * enter).astype(BF), ga[:, j * HD : (j + 1) * HD], TN)

    n = gb.shape[0] // ROWS
    ins = [
        (gb, block_spec((ROWS, gb.shape[1]))),
        (w_out, whole_spec(w_out)),
        (attn, block_spec((ROWS, cols))),
        (gate, block_spec((ROWS, cols))),
        (qkv, block_spec((ROWS, 3 * cols))),
        (seg_c, block_spec((1, ROWS, 1))),
    ] + [(a, scalar_spec()) for a in (prev, last, rate)]
    outs = [((n * ROWS, cols), BF, (ROWS, cols))] * 3
    outs += [((n, own, HD, HD), F32, (1, own, HD, HD))]
    return call(kernel, n, ins, outs, 2 * n * ROWS * cols * width)


def project_back(qkv, raw, ga, gg, state, later, w_in, width, seg_c, seg_r, prev, last, rate):
    own = rate.shape[0]
    cols = own * HD
    parts = len(w_in)
    deep = width // parts

    def kernel(*refs):
        qkv_ref, raw_ref, ga_ref, gg_ref, state_ref, later_ref = refs[:6]
        w_refs = refs[6 : 6 + parts]
        sc_ref, sr_ref, prev_ref, last_ref, rate_ref, gp_ref, back_ref = refs[6 + parts :]
        i = pl.program_id(0)
        for j in range(own):
            at = slice(j * HD, (j + 1) * HD)
            kt = slice(cols + j * HD, cols + (j + 1) * HD)
            vt = slice(2 * cols + j * HD, 2 * cols + (j + 1) * HD)
            q, k, v = qkv_ref[:, at], qkv_ref[:, kt], qkv_ref[:, vt]
            g = ga_ref[:, at]
            mask = mask_of(rate_ref[j], sc_ref[0], sr_ref[0])
            enter, leave = fades(rate_ref[j], sc_ref[0], prev_ref[i], last_ref[i])
            weights = (dot(q, k, NT) * mask).astype(BF)
            gs = (dot(g, v, NT) * mask).astype(BF)
            st, lt = state_ref[0, j].astype(BF), later_ref[0, j].astype(BF)
            gq = dot(gs, k) + enter * dot(g, st, NT)
            gk = dot(gs, q, TN) + leave * dot(v, lt, NT)
            gv = dot(weights, g, TN) + leave * dot(k, lt)
            rq, rk = raw_ref[:, at], raw_ref[:, kt]
            sq, sk = jax.nn.sigmoid(rq), jax.nn.sigmoid(rk)
            gp_ref[:, at] = (gq * (sq * (1.0 + rq * (1.0 - sq)))).astype(BF)
            gp_ref[:, kt] = (gk * (sk * (1.0 + rk * (1.0 - sk)))).astype(BF)
            gp_ref[:, vt] = gv.astype(BF)
        gp_ref[:, 3 * cols :] = gg_ref[...]
        for k in range(parts):
            at = slice(k * deep, (k + 1) * deep)
            back_ref[:, at] = dot(gp_ref[...], w_refs[k][...], NT).astype(BF)

    n = qkv.shape[0] // ROWS
    some = pl.BlockSpec((deep, 4 * cols), lambda i: (0, 0))
    ins = [
        (qkv, block_spec((ROWS, 3 * cols))),
        (raw, block_spec((ROWS, 2 * cols))),
        (ga, block_spec((ROWS, cols))),
        (gg, block_spec((ROWS, cols))),
        (state, block_spec((1, own, HD, HD))),
        (later, block_spec((1, own, HD, HD))),
    ] + [(w, some) for w in w_in]
    ins += [(seg_c, block_spec((1, ROWS, 1))), (seg_r, block_spec((1, 1, ROWS)))]
    ins += [(a, scalar_spec()) for a in (prev, last, rate)]
    outs = [
        ((n * ROWS, 4 * cols), BF, (ROWS, 4 * cols)),
        ((n * ROWS, width), BF, (ROWS, width)),
    ]
    return call(kernel, n, ins, outs, 2 * n * ROWS * 4 * cols * width)


def grads_by_left(left, right, cut):
    def kernel(l0, l1, r0, r1, out):
        out[0] = (dot(l0[...], r0[...], TN) + dot(l1[...], r1[...], TN)).astype(BF)

    n, cols = left[0].shape[1] // cut, right[0].shape[1]
    ins = [(a, pl.BlockSpec((a.shape[0], cut), lambda i: (0, i))) for a in left]
    ins += [(a, whole_spec(a)) for a in right]
    return call(
        kernel, n, ins, [((n, cut, cols), BF, (1, cut, cols))], 4 * left[0].size * cols
    )[0]


def grads_by_right(lefts, right, cut, width):
    count = len(lefts)

    def kernel(*refs):
        r0, r1, out = refs[2 * count :]
        for m in range(count):
            l0, l1 = refs[2 * m : 2 * m + 2]
            out[0, m] = (dot(l0[...], r0[...]) + dot(l1[...], r1[...])).astype(BF)

    n = width // cut
    tall = lefts[0][0].shape[0]
    ins = [(a, whole_spec(a)) for left in lefts for a in left]
    ins += [(a, pl.BlockSpec((a.shape[0], cut), lambda i: (0, i))) for a in right]
    outs = [((n, count, tall, cut), BF, (1, count, tall, cut))]
    return call(kernel, n, ins, outs, 4 * count * right[0].size * tall)[0]


def grads_out(left, right, width):
    def kernel(l0, l1, r0, r1, out):
        out[...] = (dot(l0[...], r0[...], TN) + dot(l1[...], r1[...], TN)).astype(BF)

    cut, tall = width // 4, left[0].shape[1]
    spec = lambda rows: pl.BlockSpec((rows, cut), lambda i: (0, i))
    ins = [(a, whole_spec(a)) for a in left] + [(a, spec(a.shape[0])) for a in right]
    return call(kernel, 4, ins, [((tall, width), BF, spec(tall))], 4 * left[0].size * width)[0]


def add_strips(width, *parts):
    total = parts[0][:, :width].astype(F32)
    for p in parts[1:]:
        total = total + p[:, :width].astype(F32)
    out = [total.astype(BF)]
    if parts[0].shape[1] > width:
        rest = 0.0
        for p in parts:
            for n in range(3):
                rest = rest + p[:, width + n : width + n + 1].astype(F32)
        lane = lax.broadcasted_iota(jnp.int32, (total.shape[0], EXTRA), 1)
        strip = jnp.zeros((total.shape[0], EXTRA), F32)
        for n in range(3):
            top = rest.astype(BF).astype(F32)
            strip = jnp.where(lane == n, top, strip)
            rest = rest - top
        out.append(strip.astype(BF))
    return out


def add_rows(a, b, width):
    n, wide = a.shape[0] // ROWS, a.shape[1]
    half = ROWS // 2

    block = pl.BlockSpec((ROWS, wide), lambda i: ((i + n - 1) % n, 0))
    one = pl.BlockSpec((half, wide), lambda i: (0, 0))

    def kernel(a_ref, b_ref, out_ref, low_ref, high_ref):
        parts = add_strips(width, a_ref[...], b_ref[...])
        for v, at in zip(parts, (slice(0, width), slice(width, wide))):
            out_ref[:, at] = v

            @pl.when(pl.program_id(0) == 0)
            def _():
                low_ref[:, at] = v[:half]
                high_ref[:, at] = v[half:]

    outs = [((n * ROWS, wide), BF, block)] + [((half, wide), BF, one)] * 2
    return call(kernel, n, [(a, block), (b, block)], outs, a.size)


def add_halves(sums, u, v, width):
    wide = sums.shape[1]
    half = ROWS // 2

    def kernel(s2_ref, s4_ref, u_ref, v_ref, to_2, to_4):
        to_2[:half] = s2_ref[:half]
        to_4[half:] = s4_ref[half:]
        two = add_strips(width, s2_ref[half:], v_ref[...])
        four = add_strips(width, s4_ref[:half], u_ref[...])
        for a, b, at in zip(two, four, (slice(0, width), slice(width, wide))):
            to_2[half:, at] = a
            to_4[:half, at] = b

    ins = [(sums, pl.BlockSpec((ROWS, wide), lambda i, k=k: (k, 0))) for k in (1, 2)]
    ins += [(u, whole_spec(u)), (v, whole_spec(v))]
    whole = pl.BlockSpec((ROWS, wide), lambda i: (0, 0))
    return call(kernel, 1, ins, [((ROWS, wide), BF, whole)] * 2, sums.size)


def cut4(v, axis):
    n = v.shape[axis] // 4
    return [lax.slice_in_dim(v, k * n, (k + 1) * n, axis=axis) for k in range(4)]


def strip_sum(v):
    strip = v[:, v.shape[1] - EXTRA :].astype(F32)
    return strip[:, 0:1] + strip[:, 1:2] + strip[:, 2:3]


def pieces(v):
    out = []
    for _ in range(3):
        top = lax.reduce_precision(v, 8, 7)
        out.append(top.astype(BF))
        v = v - top
    return out


class Places:
    def __init__(self, plan, seq_lengths, decay_rate, rows):
        size = plan.size
        group_rows = size * rows
        tokens = group_rows * plan.groups
        ends = jnp.cumsum(seq_lengths)

        def seg_at(place):
            mark = jnp.sum((place[..., None] >= ends).astype(jnp.int32), axis=-1)
            return jnp.where(place < 0, -1, mark)

        first_block = plan.group * size
        blocks = first_block + plan.slot_ids
        seg = seg_at(blocks[:, None] * rows + jnp.arange(rows, dtype=jnp.int32)[None, :])
        prev = seg_at(blocks * rows - 1)
        last = seg[:, rows - 1]
        head_ids = plan.head_ids if hasattr(plan, "head_ids") else plan.own * plan.p + jnp.arange(plan.own)
        rate = jnp.take(decay_rate, head_ids)

        def reach(gap, same):
            return jnp.where(
                same & (gap >= 0), jnp.exp(-rate[:, None, None] * (rows * jnp.maximum(gap, 0))), 0.0
            )

        inner = reach(
            (blocks[:, None] - blocks[None, :] - 1).astype(F32)[None],
            (prev[:, None] == last[None, :])[None],
        )
        border = seg_at((first_block + size) * rows - 1)
        out_reach = reach(
            (first_block + size - 1 - blocks).astype(F32)[None, None], (last == border)[None, None]
        )[:, 0]
        entry = seg_at(first_block * rows - 1)
        in_reach = reach((blocks - first_block).astype(F32)[None, None], (prev == entry)[None, None])[
            :, 0
        ]
        longest = tokens // 4
        hops = min(-(-longest // group_rows), plan.groups - 1)

        def hop_factor(j, ahead):
            if ahead:
                here, there = border, seg_at((first_block + j * size) * rows - 1)
            else:
                here, there = entry, seg_at((first_block - (j - 1) * size) * rows - 1)
            return jnp.where(here == there, jnp.exp(-rate * ((j - 1) * group_rows)), 0.0)

        def bring(total, ahead):
            n = plan.groups
            got = jnp.zeros_like(total)
            for j in range(1, hops + 1):
                pairs = [(i + j, i) if ahead else (i, i + j) for i in range(n - j)]
                part = lax.ppermute(total, plan.fs, pairs)
                got = got + hop_factor(j, ahead)[:, None, None] * part
            return got

        self.rate, self.bring = rate, bring
        self.inner, self.out_reach, self.in_reach = inner, out_reach, in_reach
        cut = lambda v: (v[:HALF], v[HALF:])
        self.cols, self.rows = cut(seg[:, :, None]), cut(seg[:, None, :])
        self.prev, self.last = cut(prev), cut(last)

    def states(self, term):
        leaving = jnp.einsum("hb,bhde->hde", self.out_reach, term, precision=HIGH)
        entering = self.bring(leaving, False)
        state = jnp.einsum("hbc,chde->bhde", self.inner, term, precision=HIGH)
        state = state + self.in_reach.T[:, :, None, None] * entering[None]
        return state[:HALF], state[HALF:]

    def states_back(self, term):
        leaving = jnp.einsum("hb,bhde->hde", self.in_reach, term, precision=HIGH)
        entering = self.bring(leaving, True)
        state = jnp.einsum("hcb,chde->bhde", self.inner, term, precision=HIGH)
        state = state + self.out_reach.T[:, :, None, None] * entering[None]
        return state[:HALF], state[HALF:]


class Square:
    def __init__(self):
        self.tp = ("y", "x", "c")
        self.fs = ("z",)
        self.size = 8
        self.groups = 4

    def begin(self):
        self.z = lax.axis_index("z")
        self.y = lax.axis_index("y")
        self.c = lax.axis_index("c")
        self.p = lax.axis_index(self.tp)
        self.q = self.p // 2
        self.group = self.z
        self.slot_ids = self.p ^ jnp.array(XORS, jnp.int32)
        self.head_ids = 8 * self.c + 4 * jnp.arange(2) + self.q

    def turn(self, v):
        wide = v.shape[1] // 4
        return jnp.concatenate(
            [
                lax.dynamic_slice_in_dim(v, ((self.z - k) % 4) * wide, wide, axis=1)
                for k in range(4)
            ],
            axis=1,
        )

    def slots(self, own, one, two, three):
        return [
            own,
            pin(jnp.where(self.z >= 1, one[0], three[1])),
            pin(jnp.where(self.z >= 2, two[0], two[1])),
            pin(jnp.where(self.z >= 3, three[0], one[1])),
        ]

    def by_y(self, mine, got, axis):
        first = self.y == 0
        parts = [jnp.where(first, mine, got), jnp.where(first, got, mine)]
        return pin(jnp.concatenate(parts, axis=axis))

    def of_y(self, one, two):
        first = self.y == 0
        return pin(jnp.where(first, one, two)), pin(jnp.where(first, two, one))


def over(axis, pairs=SWAP):
    return lambda v: pin(lax.ppermute(pin(v), axis, pairs))


to_x, to_y, to_core = over("x"), over("y"), over("c")


def spread(pair, step):
    up = over("z", [(i, i + 1) for i in range(step, 3)])
    down = over("z", [(3 - i, 2 - i) for i in range(step, 3)])
    return up(pair[0]), down(pair[1])


def gather(up, down, step):
    go_up = over("z", [(i, i + 1) for i in range(step)])
    go_down = over("z", [(3 - i, 2 - i) for i in range(step)])
    return go_up(up), go_down(down)


def plus(a, b):
    return (a.astype(F32) + b.astype(F32)).astype(BF)


def square_layer(plan, at, inputs, out_grad, attn_in, attn_out, sglu_in, sglu_out):
    rows, width = inputs.shape
    h2 = rows // 2
    cut = width // 4
    clock = Clock()
    now, end = clock.now, clock.end
    rate = at.rate

    def pick(slots, plane):
        return lax.dynamic_index_in_dim(slots, (plan.z - plane) % 4, 0, False)

    xf = inputs.astype(F32)
    n1 = pin(plan.turn((xf * inverse_rms(xf)).astype(BF)))
    og = pin(plan.turn(out_grad))
    few = attn_in.shape[0]
    view = attn_in.astype(BF).reshape(few, 4, 2, 2, 4, HD).transpose(4, 2, 0, 1, 3, 5)
    own_in = lax.all_to_all(view.reshape(8, few, -1), plan.tp, 0, 0, tiled=True)
    own_in = own_in.reshape(8 * few, -1)
    deep, across = own_in.shape
    own_out = attn_out.astype(BF)
    own_w = pin(jnp.concatenate([own_in, own_out[:, :across], own_out[:, across:]]))
    hid = sglu_in.shape[2] // 2
    three = jnp.concatenate([sglu_in.astype(BF).swapaxes(1, 2), sglu_out.astype(BF)[None]])
    my_three, to_three = plan.of_y(three[:, :hid], three[:, hid:])
    end(own_w, n1, og, to_three)

    a_w, a_n1 = now(own_w, n1)
    w1 = spread((a_w, a_w), 0)
    nx, ny, nc = to_x(a_n1), to_y(a_n1), to_core(a_n1)
    end(*w1, nx, ny, nc)

    w2 = spread(now(*w1), 1)
    ax, ay = now(nx, ny)
    nd = to_x(ay[:h2]), to_y(ax[h2:])
    nxyc = to_core(jnp.concatenate([ax, ay]))
    end(*w2, *nd, nxyc)

    w3 = spread(now(*w2), 2)
    a_og, a_three = now(og, to_three)
    gx = to_x(a_og)
    got = to_y(a_three)
    ndc = to_core(jnp.concatenate(now(*nd)))
    norm1 = pin(jnp.concatenate([n1, nx, ny, *nd])), pin(jnp.concatenate([nc, nxyc, ndc]))
    own_three = plan.by_y(my_three, got, 2)
    owns = [pin(own_three[m]) for m in range(3)]
    end(*w3, gx, *norm1, *owns)

    owns = now(*owns)
    third1 = spread((owns[2],) * 2, 0)
    w_in = plan.slots(own_w, *[now(*v) for v in (w1, w2, w3)])
    a_rate, a_og, a_gx = now(rate, og, gx)
    gy = to_y(a_og)
    crossed = to_core(jnp.concatenate([a_og, a_gx]))
    outs = jnp.stack([w[deep:] for w in w_in])
    w_mine = [pick(outs, 2 * plan.c + j) for j in (0, 1)]
    w_got = to_core(jnp.concatenate([pick(outs, 2 * (1 - plan.c) + j) for j in (0, 1)]))
    core0 = plan.c == 0
    raw, gate, qkv, term = zip(
        *[project(norm1[h], w_in, at.cols[h], at.prev[h], at.last[h], a_rate) for h in (0, 1)]
    )
    end(*third1, gy, crossed, w_got, *term)

    first1 = spread((now(owns[0]),) * 2, 0)
    a_gx, a_gy = now(gx, gy)
    gd = to_x(a_gy[:h2]), to_y(a_gx[h2:])
    w_rows = []
    for j in (0, 1):
        got = w_got[j * 2 * few : (j + 1) * 2 * few]
        for half in (jnp.where(core0, w_mine[j], got), jnp.where(core0, got, w_mine[j])):
            w_rows.append(jnp.concatenate([half[:few], half[few:]], axis=1))
    w_out = pin(jnp.concatenate(w_rows))
    state = at.states(jnp.concatenate(now(*term)))

    def attend_half(h, fade):
        return attend(
            qkv[h], gate[h], state[h], w_out, at.cols[h], at.rows[h], at.prev[h], at.last[h], fade
        )

    attn_b, give = attend_half(1, rate)
    end(*first1, *gd, give)

    second1 = spread((now(owns[1]),) * 2, 0)
    a_rate, give = now(rate, give)
    attn_a, keep = attend_half(0, a_rate)
    got = to_core(give)
    end(*second1, got, keep)

    def last_sum(own, x, y):
        return own.astype(F32) + x.astype(F32) + y.astype(F32)

    def first_step(keep, got):
        sums, low, high = add_rows(keep, got, width)
        return sums, to_x(low), to_y(high)

    def second_step(sums, u, v):
        to_2, to_4 = add_halves(sums, u, v, width)
        return to_x(to_2), to_y(to_4)

    sums, u, v = first_step(*now(keep, got))
    third2 = spread(now(*third1), 1)
    gydc = to_core(jnp.concatenate(now(gy, *gd)))
    end(u, v, *third2, gydc)

    sx, sy = second_step(sums, *now(u, v))
    first2 = spread(now(*first1), 1)
    second2 = spread(now(*second1), 1)
    g_a = pin(jnp.concatenate([og, gx, gy, *gd]))
    g_b = pin(jnp.concatenate([crossed, gydc]))
    end(sx, sy, *first2, *second2, g_a, g_b)

    third3 = spread(now(*third2), 2)
    first3 = spread(now(*first2), 2)
    sx, sy = now(sx, sy)
    branch = pin(last_sum(sums[:rows, :width], sx[:, :width], sy[:, :width]))
    square = strip_sum(sums[:rows]) + strip_sum(sx) + strip_sum(sy)
    r_attn = lax.rsqrt(square / width + EPS)
    mid = pin(xf + r_attn * branch)
    n2 = pin(plan.turn((mid * inverse_rms(mid)).astype(BF)))
    mx, my, mc = to_x(n2), to_y(n2), to_core(n2)
    w_third = plan.slots(owns[2], third1, third2, third3)
    end(mx, my, mc, *third3, *first3)

    second3 = spread(now(*second2), 2)
    ax, ay = now(mx, my)
    md = to_x(ay[:h2]), to_y(ax[h2:])
    mxyc = to_core(jnp.concatenate([ax, ay]))
    mdc = to_core(jnp.concatenate(md))
    n2_a = pin(jnp.concatenate([n2, mx, my, *md]))
    n2_b = pin(jnp.concatenate([mc, mxyc, mdc]))
    end(*second3, n2_a, n2_b)

    both = [[now(*v) for v in s] for s in ((first1, first2, first3), (second1, second2, second3))]
    w_pair = [
        pin(jnp.stack([a, b]))
        for a, b in zip(plan.slots(owns[0], *both[0]), plan.slots(owns[1], *both[1]))
    ]
    prod_b, turned_b, gf_b, gs_b, give = sglu_rows(n2_b, g_b, w_pair, w_third)
    end(give)

    give, a_n2 = now(give, n2_a)
    got = to_core(give)
    prod_a, turned_a, gf_a, gs_a, keep = sglu_rows(a_n2, g_a, w_pair, w_third)
    end(keep, got)

    sums, u, v = first_step(*now(keep, got))
    d_third = grads_by_right([(now(turned_a), turned_b)], (g_a, g_b), cut, width)[:, 0]
    end(u, v, d_third)

    sx, sy = second_step(sums, *now(u, v))
    d_third = now(d_third)
    third1 = gather(d_third[1], d_third[3], 1)
    d_pair = grads_by_right([(now(gf_a), gf_b), (gs_a, gs_b)], (n2_a, n2_b), cut, width)
    d_one = [[d_pair[k, m] for k in range(4)] for m in (0, 1)]
    ready = [v for m in (0, 1) for v in (pin(d_one[m][1]), pin(d_one[m][3]))]
    end(sx, sy, *third1, d_pair, *ready)

    ready = now(*ready)
    first1 = gather(ready[0], ready[1], 1)
    second1 = gather(ready[2], ready[3], 1)
    grad_norm2 = last_sum(sums[:rows], *now(sx, sy))
    grad_mid = pin(out_grad.astype(F32) + srms_back(mid, plan.turn(grad_norm2)))
    gb = grad_mid.astype(BF)
    inward = jnp.mean(gb.astype(F32) * branch, axis=1, keepdims=True)
    extra = pieces(r_attn) + pieces(r_attn * r_attn * r_attn * inward)
    extra.append(jnp.zeros((rows, EXTRA - len(extra)), BF))
    gb = pin(jnp.concatenate([gb] + extra, axis=1))
    bx, by, bc = to_x(gb), to_y(gb), to_core(gb)
    give = sglu_last(now(prod_b), w_third)
    keep = sglu_last(now(prod_a), w_third)

    def join(parts, up, down, k_up, k_down):
        a, b = now(up, down)
        return pin(plus(parts[k_up], a)), pin(plus(parts[k_down], b))

    ready = join(d_third, *third1, 2, 2)
    end(bx, by, bc, *first1, *second1, keep, give, *ready)

    third2 = gather(*now(*ready), 2)
    ax, ay = now(bx, by)
    bd = to_x(ay[:h2]), to_y(ax[h2:])
    bxyc = to_core(jnp.concatenate([ax, ay]))
    bdc = to_core(jnp.concatenate(bd))
    gb_a = pin(jnp.concatenate([gb, bx, by, *bd]))
    gb_b = pin(jnp.concatenate([bc, bxyc, bdc]))
    ready = join(d_one[0], *first1, 2, 2) + join(d_one[1], *second1, 2, 2)
    end(*third2, gb_a, gb_b, *ready)

    ready = now(*ready)
    first2 = gather(ready[0], ready[1], 2)
    second2 = gather(ready[2], ready[3], 2)
    o_got = to_core(now(give))
    a_rate = now(rate)
    ga, gg, mixed, d_term = zip(
        *[
            attend_back_rows(g, w_out, attn, gate[h], qkv[h], at.cols[h],
                             at.prev[h], at.last[h], a_rate)
            for h, g, attn in ((0, gb_a, attn_a), (1, gb_b, attn_b))
        ]
    )
    d_out = grads_out(mixed, (gb_a, gb_b), width)
    ready = join(d_third, *third2, 3, 1)
    end(*first2, *second2, *d_term, d_out, o_got, *ready)

    third3 = gather(*now(*ready), 3)
    o_sums, ou, ov = first_step(*now(keep, o_got))
    later = at.states_back(jnp.concatenate(now(*d_term)))

    def back_half(h, fade):
        return project_back(
            qkv[h], raw[h], ga[h], gg[h], state[h], later[h], w_in, width,
            at.cols[h], at.rows[h], at.prev[h], at.last[h], fade,
        )

    gp_b, give = back_half(1, rate)
    ready = join(d_one[0], *first2, 3, 1)
    end(*third3, ou, ov, give, *ready)

    first3 = gather(*now(*ready), 3)
    a_rate, give = now(rate, give)
    gp_a, keep = back_half(0, a_rate)
    got = to_core(give)
    parts = now(d_out).reshape(2, 2, few, width)
    o_keep = jnp.where(core0, parts[:, 0], parts[:, 1])
    o_got = to_core(jnp.where(core0, parts[:, 1], parts[:, 0]))
    ready = join(d_one[1], *second2, 3, 1)
    end(*first3, keep, got, o_got, *ready)

    second3 = gather(*now(*ready), 3)
    sums, u, v = first_step(*now(keep, got))
    d_in = grads_by_left(norm1, (now(gp_a), gp_b), cut)
    planes = jnp.concatenate([jnp.where(core0, o_keep, o_got), jnp.where(core0, o_got, o_keep)])
    planes = [pick(planes, k) for k in range(4)]
    d_w = [
        pin(jnp.concatenate([d_in[k], planes[k][:, :across], planes[k][:, across:]]))
        for k in range(4)
    ]
    end(u, v, *second3, *d_w)

    d_w = now(*d_w)
    w1 = gather(d_w[1], d_w[3], 1)
    sx, sy = second_step(sums, *now(u, v))
    sum_three = [last_sum(d_one[m][0], *now(*v)) for m, v in ((0, first3), (1, second3))]
    sum_three.append(last_sum(d_third[0], *now(*third3)))
    sum_three = jnp.stack([v.astype(BF) for v in sum_three])
    my_three, to_three = plan.of_y(sum_three[:, :, :rows], sum_three[:, :, rows:])
    end(sx, sy, *w1, my_three, to_three)

    w2 = gather(*join(d_w, *w1, 2, 2), 2)
    ox, oy = second_step(o_sums, *now(ou, ov))
    grad_norm1 = last_sum(sums[:rows], *now(sx, sy))
    input_grad = grad_mid + srms_back(xf, plan.turn(grad_norm1))
    end(*w2, ox, oy)

    w3 = gather(*join(d_w, *w2, 3, 1), 3)
    got = to_y(now(to_three))
    output = mid + plan.turn(last_sum(o_sums[:rows], *now(ox, oy)))
    end(*w3, got)

    sum_w = pin(last_sum(d_w[0], *now(*w3)))
    sum_in = sum_w[:deep].astype(BF).reshape(8, few, across)
    mine = lax.all_to_all(sum_in, plan.tp, 0, 0, tiled=True)
    mine = mine.reshape(4, 2, few, 4, 2, HD).transpose(2, 3, 1, 4, 0, 5)
    sum_in = mine.reshape(few, -1).astype(F32)
    sum_out = jnp.concatenate([sum_w[deep : deep + few], sum_w[deep + few :]], axis=1)
    sum_three = plan.by_y(my_three, got, 1)
    sum_pair = sum_three[:2].swapaxes(1, 2).astype(F32)
    sum_third = sum_three[2].astype(F32)
    return output, input_grad, sum_in, sum_out, sum_pair, sum_third


class Plain:
    def __init__(self, wide, narrow):
        self.tp = ("narrow",)
        self.fs = ("wide",)
        self.size = narrow
        self.groups = wide

    def begin(self):
        self.p = lax.axis_index("narrow")
        self.group = lax.axis_index("wide")
        self.slot_ids = jnp.arange(self.size, dtype=jnp.int32)

    def turn(self, v):
        return v

    def rows_all(self, a):
        whole = lax.all_gather(a, "narrow", axis=0, tiled=True)
        return whole[: whole.shape[0] // 2], whole[whole.shape[0] // 2 :]

    def rows_sum(self, keep, give, kind=BF):
        total = lax.psum_scatter(
            jnp.concatenate([keep, give]), "narrow", scatter_dimension=0, tiled=True
        )
        return total.astype(F32)

    def attn_in(self, w):
        rows, cols = w.shape
        each = cols // 4 // self.size
        view = w.reshape(rows, 4, self.size, each).transpose(2, 0, 1, 3)
        view = view.reshape(self.size, rows, 4 * each)
        mine = lax.all_to_all(view, "narrow", 0, 0, tiled=True)
        mine = mine.reshape(self.size * rows, 4 * each)
        return cut4(lax.all_gather(mine, "wide", axis=0, tiled=True), 0)

    def attn_in_back(self, g):
        cols = g.shape[2]
        g = g.reshape(-1, cols)
        total = lax.psum_scatter(g.astype(BF), "wide", scatter_dimension=0, tiled=True)
        rows = total.shape[0] // self.size
        view = total.reshape(self.size, rows, cols)
        mine = lax.all_to_all(view, "narrow", 0, 0, tiled=True)
        mine = mine.reshape(self.size, rows, 4, cols // 4).transpose(1, 2, 0, 3)
        return mine.reshape(rows, cols * self.size).astype(F32)

    def attn_out(self, w):
        whole = lax.all_gather(w, ("wide", "narrow"), axis=0, tiled=True)
        each = whole.shape[0] // self.size
        return lax.dynamic_slice_in_dim(whole, self.p * each, each)

    def attn_out_back(self, g):
        each = g.shape[0]
        whole = jnp.zeros((each * self.size, g.shape[1]), BF)
        whole = lax.dynamic_update_slice_in_dim(whole, g.astype(BF), self.p * each, 0)
        total = lax.psum_scatter(whole, ("wide", "narrow"), scatter_dimension=0, tiled=True)
        return total.astype(F32)

    def sglu(self, pair, third):
        return pair, third

    def sglu_all(self, both, back):
        pair = lax.all_gather(both.swapaxes(1, 2), "wide", axis=2, tiled=True)
        third = lax.all_gather(back, "wide", axis=1, tiled=True)
        return cut4(pair, 2), cut4(third, 1)

    def pair_back(self, g):
        g = jnp.concatenate([g[k] for k in range(4)], axis=2)
        total = lax.psum_scatter(g, "wide", scatter_dimension=2, tiled=True)
        return total.swapaxes(1, 2).astype(F32)

    def third_back(self, g):
        g = jnp.concatenate([g[k] for k in range(4)], axis=1)
        total = lax.psum_scatter(g, "wide", scatter_dimension=1, tiled=True)
        return total.astype(F32)


def plain_layer(
    plan, at, inputs, out_grad, attn_in, attn_out, sglu_in, sglu_out
):
    rows, width = inputs.shape
    w_out = plan.attn_out(attn_out.astype(BF))
    w_in = plan.attn_in(attn_in.astype(BF))
    w_pair, w_third = plan.sglu_all(sglu_in.astype(BF), sglu_out.astype(BF))
    xf = inputs.astype(F32)
    norm1 = plan.rows_all(plan.turn((xf * inverse_rms(xf)).astype(BF)))
    grad_rows = plan.rows_all(plan.turn(out_grad))
    raw, gate, qkv, term = zip(
        *[project(norm1[h], w_in, at.cols[h], at.prev[h], at.last[h], at.rate) for h in (0, 1)]
    )
    state = at.states(jnp.concatenate(term))
    attn, branch = [None] * 2, [None] * 2
    for h in (1, 0):
        attn[h], branch[h] = attend(
            qkv[h], gate[h], state[h], w_out, at.cols[h], at.rows[h], at.prev[h], at.last[h], at.rate
        )
    square = plan.rows_sum(*[strip_sum(v) for v in branch], F32)
    branch = plan.rows_sum(*[v[:, :width] for v in branch])
    r_attn = lax.rsqrt(square / width + EPS)
    mid = xf + r_attn * branch
    r_mid = inverse_rms(mid)
    norm2 = plan.rows_all(plan.turn((mid * r_mid).astype(BF)))

    product, turned, grad_first, grad_second, back = [[None] * 2 for _ in range(5)]
    for h in (1, 0):
        product[h], turned[h], grad_first[h], grad_second[h], back[h] = sglu_rows(
            norm2[h], grad_rows[h], w_pair, w_third
        )
    cut = width // 4
    sum_third = plan.third_back(grads_by_right([turned], grad_rows, cut, width)[:, 0])
    grad_norm2 = plan.rows_sum(*back)
    sum_pair = plan.pair_back(grads_by_right([grad_first, grad_second], norm2, cut, width))

    grad_mid = out_grad.astype(F32) + srms_back(mid, plan.turn(grad_norm2))
    grad_branch = grad_mid.astype(BF)
    inward = jnp.mean(grad_branch.astype(F32) * branch, axis=1, keepdims=True)
    extra = pieces(r_attn) + pieces(r_attn * r_attn * r_attn * inward)
    extra.append(jnp.zeros((rows, 128 - len(extra)), BF))
    grad_branch = jnp.concatenate([grad_branch] + extra, axis=1)
    grad_branch = plan.rows_all(grad_branch)
    branch_out = plan.rows_sum(*[sglu_last(v, w_third) for v in product])
    output = mid + plan.turn(branch_out)
    grad_attn, grad_gate, mixed, d_term = zip(
        *[
            attend_back_rows(
                grad_branch[h], w_out, attn[h], gate[h], qkv[h], at.cols[h],
                at.prev[h], at.last[h], at.rate,
            )
            for h in (0, 1)
        ]
    )
    later = at.states_back(jnp.concatenate(d_term))
    grad_pre, back = [None] * 2, [None] * 2
    for h in (1, 0):
        grad_pre[h], back[h] = project_back(
            qkv[h], raw[h], grad_attn[h], grad_gate[h], state[h], later[h], w_in, width,
            at.cols[h], at.rows[h], at.prev[h], at.last[h], at.rate,
        )
    grad_win = grads_by_left(norm1, grad_pre, cut)
    sum_in = plan.attn_in_back(grad_win)
    sum_out = plan.attn_out_back(grads_out(mixed, grad_branch, width))
    grad_norm1 = plan.rows_sum(*back)
    input_grad = grad_mid + srms_back(xf, plan.turn(grad_norm1))
    return output, input_grad, sum_in, sum_out, sum_pair, sum_third


def per_device(plan, layer, *args):
    inputs, out_grad, seq_lengths, decay_rate = args[:4]
    weights, moments, averages = args[4:8], args[8:12], args[12:16]
    plan.begin()
    rows, width = inputs.shape
    plan.own = decay_rate.shape[0] // plan.size
    at = Places(plan, seq_lengths, decay_rate, rows)
    output, input_grad, *grads = layer(plan, at, inputs, out_grad, *weights)
    tokens = plan.size * rows * plan.groups
    fans = (width, width, width, weights[3].shape[0] * lax.axis_size(plan.narrow))
    new = [renew(*v, tokens) for v in zip(weights, moments, averages, grads, fans)]
    return (output, input_grad) + tuple(n[i] for i in range(3) for n in new)


def solution(mesh):
    wide, narrow = mesh.shape["wide"], mesh.shape["narrow"]
    if (wide, narrow) == (8, 4):
        mesh = Mesh(mesh.devices.reshape(4, 2, 2, 2), ("z", "y", "x", "c"))
        plan, layer, w, n = Square(), square_layer, ("z", "y"), ("x", "c")
    else:
        plan, layer, w, n = Plain(wide, narrow), plain_layer, ("wide",), ("narrow",)
    plan.narrow = n
    by_rows = P(w + n, None)
    pair, third = P(None, w, n), P(n, w)
    weights = (by_rows, by_rows, pair, third)

    def run(*args):
        return per_device(plan, layer, *args)

    return jax.shard_map(
        run,
        mesh=mesh,
        in_specs=(by_rows, by_rows, P(), P()) + weights * 3,
        out_specs=(by_rows, by_rows) + weights * 3,
        check_vma=False,
    )
```

```python
import math

import jax
import jax.numpy as jnp
from jax import lax
from jax.experimental import pallas as pl
from jax.experimental.layout import Layout, with_layout_constraint
from jax.experimental.pallas import tpu as pltpu
from jax.sharding import Mesh
from jax.sharding import PartitionSpec as P

BLOCK = 256
EPS = 1e-06
MU = 0.9
BETA = 0.8
HIGH = lax.Precision.HIGHEST
BF = jnp.bfloat16
F32 = jnp.float32
SWAP = [(0, 1), (1, 0)]
XORS = (0, 2, 4, 6, 1, 3, 5, 7)


def dot(a, b, dims=((1,), (0,))):
    return lax.dot_general(a, b, (dims, ((), ())), preferred_element_type=F32)


def inverse_rms(v):
    return lax.rsqrt(jnp.mean(v * v, axis=-1, keepdims=True) + EPS)


def srms_back(v, grad):
    r = inverse_rms(v)
    return r * grad - v * (r * r * r) * jnp.mean(grad * v, axis=-1, keepdims=True)


def renew(weight, moment, average, grad, fan, tokens):
    step = 0.4 / math.sqrt(fan * tokens)
    moment_new = MU * moment + grad
    weight_new = weight - step * (grad + MU * moment_new)
    average_new = BETA * average + (1.0 - BETA) * weight_new
    return (moment_new, weight_new, average_new)


ROWS = 256
HALF = 4
HD = 128
VMEM = 56 * 1024 * 1024
EXTRA = 128


def pin(v):
    return with_layout_constraint(v, Layout(major_to_minor=tuple(range(v.ndim))))


def after(value, *done):
    return lax.optimization_barrier((value,) + done)[0]


class Clock:
    def __init__(self):
        self.token = jnp.zeros((8, 128), F32)

    def now(self, *values):
        out = [lax.optimization_barrier((v, self.token))[0] for v in values]
        return out if len(out) > 1 else out[0]

    def end(self, *done):
        self.token = lax.optimization_barrier((self.token,) + done)[0]


def block_spec(shape):
    return pl.BlockSpec(shape, lambda i: (i,) + (0,) * (len(shape) - 1))


def whole_spec(a):
    return pl.BlockSpec(a.shape, lambda i: (0,) * a.ndim, pipeline_mode=pl.Buffered(1))


def scalar_spec():
    return pl.BlockSpec(memory_space=pltpu.SMEM)


def call(kernel, steps, ins, outs, flops):
    moved = sum(a.size * a.dtype.itemsize for a, _ in ins)
    moved += sum(math.prod(s) * jnp.dtype(d).itemsize for s, d, _ in outs)
    return pl.pallas_call(
        kernel,
        grid=(steps,),
        in_specs=[s for _, s in ins],
        out_specs=[b if isinstance(b, pl.BlockSpec) else block_spec(b) for _, _, b in outs],
        out_shape=[jax.ShapeDtypeStruct(s, d) for s, d, _ in outs],
        compiler_params=pltpu.CompilerParams(
            vmem_limit_bytes=VMEM, dimension_semantics=("arbitrary",)
        ),
        cost_estimate=pl.CostEstimate(
            flops=int(flops), bytes_accessed=int(moved), transcendentals=0
        ),
    )(*[a for a, _ in ins])


NT = ((1,), (1,))
TN = ((0,), (0,))


def mask_of(fade, seg_c, seg_r):
    return jnp.where(seg_c == seg_r, fade, 0.0)


def pair_spec(shape, late):
    if late:
        return pl.BlockSpec(shape, lambda i: (jnp.maximum(i - HALF, 0),) + (0,) * (len(shape) - 1))
    return pl.BlockSpec(shape, lambda i: (jnp.minimum(i, HALF - 1),) + (0,) * (len(shape) - 1))


def half_spec(shape, h):
    return pl.BlockSpec(shape, lambda i: (i + h * HALF,) + (0,) * (len(shape) - 1))


def project(n1, w_in, at):
    own = at.own
    cols = own * HD
    parts = len(w_in)
    width = n1[0].shape[1]
    deep = width // parts

    def kernel(*refs):
        a_ref, b_ref, w_refs = refs[0], refs[1], refs[2 : 2 + parts]
        seg_ref, ramp_ref, last_ref, reach_ref = refs[2 + parts : 6 + parts]
        raw_ref, gate_ref, qkv_ref, term_ref, leaving_ref = refs[6 + parts :]
        i = pl.program_id(0)
        pre = None
        for k in range(parts):
            some = slice(k * deep, (k + 1) * deep)
            x = jnp.where(i < HALF, a_ref[:, some], b_ref[:, some])
            new = dot(x, w_refs[k][...])
            pre = new if pre is None else pre + new
        pq, pk, pv = pre[:, :cols], pre[:, cols : 2 * cols], pre[:, 2 * cols : 3 * cols]
        raw_ref[...] = pre[:, : 2 * cols]
        gate_ref[...] = pre[:, 3 * cols :]
        key = (pk * jax.nn.sigmoid(pk)).astype(BF)
        value = pv.astype(BF)
        qkv_ref[:, :cols] = (pq * jax.nn.sigmoid(pq)).astype(BF)
        qkv_ref[:, cols : 2 * cols] = key
        qkv_ref[:, 2 * cols :] = value

        @pl.when(i == 0)
        def _():
            leaving_ref[...] = jnp.zeros_like(leaving_ref)

        for j in range(own):
            leave = jnp.where(seg_ref[0] == last_ref[i], ramp_ref[:, own + j : own + j + 1], 0.0)
            head = slice(j * HD, (j + 1) * HD)
            scaled = (key[:, head].astype(F32) * leave).astype(BF)
            term = dot(scaled, value[:, head], TN)
            term_ref[0, j] = term
            leaving_ref[j] += reach_ref[j, i] * term

    some = pl.BlockSpec((deep, 4 * cols), lambda i: (0, 0), pipeline_mode=pl.Buffered(1))
    ins = [(v, pair_spec((ROWS, width), late)) for late, v in enumerate(n1)]
    ins += [(w, some) for w in w_in]
    ins += [(at.cols, block_spec((1, ROWS, 1))), (at.ramps, whole_spec(at.ramps))]
    ins += [(v, scalar_spec()) for v in (at.last, at.out_reach)]
    n = 2 * HALF
    outs = [
        ((n * ROWS, 2 * cols), F32, (ROWS, 2 * cols)),
        ((n * ROWS, cols), F32, (ROWS, cols)),
        ((n * ROWS, 3 * cols), BF, (ROWS, 3 * cols)),
        ((n, own, HD, HD), F32, (1, own, HD, HD)),
        ((own, HD, HD), F32, pl.BlockSpec((own, HD, HD), lambda i: (0, 0, 0))),
    ]
    return call(kernel, n, ins, outs, 4 * n1[0].size * 4 * cols)


def combine(weights, terms, more, reach):
    state = reach * more
    for c in range(2 * HALF):
        state = state + weights(c) * terms(c)
    return state


def attend(h, qkv, gate, term, entering, w_out, at):
    own = at.own
    cols = own * HD
    width = w_out.shape[1]

    def kernel(
        qkv_ref, gate_ref, term_ref, more_ref, w_ref, sc_ref, sr_ref, fade_ref, ramp_ref,
        prev_ref, inner_ref, reach_ref, attn_ref, branch_ref, state_ref,
    ):
        i = pl.program_id(0) + h * HALF
        for j in range(own):
            head = slice(j * HD, (j + 1) * HD)
            q = qkv_ref[:, j * HD : (j + 1) * HD]
            k = qkv_ref[:, cols + j * HD : cols + (j + 1) * HD]
            v = qkv_ref[:, 2 * cols + j * HD : 2 * cols + (j + 1) * HD]
            state = combine(
                lambda c: inner_ref[j, i * 2 * HALF + c],
                lambda c: term_ref[c, j],
                more_ref[j],
                reach_ref[j, i],
            ).astype(BF)
            state_ref[0, j] = state
            enter = jnp.where(sc_ref[0] == prev_ref[i], ramp_ref[:, j : j + 1], 0.0)
            weights = (dot(q, k, NT) * mask_of(fade_ref[j], sc_ref[0], sr_ref[0])).astype(BF)
            attn_ref[:, head] = dot(weights, v) + enter * dot(q, state)
        attn = attn_ref[...]
        branch_ref[:, :width] = dot((attn * gate_ref[...]).astype(BF), w_ref[...]).astype(BF)
        rest = jnp.sum(attn * attn, axis=1, keepdims=True)
        lane = lax.broadcasted_iota(jnp.int32, (ROWS, EXTRA), 1)
        strip = jnp.zeros((ROWS, EXTRA), F32)
        for n in range(3):
            top = rest.astype(BF).astype(F32)
            strip = jnp.where(lane == n, top, strip)
            rest = rest - top
        branch_ref[:, width:] = strip.astype(BF)

    n = HALF
    ins = [
        (qkv, half_spec((ROWS, 3 * cols), h)),
        (gate, half_spec((ROWS, cols), h)),
        (term, whole_spec(term)),
        (entering, whole_spec(entering)),
        (w_out, whole_spec(w_out)),
        (at.cols, half_spec((1, ROWS, 1), h)),
        (at.rows, half_spec((1, 1, ROWS), h)),
        (at.fade, whole_spec(at.fade)),
        (at.ramps, whole_spec(at.ramps)),
    ] + [(v, scalar_spec()) for v in (at.prev, at.inner, at.in_reach)]
    outs = [
        ((n * ROWS, cols), F32, (ROWS, cols)),
        ((n * ROWS, width + EXTRA), BF, (ROWS, width + EXTRA)),
        ((n, own, HD, HD), BF, (1, own, HD, HD)),
    ]
    return call(kernel, n, ins, outs, 2 * n * ROWS * cols * (width + 2 * ROWS))


def sglu_rows(n2, g, w_pair, w_third):
    parts = len(w_pair)
    _, hidden, deep = w_pair[0].shape
    block = 2 * ROWS

    def kernel(*refs):
        x_ref, g_ref = refs[:2]
        both, three = (refs[2 + k * parts : 2 + (k + 1) * parts] for k in range(2))
        prod_ref, prod_t, gf_t, gs_t, back_ref = refs[2 + 2 * parts :]
        first = second = grad = None
        for k in range(parts):
            at = slice(k * deep, (k + 1) * deep)
            x, gk = x_ref[:, at], g_ref[:, at]
            a, b, c = dot(x, both[k][0], NT), dot(x, both[k][1], NT), dot(gk, three[k][...], NT)
            first = a if first is None else first + a
            second = b if second is None else second + b
            grad = c if grad is None else grad + c
        prod = (first * second).astype(BF)
        gf = (grad * second).astype(BF)
        gs = (grad * first).astype(BF)
        prod_ref[...] = prod
        prod_t[...] = prod.T
        gf_t[...] = gf.T
        gs_t[...] = gs.T
        for k in range(parts):
            at = slice(k * deep, (k + 1) * deep)
            back_ref[:, at] = (dot(gf, both[k][0]) + dot(gs, both[k][1])).astype(BF)

    n = n2.shape[0] // block
    width = n2.shape[1]
    ins = [(n2, block_spec((block, width))), (g, block_spec((block, width)))]
    ins += [(w, whole_spec(w)) for w in w_pair + w_third]
    outs = [((n * block, hidden), BF, (block, hidden))]
    turned = pl.BlockSpec((hidden, block), lambda i: (0, i))
    outs += [((hidden, n * block), BF, turned)] * 3
    outs += [((n * block, width), BF, (block, width))]
    return call(kernel, n, ins, outs, 10 * n2.size * hidden)


def sglu_last(product, w_third):
    parts = len(w_third)
    deep = w_third[0].shape[1]
    block = 2 * ROWS

    def kernel(*refs):
        for k in range(parts):
            refs[-1][:, k * deep : (k + 1) * deep] = dot(refs[0][...], refs[1 + k][...]).astype(BF)

    n, width = product.shape[0] // block, parts * deep
    ins = [(product, block_spec((block, product.shape[1])))]
    ins += [(w, whole_spec(w)) for w in w_third]
    return call(
        kernel, n, ins, [((n * block, width), BF, (block, width))], 2 * product.size * width
    )[0]


def attend_back_rows(gb, w_out, attn, gate, qkv, at):
    own = at.own
    cols = own * HD
    width = w_out.shape[1]

    def kernel(
        gb_a, gb_b, w_ref, attn_a, attn_b, gate_ref, qkv_ref, sc_ref, ramp_ref, prev_ref, reach_ref,
        ga_ref, gg_ref, mixed_ref, term_ref, leaving_ref,
    ):
        i = pl.program_id(0)
        early = i < HALF
        extra = jnp.where(early, gb_a[:, width:], gb_b[:, width:]).astype(F32)
        r = extra[:, 0:1] + extra[:, 1:2] + extra[:, 2:3]
        pull = extra[:, 3:4] + extra[:, 4:5] + extra[:, 5:6]
        gm = dot(jnp.where(early, gb_a[:, :width], gb_b[:, :width]), w_ref[...], NT)
        attn, gate = jnp.where(early, attn_a[...], attn_b[...]), gate_ref[...]
        normed = r * attn
        gg_ref[...] = (gm * normed).astype(BF)
        mixed_ref[...] = (normed * gate).astype(BF)
        ga = (r * (gm * gate) - attn * pull).astype(BF)
        ga_ref[...] = ga

        @pl.when(i == 0)
        def _():
            leaving_ref[...] = jnp.zeros_like(leaving_ref)

        for j in range(own):
            enter = jnp.where(sc_ref[0] == prev_ref[i], ramp_ref[:, j : j + 1], 0.0)
            q = qkv_ref[:, j * HD : (j + 1) * HD].astype(F32)
            term = dot((q * enter).astype(BF), ga[:, j * HD : (j + 1) * HD], TN)
            term_ref[0, j] = term
            leaving_ref[j] += reach_ref[j, i] * term

    n = 2 * HALF
    ins = [(v, pair_spec((ROWS, v.shape[1]), late)) for late, v in enumerate(gb)]
    ins += [(w_out, whole_spec(w_out))]
    ins += [(v, pair_spec((ROWS, cols), late)) for late, v in enumerate(attn)]
    ins += [
        (gate, block_spec((ROWS, cols))),
        (qkv, block_spec((ROWS, 3 * cols))),
        (at.cols, block_spec((1, ROWS, 1))),
        (at.ramps, whole_spec(at.ramps)),
    ] + [(v, scalar_spec()) for v in (at.prev, at.in_reach)]
    outs = [((n * ROWS, cols), BF, (ROWS, cols))] * 3
    outs += [((n, own, HD, HD), F32, (1, own, HD, HD))]
    outs += [((own, HD, HD), F32, pl.BlockSpec((own, HD, HD), lambda i: (0, 0, 0)))]
    return call(kernel, n, ins, outs, 2 * n * ROWS * cols * width)


def project_back(h, qkv, raw, ga, gg, state, term, entering, w_in, width, at):
    own = at.own
    cols = own * HD
    parts = len(w_in)
    deep = width // parts

    def kernel(*refs):
        qkv_ref, raw_ref, ga_ref, gg_ref, state_ref, term_ref, more_ref = refs[:7]
        w_refs = refs[7 : 7 + parts]
        sc_ref, sr_ref, fade_ref, ramp_ref = refs[7 + parts : 11 + parts]
        prev_ref, last_ref, inner_ref, reach_ref, gp_ref, back_ref = refs[11 + parts :]
        i = pl.program_id(0) + h * HALF
        for j in range(own):
            head = slice(j * HD, (j + 1) * HD)
            kt = slice(cols + j * HD, cols + (j + 1) * HD)
            vt = slice(2 * cols + j * HD, 2 * cols + (j + 1) * HD)
            q, k, v = qkv_ref[:, head], qkv_ref[:, kt], qkv_ref[:, vt]
            g = ga_ref[:, head]
            mask = mask_of(fade_ref[j], sc_ref[0], sr_ref[0])
            enter = jnp.where(sc_ref[0] == prev_ref[i], ramp_ref[:, j : j + 1], 0.0)
            leave = jnp.where(sc_ref[0] == last_ref[i], ramp_ref[:, own + j : own + j + 1], 0.0)
            later = combine(
                lambda c: inner_ref[j, c * 2 * HALF + i],
                lambda c: term_ref[c, j],
                more_ref[j],
                reach_ref[j, i],
            ).astype(BF)
            weights = (dot(q, k, NT) * mask).astype(BF)
            gs = (dot(g, v, NT) * mask).astype(BF)
            gq = dot(gs, k) + enter * dot(g, state_ref[0, j], NT)
            gk = dot(gs, q, TN) + leave * dot(v, later, NT)
            gv = dot(weights, g, TN) + leave * dot(k, later)
            rq, rk = raw_ref[:, head], raw_ref[:, kt]
            sq, sk = jax.nn.sigmoid(rq), jax.nn.sigmoid(rk)
            gp_ref[:, head] = (gq * (sq * (1.0 + rq * (1.0 - sq)))).astype(BF)
            gp_ref[:, kt] = (gk * (sk * (1.0 + rk * (1.0 - sk)))).astype(BF)
            gp_ref[:, vt] = gv.astype(BF)
        gp_ref[:, 3 * cols :] = gg_ref[...]
        for k in range(parts):
            some = slice(k * deep, (k + 1) * deep)
            back_ref[:, some] = dot(gp_ref[...], w_refs[k][...], NT).astype(BF)

    n = HALF
    some = pl.BlockSpec((deep, 4 * cols), lambda i: (0, 0), pipeline_mode=pl.Buffered(1))
    ins = [
        (qkv, half_spec((ROWS, 3 * cols), h)),
        (raw, half_spec((ROWS, 2 * cols), h)),
        (ga, half_spec((ROWS, cols), h)),
        (gg, half_spec((ROWS, cols), h)),
        (state, block_spec((1, own, HD, HD))),
        (term, whole_spec(term)),
        (entering, whole_spec(entering)),
    ] + [(w, some) for w in w_in]
    ins += [
        (at.cols, half_spec((1, ROWS, 1), h)),
        (at.rows, half_spec((1, 1, ROWS), h)),
        (at.fade, whole_spec(at.fade)),
        (at.ramps, whole_spec(at.ramps)),
    ]
    ins += [(v, scalar_spec()) for v in (at.prev, at.last, at.inner, at.out_reach)]
    outs = [
        ((n * ROWS, 4 * cols), BF, (ROWS, 4 * cols)),
        ((n * ROWS, width), BF, (ROWS, width)),
    ]
    return call(kernel, n, ins, outs, 2 * n * ROWS * 4 * cols * width)


def one_by_one(count, shape):
    spec = pl.BlockSpec(shape, lambda i: (0,) * len(shape), pipeline_mode=pl.Buffered(1))
    return [(shape, BF, spec) for _ in range(count)]


def grads_by_left(left, right, more):
    n = len(more)
    cut, cols = left[0].shape[1] // n, right[0].shape[1]

    def kernel(*refs):
        l0, l1, r0, r1 = refs[:4]
        grad = (dot(l0[...], r0[...], TN) + dot(l1[...], r1[...], TN)).astype(BF)
        for k in range(n):

            @pl.when(pl.program_id(0) == k)
            def _():
                refs[4 + n + k][:cut] = grad
                refs[4 + n + k][cut:] = refs[4 + k][...]

    ins = [(a, pl.BlockSpec((a.shape[0], cut), lambda i: (0, i))) for a in left]
    ins += [(a, whole_spec(a)) for a in (*right, *more)]
    outs = one_by_one(n, (cut + more[0].shape[0], cols))
    return call(kernel, n, ins, outs, 4 * left[0].size * cols)


def grads_by_right(lefts, right, cut, width):
    count = len(lefts)
    n = width // cut
    tall = lefts[0][0].shape[0]

    def kernel(*refs):
        r0, r1 = refs[2 * count : 2 * count + 2]
        outs = refs[2 * count + 2 :]
        for m in range(count):
            l0, l1 = refs[2 * m : 2 * m + 2]
            grad = (dot(l0[...], r0[...]) + dot(l1[...], r1[...])).astype(BF)
            for k in range(n):

                @pl.when(pl.program_id(0) == k)
                def _():
                    outs[k][m] = grad

    ins = [(a, whole_spec(a)) for left in lefts for a in left]
    ins += [(a, pl.BlockSpec((a.shape[0], cut), lambda i: (0, i))) for a in right]
    outs = one_by_one(n, (count, tall, cut))
    return call(kernel, n, ins, outs, 4 * count * right[0].size * tall)


def grads_out(left, right, width):
    def kernel(l0, l1, r0, r1, out):
        out[...] = (dot(l0[...], r0[...], TN) + dot(l1[...], r1[...], TN)).astype(BF)

    cut, (rows, tall) = width // 4, left.shape
    spec = lambda rows: pl.BlockSpec((rows, cut), lambda i: (0, i))
    half = lambda k: pl.BlockSpec((rows // 2, tall), lambda i: (k, 0))
    ins = [(left, half(k)) for k in (0, 1)] + [(a, spec(a.shape[0])) for a in right]
    return call(kernel, 4, ins, [((tall, width), BF, spec(tall))], 2 * left.size * width)[0]


def add_strips(width, *parts):
    total = parts[0][:, :width].astype(F32)
    for p in parts[1:]:
        total = total + p[:, :width].astype(F32)
    out = [total.astype(BF)]
    if parts[0].shape[1] > width:
        rest = 0.0
        for p in parts:
            for n in range(3):
                rest = rest + p[:, width + n : width + n + 1].astype(F32)
        lane = lax.broadcasted_iota(jnp.int32, (total.shape[0], EXTRA), 1)
        strip = jnp.zeros((total.shape[0], EXTRA), F32)
        for n in range(3):
            top = rest.astype(BF).astype(F32)
            strip = jnp.where(lane == n, top, strip)
            rest = rest - top
        out.append(strip.astype(BF))
    return out


def add_last(a, b, width):
    n, wide = a.shape[0] // ROWS, a.shape[1]
    half = ROWS // 2

    def kernel(a_ref, b_ref, low_ref, high_ref):
        parts = add_strips(width, a_ref[...], b_ref[...])
        for v, at in zip(parts, (slice(0, width), slice(width, wide))):
            low_ref[:, at] = v[:half]
            high_ref[:, at] = v[half:]

    block = pl.BlockSpec((ROWS, wide), lambda i: (n - 1, 0))
    one = pl.BlockSpec((half, wide), lambda i: (0, 0))
    return call(kernel, 1, [(a, block), (b, block)], [((half, wide), BF, one)] * 2, ROWS * wide)


def add_halves(a, b, u, v, width):
    wide = a.shape[1]
    half = ROWS // 2

    def kernel(a2, a4, b2, b4, u_ref, v_ref, to_2, to_4):
        low, high = slice(0, half), slice(half, ROWS)
        for out, rows, terms in (
            (to_2, low, (a2[low], b2[low])),
            (to_2, high, (a2[high], b2[high], v_ref[...])),
            (to_4, low, (a4[low], b4[low], u_ref[...])),
            (to_4, high, (a4[high], b4[high])),
        ):
            parts = add_strips(width, *terms)
            for p, at in zip(parts, (slice(0, width), slice(width, wide))):
                out[rows, at] = p

    spec = lambda k: pl.BlockSpec((ROWS, wide), lambda i: (k, 0))
    ins = [(t, spec(k)) for t in (a, b) for k in (1, 2)] + [(u, whole_spec(u)), (v, whole_spec(v))]
    return call(kernel, 1, ins, [((ROWS, wide), BF, spec(0))] * 2, ROWS * wide)


def strip_of(column):
    lane = lax.broadcasted_iota(jnp.int32, (column[0].shape[0], EXTRA), 1)
    strip = jnp.zeros(lane.shape, F32)
    for m, rest in enumerate(column):
        for n in range(3):
            top = rest.astype(BF).astype(F32)
            strip = jnp.where(lane == 3 * m + n, top, strip)
            rest = rest - top
    return strip.astype(BF)


def mid_rows(sums, inputs, dest):
    width = inputs.shape[1]
    cut = width // 4
    block = ROWS // 2

    def kernel(a, b, c, d, x_ref, dest_ref, mid_ref, branch_ref, scale_ref, norm_ref):
        branch = square = None
        for ref in (a, b, c, d):
            part = ref[:, :width].astype(F32)
            extra = ref[:, width:].astype(F32)
            more = extra[:, 0:1] + extra[:, 1:2] + extra[:, 2:3]
            branch = part if branch is None else branch + part
            square = more if square is None else square + more
        r = lax.rsqrt(square / width + EPS)
        mid = x_ref[...].astype(F32) + r * branch
        branch_ref[...] = branch.astype(BF)
        scale_ref[...] = jnp.broadcast_to(r, (block, EXTRA))
        mid_ref[...] = mid
        norm = (mid * inverse_rms(mid)).astype(BF)
        for p in range(4):
            to = pl.ds(pl.multiple_of(dest_ref[p] * cut, cut), cut)
            norm_ref[:, to] = norm[:, p * cut : (p + 1) * cut]

    ins = [(v, block_spec((block, width + EXTRA))) for v in sums]
    ins += [(inputs, block_spec((block, width))), (dest, scalar_spec())]
    outs = [
        ((ROWS, width), F32, (block, width)),
        ((ROWS, width), BF, (block, width)),
        ((ROWS, EXTRA), F32, (block, EXTRA)),
        ((ROWS, width), BF, (block, width)),
    ]
    return call(kernel, 2, ins, outs, 20 * ROWS * width)


def mid_back_rows(sums, out_grad, mid, branch, scale, dest):
    width = mid.shape[1]
    cut = width // 4
    block = ROWS // 2

    def kernel(a, b, c, d, g_ref, mid_ref, branch_ref, scale_ref, dest_ref, grad_ref, out_ref):
        parts = []
        for p in range(4):
            at = pl.ds(pl.multiple_of(dest_ref[p] * cut, cut), cut)
            part = a[:, at].astype(F32)
            for ref in (b, c, d):
                part = part + ref[:, at].astype(F32)
            parts.append(part)
        grad = g_ref[...].astype(F32) + srms_back(mid_ref[...], jnp.concatenate(parts, axis=1))
        grad_ref[...] = grad
        low = grad.astype(BF)
        out_ref[:, :width] = low
        inward = low.astype(F32) * branch_ref[...].astype(F32)
        inward = jnp.mean(inward, axis=1, keepdims=True)
        r = scale_ref[:, 0:1]
        out_ref[:, width:] = strip_of([r, r * r * r * inward])

    ins = [(v, block_spec((block, width))) for v in (*sums, out_grad, mid, branch)]
    ins += [(scale, block_spec((block, EXTRA))), (dest, scalar_spec())]
    outs = [
        ((ROWS, width), F32, (block, width)),
        ((ROWS, width + EXTRA), BF, (block, width + EXTRA)),
    ]
    return call(kernel, 2, ins, outs, 20 * ROWS * width)


def renew_turned(grad, weight, moment, average, fan, tokens):
    few, total = weight.shape
    block = 16

    def kernel(g_ref, w_ref, m_ref, a_ref, m_new, w_new, a_new):
        for p in range(8):
            for t in range(4):
                for j in range(2):
                    col = t * (total // 4) + (8 * (p % 2) + 4 * j + p // 2) * HD
                    to = slice(col, col + HD)
                    at = slice((2 * t + j) * HD, (2 * t + j + 1) * HD)
                    new = renew(
                        w_ref[:, to], m_ref[:, to], a_ref[:, to], g_ref[p, :, at].astype(F32),
                        fan, tokens,
                    )
                    m_new[:, to], w_new[:, to], a_new[:, to] = new

    ins = [(grad, pl.BlockSpec((8, block, grad.shape[2]), lambda i: (0, i, 0)))]
    ins += [(v, block_spec((block, total))) for v in (weight, moment, average)]
    outs = [((few, total), F32, (block, total))] * 3
    return call(kernel, few // block, ins, outs, 10 * weight.size)


def cut4(v, axis):
    n = v.shape[axis] // 4
    return [lax.slice_in_dim(v, k * n, (k + 1) * n, axis=axis) for k in range(4)]


def strip_sum(v):
    strip = v[:, v.shape[1] - EXTRA :].astype(F32)
    return strip[:, 0:1] + strip[:, 1:2] + strip[:, 2:3]


def pieces(v):
    out = []
    for _ in range(3):
        top = lax.reduce_precision(v, 8, 7)
        out.append(top.astype(BF))
        v = v - top
    return out


class Places:
    def __init__(self, plan, seq_lengths, decay_rate, rows):
        size = plan.size
        group_rows = size * rows
        tokens = group_rows * plan.groups
        ends = jnp.cumsum(seq_lengths)

        def seg_at(place):
            mark = jnp.sum((place[..., None] >= ends).astype(jnp.int32), axis=-1)
            return jnp.where(place < 0, -1, mark)

        first_block = plan.group * size
        blocks = first_block + plan.slot_ids
        seg = seg_at(blocks[:, None] * rows + jnp.arange(rows, dtype=jnp.int32)[None, :])
        prev = seg_at(blocks * rows - 1)
        last = seg[:, rows - 1]
        head_ids = plan.head_ids if hasattr(plan, "head_ids") else plan.own * plan.p + jnp.arange(plan.own)
        rate = jnp.take(decay_rate, head_ids)

        def reach(gap, same):
            return jnp.where(
                same & (gap >= 0), jnp.exp(-rate[:, None, None] * (rows * jnp.maximum(gap, 0))), 0.0
            )

        inner = reach(
            (blocks[:, None] - blocks[None, :] - 1).astype(F32)[None],
            (prev[:, None] == last[None, :])[None],
        )
        border = seg_at((first_block + size) * rows - 1)
        out_reach = reach(
            (first_block + size - 1 - blocks).astype(F32)[None, None], (last == border)[None, None]
        )[:, 0]
        entry = seg_at(first_block * rows - 1)
        in_reach = reach((blocks - first_block).astype(F32)[None, None], (prev == entry)[None, None])[
            :, 0
        ]
        longest = tokens // 4
        hops = min(-(-longest // group_rows), plan.groups - 1)

        def hop_factor(j, ahead):
            if ahead:
                here, there = border, seg_at((first_block + j * size) * rows - 1)
            else:
                here, there = entry, seg_at((first_block - (j - 1) * size) * rows - 1)
            return jnp.where(here == there, jnp.exp(-rate * ((j - 1) * group_rows)), 0.0)

        def bring(total, ahead):
            n = plan.groups
            got = jnp.zeros_like(total)
            for j in range(1, hops + 1):
                pairs = [(i + j, i) if ahead else (i, i + j) for i in range(n - j)]
                part = lax.ppermute(total, plan.fs, pairs)
                got = got + hop_factor(j, ahead)[:, None, None] * part
            return got

        self.bring, self.hop = bring, hop_factor
        self.inner = inner.reshape(inner.shape[0], -1)
        self.out_reach, self.in_reach = out_reach, in_reach
        self.own = plan.own
        self.cols, self.rows = seg[:, :, None], seg[:, None, :]
        self.prev, self.last = prev, last
        step = jnp.arange(rows).astype(F32)
        spread = step[:, None] - step[None, :]
        fade = jnp.exp(-rate[:, None, None] * jnp.maximum(spread, 0.0)[None])
        self.fade = jnp.where((spread >= 0)[None], fade, 0.0)
        ramps = [jnp.exp(-rate[None] * step[:, None]), jnp.exp(-rate[None] * (rows - step)[:, None])]
        blank = jnp.zeros((rows, EXTRA - 2 * plan.own), F32)
        self.ramps = jnp.concatenate(ramps + [blank], axis=1)


class Square:
    def __init__(self):
        self.tp = ("y", "x", "c")
        self.fs = ("z",)
        self.size = 8
        self.groups = 4

    def begin(self):
        self.z = lax.axis_index("z")
        self.y = lax.axis_index("y")
        self.c = lax.axis_index("c")
        self.p = lax.axis_index(self.tp)
        self.q = self.p // 2
        self.group = self.z
        self.slot_ids = self.p ^ jnp.array(XORS, jnp.int32)
        self.head_ids = 8 * self.c + 4 * jnp.arange(2) + self.q

    def turn(self, v):
        wide = v.shape[1] // 4
        return jnp.concatenate(
            [
                lax.dynamic_slice_in_dim(v, ((self.z - k) % 4) * wide, wide, axis=1)
                for k in range(4)
            ],
            axis=1,
        )

    def places(self):
        return (self.z - jnp.arange(4, dtype=jnp.int32)) % 4

    def slots(self, own, one, two, three):
        return [
            own,
            pin(jnp.where(self.z >= 1, one[0], three[1])),
            pin(jnp.where(self.z >= 2, two[0], two[1])),
            pin(jnp.where(self.z >= 3, three[0], one[1])),
        ]

    def by_y(self, mine, got, axis):
        first = self.y == 0
        parts = [jnp.where(first, mine, got), jnp.where(first, got, mine)]
        return pin(jnp.concatenate(parts, axis=axis))

    def of_y(self, one, two):
        first = self.y == 0
        return pin(jnp.where(first, one, two)), pin(jnp.where(first, two, one))


def over(axis, pairs=SWAP):
    return lambda v: pin(lax.ppermute(pin(v), axis, pairs))


to_x, to_y, to_core = over("x"), over("y"), over("c")


def spread(pair, step):
    up = over("z", [(i, i + 1) for i in range(step, 3)])
    down = over("z", [(3 - i, 2 - i) for i in range(step, 3)])
    return up(pair[0]), down(pair[1])


def gather(up, down, step):
    go_up = over("z", [(i, i + 1) for i in range(step)])
    go_down = over("z", [(3 - i, 2 - i) for i in range(step)])
    return go_up(up), go_down(down)


def plus(a, b):
    return (a.astype(F32) + b.astype(F32)).astype(BF)


def square_layer(plan, places, lengths, inputs, out_grad, attn_in, attn_out, sglu_in, sglu_out):
    rows, width = inputs.shape
    h2 = rows // 2
    cut = width // 4
    clock = Clock()
    now, end = clock.now, clock.end

    def pick(slots, plane):
        return lax.dynamic_index_in_dim(slots, (plan.z - plane) % 4, 0, False)

    xf = inputs.astype(F32)
    n1 = pin(plan.turn((xf * inverse_rms(xf)).astype(BF)))
    og = pin(plan.turn(out_grad))
    few = attn_in.shape[0]
    view = attn_in.astype(BF).reshape(few, 4, 2, 2, 4, HD).transpose(4, 2, 0, 1, 3, 5)
    own_in = lax.all_to_all(view.reshape(8, few, -1), plan.tp, 0, 0, tiled=True)
    own_in = own_in.reshape(8 * few, -1)
    deep, across = own_in.shape
    own_out = attn_out.astype(BF)
    own_w = pin(jnp.concatenate([own_in, own_out[:, :across], own_out[:, across:]]))
    end(own_w, n1, og)

    a_w, a_n1 = now(own_w, n1)
    w1 = spread((a_w, a_w), 0)
    nx, ny = to_x(a_n1), to_y(a_n1)
    at = places(now(lengths))
    hid = sglu_in.shape[2] // 2
    three = pin(now(sglu_in).astype(BF)).swapaxes(1, 2)
    three = jnp.concatenate([three, sglu_out.astype(BF)[None]])
    my_three, to_three = plan.of_y(three[:, :hid], three[:, hid:])
    tables = [at.cols, at.rows, at.prev, at.last, at.fade, at.ramps]
    tables += [at.inner, at.out_reach, at.in_reach, at.hop(1, False), at.hop(1, True)]
    end(*w1, nx, ny, my_three, to_three, *tables)

    w2 = spread(now(*w1), 1)
    ax, ay = now(nx, ny)
    nd = to_x(ay[:h2]), to_y(ax[h2:])
    end(*w2, *nd)

    w3 = spread(now(*w2), 2)
    a_og, a_three = now(og, to_three)
    gx = to_x(a_og)
    got = to_y(a_three)
    n1_a = pin(jnp.concatenate([n1, nx, ny, *now(*nd)]))
    norm1 = n1_a, to_core(n1_a)
    own_three = plan.by_y(my_three, got, 2)
    own_pair, own_third = pin(own_three[:2]), pin(own_three[2])
    own_first, own_second = pin(own_three[0]), pin(own_three[1])
    end(*w3, gx, *norm1, own_pair, own_first, own_second, own_third)

    first1 = spread((now(own_first),) * 2, 0)
    w_in = plan.slots(own_w, *[now(*v) for v in (w1, w2, w3)])
    outs = jnp.stack([w[deep:] for w in w_in])
    w_mine = [pick(outs, 2 * plan.c + j) for j in (0, 1)]
    w_got = to_core(jnp.concatenate([pick(outs, 2 * (1 - plan.c) + j) for j in (0, 1)]))
    core0 = plan.c == 0
    raw, gate, qkv, term, leaving = project((now(norm1[0]), norm1[1]), w_in, at)
    end(*first1, w_got, leaving)

    gy = to_y(now(og))
    w_rows = []
    for j in (0, 1):
        got = w_got[j * 2 * few : (j + 1) * 2 * few]
        for half in (jnp.where(core0, w_mine[j], got), jnp.where(core0, got, w_mine[j])):
            w_rows.append(jnp.concatenate([half[:few], half[few:]], axis=1))
    w_out = pin(jnp.concatenate(w_rows))
    entering = at.bring(now(leaving), False)
    second1 = spread((after(now(own_second), entering),) * 2, 0)
    attn_b, give, state_b = attend(1, qkv, gate, term, entering, w_out, at)
    end(*second1, gy, give)

    third1 = spread((now(own_third),) * 2, 0)
    a_qkv, give = now(qkv, give)
    attn_a, keep, state_a = attend(0, a_qkv, gate, term, entering, w_out, at)
    got = to_core(give)
    a_gx, a_gy = now(gx, gy)
    gd = to_x(a_gy[:h2]), to_y(a_gx[h2:])
    f1, s1 = now(*first1), now(*second1)
    pair1 = pin(jnp.stack([f1[0], s1[0]])), pin(jnp.stack([f1[1], s1[1]]))
    end(*third1, got, keep, *pair1, *gd)

    def first_step(keep, got):
        low, high = add_last(keep, got, width)
        return to_x(low), to_y(high)

    def total(*parts):
        out = parts[0].astype(F32)
        for p in parts[1:]:
            out = out + p.astype(F32)
        return out

    keep, got = now(keep, got)
    u, v = first_step(keep, got)
    third2 = spread(now(*third1), 1)
    g_a = pin(jnp.concatenate([og, gx, gy, *now(*gd)]))
    end(u, v, *third2, g_a)

    to_2, to_4 = add_halves(keep, got, *now(u, v), width)
    sx, sy = to_x(to_2), to_y(to_4)
    pair2 = spread(now(*pair1), 1)
    g_b = to_core(now(g_a))
    end(sx, sy, *pair2, g_b)

    pair3 = spread(now(*pair2), 2)
    dest = plan.places()
    mid, branch, r_attn, n2 = mid_rows((keep, got, *now(sx, sy)), inputs, dest)
    mx, my, mc = to_x(n2), to_y(n2), to_core(n2)
    end(mx, my, mc, *pair3)

    third3 = spread(now(*third2), 2)
    ax, ay = now(mx, my)
    md = to_x(ay[:h2]), to_y(ax[h2:])
    mxyc = to_core(jnp.concatenate([ax, ay]))
    mdc = to_core(jnp.concatenate(md))
    n2_a = pin(jnp.concatenate([n2, mx, my, *md]))
    n2_b = pin(jnp.concatenate([mc, mxyc, mdc]))
    w_pair = plan.slots(own_pair, now(*pair1), now(*pair2), now(*pair3))
    end(*third3, n2_a, n2_b, *w_pair)

    w_third = plan.slots(own_third, *[now(*v) for v in (third1, third2, third3)])
    prod_b, turned_b, gf_b, gs_b, give = sglu_rows(n2_b, g_b, w_pair, w_third)
    end(give)

    give, a_n2 = now(give, n2_a)
    got = to_core(give)
    prod_a, turned_a, gf_a, gs_a, keep = sglu_rows(a_n2, g_a, w_pair, w_third)
    end(keep, got)

    keep, got = now(keep, got)
    u, v = first_step(keep, got)
    d_pair = grads_by_right([(now(gf_a), gf_b), (gs_a, gs_b)], (n2_a, n2_b), cut, width)
    end(u, v, *d_pair)

    d_pair = now(*d_pair)
    pair1 = gather(d_pair[1], d_pair[3], 1)
    to_2, to_4 = add_halves(keep, got, *now(u, v), width)
    sx, sy = to_x(to_2), to_y(to_4)
    d_third = grads_by_right([(now(turned_a), turned_b)], (g_a, g_b), cut, width)

    def join(to_up, to_down, up, down):
        a, b = now(up, down)
        return pin(plus(to_up, a)), pin(plus(to_down, b))

    def join_part(m, up, down, moved):
        a, b = now(*moved)
        return pin(plus(up[m], a[m])), pin(plus(down[m], b[m]))

    end(sx, sy, *pair1, *d_third)

    d_third = [d[0] for d in now(*d_third)]
    third1 = gather(d_third[1], d_third[3], 1)
    first2 = gather(*join_part(0, d_pair[2], d_pair[2], pair1), 2)
    ready = join_part(1, d_pair[2], d_pair[2], pair1)
    grad_mid, gb = mid_back_rows((keep, got, *now(sx, sy)), out_grad, mid, branch, r_attn, dest)
    bx, by, bc = to_x(gb), to_y(gb), to_core(gb)
    o_give = sglu_last(now(prod_b), w_third)
    o_keep = sglu_last(now(prod_a), w_third)

    end(bx, by, bc, *third1, *first2, o_keep, o_give, *ready)

    second2 = gather(*now(*ready), 2)
    ax, ay = now(bx, by)
    bd = to_x(ay[:h2]), to_y(ax[h2:])
    bxyc = to_core(jnp.concatenate([ax, ay]))
    bdc = to_core(jnp.concatenate(bd))
    gb_a = pin(jnp.concatenate([gb, bx, by, *bd]))
    gb_b = pin(jnp.concatenate([bc, bxyc, bdc]))
    ready = join(d_third[2], d_third[2], *third1)
    end(*second2, gb_a, gb_b, *ready)

    third2 = gather(*now(*ready), 2)
    o_got = to_core(now(o_give))
    ga, gg, mixed, d_term, d_leaving = attend_back_rows(
        (now(gb_a), gb_b), w_out, (attn_a, attn_b), gate, qkv, at
    )
    d_out = grads_out(mixed, (gb_a, gb_b), width).reshape(2, 2, few, width)
    ready = join(d_pair[3][0], d_pair[1][0], *first2)
    core0 = plan.c == 0
    w_keep = jnp.where(core0, d_out[:, 0], d_out[:, 1])
    w_got = to_core(jnp.where(core0, d_out[:, 1], d_out[:, 0]))
    end(*third2, d_leaving, o_got, w_keep, w_got, *ready)

    first3 = gather(*now(*ready), 3)
    w_got = now(w_got)
    planes = jnp.concatenate([jnp.where(core0, w_keep, w_got), jnp.where(core0, w_got, w_keep)])
    planes = [pick(planes, k) for k in range(4)]
    planes = [pin(jnp.concatenate([v[:, :across], v[:, across:]])) for v in planes]
    d_entering = at.bring(now(d_leaving), True)

    def back_half(h, first, state):
        return project_back(
            h, first, raw, ga, gg, state, d_term, d_entering, w_in, width, at
        )

    gp_b, give = back_half(1, qkv, state_b)
    ready = join(d_pair[3][1], d_pair[1][1], *second2)
    end(*first3, give, *planes, *ready)

    second3 = gather(*now(*ready), 3)
    a_qkv, give = now(qkv, give)
    gp_a, keep = back_half(0, a_qkv, state_a)
    got = to_core(give)
    ready = join(d_third[3], d_third[1], *third2)
    end(*second3, keep, got, *ready)

    third3 = gather(*now(*ready), 3)
    keep, got = now(keep, got)
    u, v = first_step(keep, got)
    d_w = grads_by_left(norm1, (now(gp_a), gp_b), planes)
    end(u, v, *third3, *d_w)

    d_w = now(*d_w)
    w1 = gather(d_w[1], d_w[3], 1)
    to_2, to_4 = add_halves(keep, got, *now(u, v), width)
    sx, sy = to_x(to_2), to_y(to_4)
    sum_three = [
        total(d_pair[0][0], *now(*first3)),
        total(d_pair[0][1], *now(*second3)),
        total(d_third[0], *now(*third3)),
    ]
    sum_three = jnp.stack([v.astype(BF) for v in sum_three])
    my_three, to_three = plan.of_y(sum_three[:, :, :rows], sum_three[:, :, rows:])
    end(sx, sy, *w1, my_three, to_three)

    ready = join(d_w[2], d_w[2], *w1)
    w2 = gather(*ready, 2)
    three_got = to_y(now(to_three))
    o_keep = after(o_keep, *ready)
    ou, ov = first_step(o_keep, o_got)
    grad_norm1 = total(keep[:rows], got[:rows], *now(sx, sy))
    input_grad = grad_mid + srms_back(xf, plan.turn(grad_norm1))
    end(*w2, three_got, ou, ov)

    ready = join(d_w[3], d_w[1], *w2)
    w3 = gather(*ready, 3)
    to_2, to_4 = add_halves(after(o_keep, *ready), o_got, *now(ou, ov), width)
    ox, oy = to_x(to_2), to_y(to_4)
    sum_three = plan.by_y(my_three, now(three_got), 1)
    sum_pair = pin(sum_three[:2].swapaxes(1, 2)).astype(F32)
    sum_third = sum_three[2].astype(F32)
    end(*w3, ox, oy)

    sum_w = pin(total(d_w[0], *now(*w3)))
    sum_in = pin(sum_w[:deep].astype(BF)).reshape(8, few, across)
    sum_in = lax.all_to_all(sum_in, plan.tp, 0, 0, tiled=True)
    sum_out = jnp.concatenate([sum_w[deep : deep + few], sum_w[deep + few :]], axis=1)
    output = mid + plan.turn(total(o_keep[:rows], o_got[:rows], *now(ox, oy)))
    return output, input_grad, sum_in, sum_out, sum_pair, sum_third


class Plain:
    def __init__(self, wide, narrow):
        self.tp = ("narrow",)
        self.fs = ("wide",)
        self.size = narrow
        self.groups = wide

    def begin(self):
        self.p = lax.axis_index("narrow")
        self.group = lax.axis_index("wide")
        self.slot_ids = jnp.arange(self.size, dtype=jnp.int32)

    def turn(self, v):
        return v

    def rows_all(self, a):
        whole = lax.all_gather(a, "narrow", axis=0, tiled=True)
        return whole[: whole.shape[0] // 2], whole[whole.shape[0] // 2 :]

    def rows_sum(self, keep, give, kind=BF):
        total = lax.psum_scatter(
            jnp.concatenate([keep, give]), "narrow", scatter_dimension=0, tiled=True
        )
        return total.astype(F32)

    def attn_in(self, w):
        rows, cols = w.shape
        each = cols // 4 // self.size
        view = w.reshape(rows, 4, self.size, each).transpose(2, 0, 1, 3)
        view = view.reshape(self.size, rows, 4 * each)
        mine = lax.all_to_all(view, "narrow", 0, 0, tiled=True)
        mine = mine.reshape(self.size * rows, 4 * each)
        return cut4(lax.all_gather(mine, "wide", axis=0, tiled=True), 0)

    def attn_in_back(self, g):
        cols = g.shape[1]
        total = lax.psum_scatter(g.astype(BF), "wide", scatter_dimension=0, tiled=True)
        rows = total.shape[0] // self.size
        view = total.reshape(self.size, rows, cols)
        mine = lax.all_to_all(view, "narrow", 0, 0, tiled=True)
        mine = mine.reshape(self.size, rows, 4, cols // 4).transpose(1, 2, 0, 3)
        return mine.reshape(rows, cols * self.size).astype(F32)

    def attn_out(self, w):
        whole = lax.all_gather(w, ("wide", "narrow"), axis=0, tiled=True)
        each = whole.shape[0] // self.size
        return lax.dynamic_slice_in_dim(whole, self.p * each, each)

    def attn_out_back(self, g):
        each = g.shape[0]
        whole = jnp.zeros((each * self.size, g.shape[1]), BF)
        whole = lax.dynamic_update_slice_in_dim(whole, g.astype(BF), self.p * each, 0)
        total = lax.psum_scatter(whole, ("wide", "narrow"), scatter_dimension=0, tiled=True)
        return total.astype(F32)

    def sglu(self, pair, third):
        return pair, third

    def sglu_all(self, both, back):
        pair = lax.all_gather(both.swapaxes(1, 2), "wide", axis=2, tiled=True)
        third = lax.all_gather(back, "wide", axis=1, tiled=True)
        return cut4(pair, 2), cut4(third, 1)

    def pair_back(self, g):
        g = jnp.concatenate([g[k] for k in range(4)], axis=2)
        total = lax.psum_scatter(g, "wide", scatter_dimension=2, tiled=True)
        return total.swapaxes(1, 2).astype(F32)

    def third_back(self, g):
        g = jnp.concatenate([g[k] for k in range(4)], axis=1)
        total = lax.psum_scatter(g, "wide", scatter_dimension=1, tiled=True)
        return total.astype(F32)


def plain_layer(plan, places, lengths, inputs, out_grad, attn_in, attn_out, sglu_in, sglu_out):
    rows, width = inputs.shape
    at = places(lengths)
    w_out = plan.attn_out(attn_out.astype(BF))
    w_in = plan.attn_in(attn_in.astype(BF))
    w_pair, w_third = plan.sglu_all(sglu_in.astype(BF), sglu_out.astype(BF))
    xf = inputs.astype(F32)
    norm1 = plan.rows_all(plan.turn((xf * inverse_rms(xf)).astype(BF)))
    grad_rows = plan.rows_all(plan.turn(out_grad))
    raw, gate, qkv, term, leaving = project(norm1, w_in, at)
    entering = at.bring(leaving, False)
    attn, branch, state = [None] * 2, [None] * 2, [None] * 2
    for h in (1, 0):
        attn[h], branch[h], state[h] = attend(h, qkv, gate, term, entering, w_out, at)
    square = plan.rows_sum(*[strip_sum(v) for v in branch], F32)
    branch = plan.rows_sum(*[v[:, :width] for v in branch])
    r_attn = lax.rsqrt(square / width + EPS)
    mid = xf + r_attn * branch
    r_mid = inverse_rms(mid)
    norm2 = plan.rows_all(plan.turn((mid * r_mid).astype(BF)))

    product, turned, grad_first, grad_second, back = [[None] * 2 for _ in range(5)]
    for h in (1, 0):
        product[h], turned[h], grad_first[h], grad_second[h], back[h] = sglu_rows(
            norm2[h], grad_rows[h], w_pair, w_third
        )
    cut = width // 4
    sum_third = plan.third_back([g[0] for g in grads_by_right([turned], grad_rows, cut, width)])
    grad_norm2 = plan.rows_sum(*back)
    sum_pair = plan.pair_back(grads_by_right([grad_first, grad_second], norm2, cut, width))

    grad_mid = out_grad.astype(F32) + srms_back(mid, plan.turn(grad_norm2))
    grad_branch = grad_mid.astype(BF)
    inward = jnp.mean(grad_branch.astype(F32) * branch, axis=1, keepdims=True)
    extra = pieces(r_attn) + pieces(r_attn * r_attn * r_attn * inward)
    extra.append(jnp.zeros((rows, 128 - len(extra)), BF))
    grad_branch = jnp.concatenate([grad_branch] + extra, axis=1)
    grad_branch = plan.rows_all(grad_branch)
    branch_out = plan.rows_sum(*[sglu_last(v, w_third) for v in product])
    output = mid + plan.turn(branch_out)
    grad_attn, grad_gate, mixed, d_term, d_leaving = attend_back_rows(
        grad_branch, w_out, attn, gate, qkv, at
    )
    d_entering = at.bring(d_leaving, True)
    grad_pre, back = [None] * 2, [None] * 2
    for h in (1, 0):
        grad_pre[h], back[h] = project_back(
            h, qkv, raw, grad_attn, grad_gate, state[h], d_term, d_entering, w_in, width, at
        )
    none = [jnp.zeros((16, grad_pre[0].shape[1]), BF)] * 4
    grad_win = jnp.concatenate([g[:cut] for g in grads_by_left(norm1, grad_pre, none)])
    sum_in = plan.attn_in_back(grad_win)
    sum_out = plan.attn_out_back(grads_out(mixed, grad_branch, width))
    grad_norm1 = plan.rows_sum(*back)
    input_grad = grad_mid + srms_back(xf, plan.turn(grad_norm1))
    return output, input_grad, sum_in, sum_out, sum_pair, sum_third


def per_device(plan, layer, *args):
    inputs, out_grad, seq_lengths, decay_rate = args[:4]
    weights, moments, averages = args[4:8], args[8:12], args[12:16]
    plan.begin()
    rows, width = inputs.shape
    plan.own = decay_rate.shape[0] // plan.size

    def places(lengths):
        return Places(plan, lengths, decay_rate, rows)

    output, input_grad, *grads = layer(plan, places, seq_lengths, inputs, out_grad, *weights)
    tokens = plan.size * rows * plan.groups
    fans = (width, width, width, weights[3].shape[0] * lax.axis_size(plan.narrow))
    new = []
    for w, m, a, grad, fan in zip(weights, moments, averages, grads, fans):
        if grad.shape == w.shape:
            new.append(renew(w, m, a, grad, fan, tokens))
        else:
            new.append(renew_turned(grad, w, m, a, fan, tokens))
    return (output, input_grad) + tuple(n[i] for i in range(3) for n in new)


def solution(mesh):
    wide, narrow = mesh.shape["wide"], mesh.shape["narrow"]
    if (wide, narrow) == (8, 4):
        mesh = Mesh(mesh.devices.reshape(4, 2, 2, 2), ("z", "y", "x", "c"))
        plan, layer, w, n = Square(), square_layer, ("z", "y"), ("x", "c")
    else:
        plan, layer, w, n = Plain(wide, narrow), plain_layer, ("wide",), ("narrow",)
    plan.narrow = n
    by_rows = P(w + n, None)
    pair, third = P(None, w, n), P(n, w)
    weights = (by_rows, by_rows, pair, third)

    def run(*args):
        return per_device(plan, layer, *args)

    return jax.shard_map(
        run,
        mesh=mesh,
        in_specs=(by_rows, by_rows, P(), P()) + weights * 3,
        out_specs=(by_rows, by_rows) + weights * 3,
        check_vma=False,
    )
```

```python
import math

import jax
import jax.numpy as jnp
from jax import lax
from jax.experimental import pallas as pl
from jax.experimental.layout import Layout, with_layout_constraint
from jax.experimental.pallas import tpu as pltpu
from jax.sharding import Mesh
from jax.sharding import PartitionSpec as P

BLOCK = 256
EPS = 1e-06
MU = 0.9
BETA = 0.8
HIGH = lax.Precision.HIGHEST
BF = jnp.bfloat16
F32 = jnp.float32
SWAP = [(0, 1), (1, 0)]
XORS = (0, 2, 4, 6, 1, 3, 5, 7)
MEETS = ((0, 1, 2, 3), (1, 0, 2, 3), (2, 3, 1, 0), (3, 2, 1, 0))
PLACES = ((0, 1, 2, 3), (1, 0, 2, 3), (3, 2, 0, 1), (3, 2, 1, 0))


def dot(a, b, dims=((1,), (0,))):
    return lax.dot_general(a, b, (dims, ((), ())), preferred_element_type=F32)


def inverse_rms(v):
    return lax.rsqrt(jnp.mean(v * v, axis=-1, keepdims=True) + EPS)


def srms_back(v, grad):
    r = inverse_rms(v)
    return r * grad - v * (r * r * r) * jnp.mean(grad * v, axis=-1, keepdims=True)


def renew(weight, moment, average, grad, fan, tokens):
    step = 0.4 / math.sqrt(fan * tokens)
    moment_new = MU * moment + grad
    weight_new = weight - step * (grad + MU * moment_new)
    average_new = BETA * average + (1.0 - BETA) * weight_new
    return (moment_new, weight_new, average_new)


ROWS = 256
HALF = 4
HD = 128
VMEM = 56 * 1024 * 1024
EXTRA = 128


def pin(v):
    return with_layout_constraint(v, Layout(major_to_minor=tuple(range(v.ndim))))


def after(value, *done):
    return lax.optimization_barrier((value,) + done)[0]


class Clock:
    def __init__(self):
        self.token = jnp.zeros((8, 128), F32)

    def now(self, *values):
        out = [lax.optimization_barrier((v, self.token))[0] for v in values]
        return out if len(out) > 1 else out[0]

    def end(self, *done):
        self.token = lax.optimization_barrier((self.token,) + done)[0]


def block_spec(shape):
    return pl.BlockSpec(shape, lambda i: (i,) + (0,) * (len(shape) - 1))


def whole_spec(a):
    return pl.BlockSpec(a.shape, lambda i: (0,) * a.ndim, pipeline_mode=pl.Buffered(1))


def scalar_spec():
    return pl.BlockSpec(memory_space=pltpu.SMEM)


def call(kernel, steps, ins, outs, flops):
    moved = sum(a.size * a.dtype.itemsize for a, _ in ins)
    moved += sum(math.prod(s) * jnp.dtype(d).itemsize for s, d, _ in outs)
    return pl.pallas_call(
        kernel,
        grid=(steps,),
        in_specs=[s for _, s in ins],
        out_specs=[b if isinstance(b, pl.BlockSpec) else block_spec(b) for _, _, b in outs],
        out_shape=[jax.ShapeDtypeStruct(s, d) for s, d, _ in outs],
        compiler_params=pltpu.CompilerParams(
            vmem_limit_bytes=VMEM, dimension_semantics=("arbitrary",)
        ),
        cost_estimate=pl.CostEstimate(
            flops=int(flops), bytes_accessed=int(moved), transcendentals=0
        ),
    )(*[a for a, _ in ins])


NT = ((1,), (1,))
TN = ((0,), (0,))


def mask_of(fade, seg_c, seg_r):
    return jnp.where(seg_c == seg_r, fade, 0.0)


def pair_spec(shape, late):
    if late:
        return pl.BlockSpec(shape, lambda i: (jnp.maximum(i - HALF, 0),) + (0,) * (len(shape) - 1))
    return pl.BlockSpec(shape, lambda i: (jnp.minimum(i, HALF - 1),) + (0,) * (len(shape) - 1))


def half_spec(shape, h):
    return pl.BlockSpec(shape, lambda i: (i + h * HALF,) + (0,) * (len(shape) - 1))


def project(n1, w_in, at):
    own = at.own
    cols = own * HD
    parts = len(w_in)
    width = n1[0].shape[1]
    deep = width // parts

    def kernel(*refs):
        a_ref, b_ref, w_refs = refs[0], refs[1], refs[2 : 2 + parts]
        seg_ref, ramp_ref, last_ref, reach_ref = refs[2 + parts : 6 + parts]
        raw_ref, gate_ref, qkv_ref, term_ref, leaving_ref = refs[6 + parts :]
        i = pl.program_id(0)
        pre = None
        for k in range(parts):
            some = slice(k * deep, (k + 1) * deep)
            x = jnp.where(i < HALF, a_ref[:, some], b_ref[:, some])
            new = dot(x, w_refs[k][...])
            pre = new if pre is None else pre + new
        pq, pk, pv = pre[:, :cols], pre[:, cols : 2 * cols], pre[:, 2 * cols : 3 * cols]
        raw_ref[...] = pre[:, : 2 * cols]
        gate_ref[...] = pre[:, 3 * cols :]
        key = (pk * jax.nn.sigmoid(pk)).astype(BF)
        value = pv.astype(BF)
        qkv_ref[:, :cols] = (pq * jax.nn.sigmoid(pq)).astype(BF)
        qkv_ref[:, cols : 2 * cols] = key
        qkv_ref[:, 2 * cols :] = value

        @pl.when(i == 0)
        def _():
            leaving_ref[...] = jnp.zeros_like(leaving_ref)

        for j in range(own):
            leave = jnp.where(seg_ref[0] == last_ref[i], ramp_ref[:, own + j : own + j + 1], 0.0)
            head = slice(j * HD, (j + 1) * HD)
            scaled = (key[:, head].astype(F32) * leave).astype(BF)
            term = dot(scaled, value[:, head], TN)
            term_ref[0, j] = term
            leaving_ref[j] += reach_ref[j, i] * term

    some = pl.BlockSpec((deep, 4 * cols), lambda i: (0, 0), pipeline_mode=pl.Buffered(1))
    ins = [(v, pair_spec((ROWS, width), late)) for late, v in enumerate(n1)]
    ins += [(w, some) for w in w_in]
    ins += [(at.cols, block_spec((1, ROWS, 1))), (at.ramps, whole_spec(at.ramps))]
    ins += [(v, scalar_spec()) for v in (at.last, at.out_reach)]
    n = 2 * HALF
    outs = [
        ((n * ROWS, 2 * cols), F32, (ROWS, 2 * cols)),
        ((n * ROWS, cols), F32, (ROWS, cols)),
        ((n * ROWS, 3 * cols), BF, (ROWS, 3 * cols)),
        ((n, own, HD, HD), F32, (1, own, HD, HD)),
        ((own, HD, HD), F32, pl.BlockSpec((own, HD, HD), lambda i: (0, 0, 0))),
    ]
    return call(kernel, n, ins, outs, 4 * n1[0].size * 4 * cols)


def combine(weights, terms, more, reach):
    state = reach * more
    for c in range(2 * HALF):
        state = state + weights(c) * terms(c)
    return state


def attend(h, qkv, gate, term, entering, w_out, at):
    own = at.own
    cols = own * HD
    width = w_out.shape[1]

    def kernel(
        qkv_ref, gate_ref, term_ref, more_ref, w_ref, sc_ref, sr_ref, fade_ref, ramp_ref,
        prev_ref, inner_ref, reach_ref, attn_ref, branch_ref, state_ref,
    ):
        i = pl.program_id(0) + h * HALF
        for j in range(own):
            head = slice(j * HD, (j + 1) * HD)
            q = qkv_ref[:, j * HD : (j + 1) * HD]
            k = qkv_ref[:, cols + j * HD : cols + (j + 1) * HD]
            v = qkv_ref[:, 2 * cols + j * HD : 2 * cols + (j + 1) * HD]
            state = combine(
                lambda c: inner_ref[j, i * 2 * HALF + c],
                lambda c: term_ref[c, j],
                more_ref[j],
                reach_ref[j, i],
            ).astype(BF)
            state_ref[0, j] = state
            enter = jnp.where(sc_ref[0] == prev_ref[i], ramp_ref[:, j : j + 1], 0.0)
            weights = (dot(q, k, NT) * mask_of(fade_ref[j], sc_ref[0], sr_ref[0])).astype(BF)
            attn_ref[:, head] = dot(weights, v) + enter * dot(q, state)
        attn = attn_ref[...]
        branch_ref[:, :width] = dot((attn * gate_ref[...]).astype(BF), w_ref[...]).astype(BF)
        rest = jnp.sum(attn * attn, axis=1, keepdims=True)
        lane = lax.broadcasted_iota(jnp.int32, (ROWS, EXTRA), 1)
        strip = jnp.zeros((ROWS, EXTRA), F32)
        for n in range(3):
            top = rest.astype(BF).astype(F32)
            strip = jnp.where(lane == n, top, strip)
            rest = rest - top
        branch_ref[:, width:] = strip.astype(BF)

    n = HALF
    ins = [
        (qkv, half_spec((ROWS, 3 * cols), h)),
        (gate, half_spec((ROWS, cols), h)),
        (term, whole_spec(term)),
        (entering, whole_spec(entering)),
        (w_out, whole_spec(w_out)),
        (at.cols, half_spec((1, ROWS, 1), h)),
        (at.rows, half_spec((1, 1, ROWS), h)),
        (at.fade, whole_spec(at.fade)),
        (at.ramps, whole_spec(at.ramps)),
    ] + [(v, scalar_spec()) for v in (at.prev, at.inner, at.in_reach)]
    outs = [
        ((n * ROWS, cols), F32, (ROWS, cols)),
        ((n * ROWS, width + EXTRA), BF, (ROWS, width + EXTRA)),
        ((n, own, HD, HD), BF, (1, own, HD, HD)),
    ]
    return call(kernel, n, ins, outs, 2 * n * ROWS * cols * (width + 2 * ROWS))


def sglu_rows(n2, g, w_pair, w_third):
    parts = len(w_pair)
    _, hidden, deep = w_pair[0].shape
    block = 2 * ROWS

    def kernel(*refs):
        x_ref, g_ref = refs[:2]
        both, three = (refs[2 + k * parts : 2 + (k + 1) * parts] for k in range(2))
        prod_ref, prod_t, gf_t, gs_t, back_ref = refs[2 + 2 * parts :]
        first = second = grad = None
        for k in range(parts):
            at = slice(k * deep, (k + 1) * deep)
            x, gk = x_ref[:, at], g_ref[:, at]
            a, b, c = dot(x, both[k][0], NT), dot(x, both[k][1], NT), dot(gk, three[k][...], NT)
            first = a if first is None else first + a
            second = b if second is None else second + b
            grad = c if grad is None else grad + c
        prod = (first * second).astype(BF)
        gf = (grad * second).astype(BF)
        gs = (grad * first).astype(BF)
        prod_ref[...] = prod
        prod_t[...] = prod.T
        gf_t[...] = gf.T
        gs_t[...] = gs.T
        for k in range(parts):
            at = slice(k * deep, (k + 1) * deep)
            back_ref[:, at] = (dot(gf, both[k][0]) + dot(gs, both[k][1])).astype(BF)

    n = n2.shape[0] // block
    width = n2.shape[1]
    ins = [(n2, block_spec((block, width))), (g, block_spec((block, width)))]
    ins += [(w, whole_spec(w)) for w in w_pair + w_third]
    outs = [((n * block, hidden), BF, (block, hidden))]
    turned = pl.BlockSpec((hidden, block), lambda i: (0, i))
    outs += [((hidden, n * block), BF, turned)] * 3
    outs += [((n * block, width), BF, (block, width))]
    return call(kernel, n, ins, outs, 10 * n2.size * hidden)


def sglu_last(product, w_third):
    parts = len(w_third)
    deep = w_third[0].shape[1]
    block = 2 * ROWS

    def kernel(*refs):
        for k in range(parts):
            refs[-1][:, k * deep : (k + 1) * deep] = dot(refs[0][...], refs[1 + k][...]).astype(BF)

    n, width = product.shape[0] // block, parts * deep
    ins = [(product, block_spec((block, product.shape[1])))]
    ins += [(w, whole_spec(w)) for w in w_third]
    return call(
        kernel, n, ins, [((n * block, width), BF, (block, width))], 2 * product.size * width
    )[0]


def attend_back_rows(gb, w_out, attn, gate, qkv, at):
    own = at.own
    cols = own * HD
    width = w_out.shape[1]

    def kernel(
        gb_a, gb_b, w_ref, attn_a, attn_b, gate_ref, qkv_ref, sc_ref, ramp_ref, prev_ref, reach_ref,
        ga_ref, gg_ref, mixed_ref, term_ref, leaving_ref,
    ):
        i = pl.program_id(0)
        early = i < HALF
        extra = jnp.where(early, gb_a[:, width:], gb_b[:, width:]).astype(F32)
        r = extra[:, 0:1] + extra[:, 1:2] + extra[:, 2:3]
        pull = extra[:, 3:4] + extra[:, 4:5] + extra[:, 5:6]
        gm = dot(jnp.where(early, gb_a[:, :width], gb_b[:, :width]), w_ref[...], NT)
        attn, gate = jnp.where(early, attn_a[...], attn_b[...]), gate_ref[...]
        normed = r * attn
        gg_ref[...] = (gm * normed).astype(BF)
        mixed_ref[...] = (normed * gate).astype(BF)
        ga = (r * (gm * gate) - attn * pull).astype(BF)
        ga_ref[...] = ga

        @pl.when(i == 0)
        def _():
            leaving_ref[...] = jnp.zeros_like(leaving_ref)

        for j in range(own):
            enter = jnp.where(sc_ref[0] == prev_ref[i], ramp_ref[:, j : j + 1], 0.0)
            q = qkv_ref[:, j * HD : (j + 1) * HD].astype(F32)
            term = dot((q * enter).astype(BF), ga[:, j * HD : (j + 1) * HD], TN)
            term_ref[0, j] = term
            leaving_ref[j] += reach_ref[j, i] * term

    n = 2 * HALF
    ins = [(v, pair_spec((ROWS, v.shape[1]), late)) for late, v in enumerate(gb)]
    ins += [(w_out, whole_spec(w_out))]
    ins += [(v, pair_spec((ROWS, cols), late)) for late, v in enumerate(attn)]
    ins += [
        (gate, block_spec((ROWS, cols))),
        (qkv, block_spec((ROWS, 3 * cols))),
        (at.cols, block_spec((1, ROWS, 1))),
        (at.ramps, whole_spec(at.ramps)),
    ] + [(v, scalar_spec()) for v in (at.prev, at.in_reach)]
    outs = [((n * ROWS, cols), BF, (ROWS, cols))] * 3
    outs += [((n, own, HD, HD), F32, (1, own, HD, HD))]
    outs += [((own, HD, HD), F32, pl.BlockSpec((own, HD, HD), lambda i: (0, 0, 0)))]
    return call(kernel, n, ins, outs, 2 * n * ROWS * cols * width)


def project_back(h, qkv, raw, ga, gg, state, term, entering, w_in, width, at):
    own = at.own
    cols = own * HD
    parts = len(w_in)
    deep = width // parts

    def kernel(*refs):
        qkv_ref, raw_ref, ga_ref, gg_ref, state_ref, term_ref, more_ref = refs[:7]
        w_refs = refs[7 : 7 + parts]
        sc_ref, sr_ref, fade_ref, ramp_ref = refs[7 + parts : 11 + parts]
        prev_ref, last_ref, inner_ref, reach_ref, gp_ref, back_ref = refs[11 + parts :]
        i = pl.program_id(0) + h * HALF
        for j in range(own):
            head = slice(j * HD, (j + 1) * HD)
            kt = slice(cols + j * HD, cols + (j + 1) * HD)
            vt = slice(2 * cols + j * HD, 2 * cols + (j + 1) * HD)
            q, k, v = qkv_ref[:, head], qkv_ref[:, kt], qkv_ref[:, vt]
            g = ga_ref[:, head]
            mask = mask_of(fade_ref[j], sc_ref[0], sr_ref[0])
            enter = jnp.where(sc_ref[0] == prev_ref[i], ramp_ref[:, j : j + 1], 0.0)
            leave = jnp.where(sc_ref[0] == last_ref[i], ramp_ref[:, own + j : own + j + 1], 0.0)
            later = combine(
                lambda c: inner_ref[j, c * 2 * HALF + i],
                lambda c: term_ref[c, j],
                more_ref[j],
                reach_ref[j, i],
            ).astype(BF)
            weights = (dot(q, k, NT) * mask).astype(BF)
            gs = (dot(g, v, NT) * mask).astype(BF)
            gq = dot(gs, k) + enter * dot(g, state_ref[0, j], NT)
            gk = dot(gs, q, TN) + leave * dot(v, later, NT)
            gv = dot(weights, g, TN) + leave * dot(k, later)
            rq, rk = raw_ref[:, head], raw_ref[:, kt]
            sq, sk = jax.nn.sigmoid(rq), jax.nn.sigmoid(rk)
            gp_ref[:, head] = (gq * (sq * (1.0 + rq * (1.0 - sq)))).astype(BF)
            gp_ref[:, kt] = (gk * (sk * (1.0 + rk * (1.0 - sk)))).astype(BF)
            gp_ref[:, vt] = gv.astype(BF)
        gp_ref[:, 3 * cols :] = gg_ref[...]
        for k in range(parts):
            some = slice(k * deep, (k + 1) * deep)
            back_ref[:, some] = dot(gp_ref[...], w_refs[k][...], NT).astype(BF)

    n = HALF
    some = pl.BlockSpec((deep, 4 * cols), lambda i: (0, 0), pipeline_mode=pl.Buffered(1))
    ins = [
        (qkv, half_spec((ROWS, 3 * cols), h)),
        (raw, half_spec((ROWS, 2 * cols), h)),
        (ga, half_spec((ROWS, cols), h)),
        (gg, half_spec((ROWS, cols), h)),
        (state, block_spec((1, own, HD, HD))),
        (term, whole_spec(term)),
        (entering, whole_spec(entering)),
    ] + [(w, some) for w in w_in]
    ins += [
        (at.cols, half_spec((1, ROWS, 1), h)),
        (at.rows, half_spec((1, 1, ROWS), h)),
        (at.fade, whole_spec(at.fade)),
        (at.ramps, whole_spec(at.ramps)),
    ]
    ins += [(v, scalar_spec()) for v in (at.prev, at.last, at.inner, at.out_reach)]
    outs = [
        ((n * ROWS, 4 * cols), BF, (ROWS, 4 * cols)),
        ((n * ROWS, width), BF, (ROWS, width)),
    ]
    return call(kernel, n, ins, outs, 2 * n * ROWS * 4 * cols * width)


def one_by_one(count, shape):
    spec = pl.BlockSpec(shape, lambda i: (0,) * len(shape), pipeline_mode=pl.Buffered(1))
    return [(shape, BF, spec) for _ in range(count)]


def grads_by_left(left, right, n, below=None):
    cut, cols = left[0].shape[1] // n, right[0].shape[1]
    more = 0 if below is None else 2 * below[0].shape[1]

    def kernel(*refs):
        l0, l1, r0, r1 = refs[:4]
        outs = refs[len(refs) - n :]
        grad = (dot(l0[...], r0[...], TN) + dot(l1[...], r1[...], TN)).astype(BF)
        for k in range(n):

            @pl.when(pl.program_id(0) == k)
            def _():
                outs[k][:cut] = grad
                if more:
                    a_ref, b_ref, from_a, row = refs[4:8]
                    part = jnp.where(from_a[k] == 1, a_ref[row[k]], b_ref[row[k]])
                    outs[k][cut : cut + more // 2] = part[:, :cols]
                    outs[k][cut + more // 2 :] = part[:, cols:]

    ins = [(a, pl.BlockSpec((a.shape[0], cut), lambda i: (0, i))) for a in left]
    ins += [(a, whole_spec(a)) for a in right]
    if more:
        ins += [(a, whole_spec(a)) for a in below[:2]] + [(a, scalar_spec()) for a in below[2:]]
    outs = one_by_one(n, (cut + more, cols))
    return call(kernel, n, ins, outs, 4 * left[0].size * cols)


def grads_by_right(lefts, right, cut, first, n, step=1):
    count = len(lefts)
    tall = lefts[0][0].shape[0]

    def kernel(*refs):
        r0, r1 = refs[2 * count : 2 * count + 2]
        outs = refs[2 * count + 2 :]
        for m in range(count):
            l0, l1 = refs[2 * m : 2 * m + 2]
            grad = (dot(l0[...], r0[...]) + dot(l1[...], r1[...])).astype(BF)
            for k in range(n):

                @pl.when(pl.program_id(0) == k)
                def _():
                    outs[k][m] = grad

    ins = [(a, whole_spec(a)) for left in lefts for a in left]
    ins += [(a, pl.BlockSpec((a.shape[0], cut), lambda i: (0, first + step * i))) for a in right]
    outs = one_by_one(n, (count, tall, cut))
    return call(kernel, n, ins, outs, 4 * count * right[0].size * tall)


def grads_out(left, right, width):
    def kernel(l0, l1, r0, r1, out):
        out[...] = (dot(l0[...], r0[...], TN) + dot(l1[...], r1[...], TN)).astype(BF)

    cut, (rows, tall) = width // 4, left.shape
    spec = lambda rows: pl.BlockSpec((rows, cut), lambda i: (0, i))
    half = lambda k: pl.BlockSpec((rows // 2, tall), lambda i: (k, 0))
    ins = [(left, half(k)) for k in (0, 1)] + [(a, spec(a.shape[0])) for a in right]
    return call(kernel, 4, ins, [((tall, width), BF, spec(tall))], 2 * left.size * width)[0]


def add_strips(width, *parts):
    total = parts[0][:, :width].astype(F32)
    for p in parts[1:]:
        total = total + p[:, :width].astype(F32)
    out = [total.astype(BF)]
    if parts[0].shape[1] > width:
        rest = 0.0
        for p in parts:
            for n in range(3):
                rest = rest + p[:, width + n : width + n + 1].astype(F32)
        lane = lax.broadcasted_iota(jnp.int32, (total.shape[0], EXTRA), 1)
        strip = jnp.zeros((total.shape[0], EXTRA), F32)
        for n in range(3):
            top = rest.astype(BF).astype(F32)
            strip = jnp.where(lane == n, top, strip)
            rest = rest - top
        out.append(strip.astype(BF))
    return out


def add_last(a, b, width):
    n, wide = a.shape[0] // ROWS, a.shape[1]
    half = ROWS // 2

    def kernel(a_ref, b_ref, low_ref, high_ref):
        parts = add_strips(width, a_ref[...], b_ref[...])
        for v, at in zip(parts, (slice(0, width), slice(width, wide))):
            low_ref[:, at] = v[:half]
            high_ref[:, at] = v[half:]

    block = pl.BlockSpec((ROWS, wide), lambda i: (n - 1, 0))
    one = pl.BlockSpec((half, wide), lambda i: (0, 0))
    return call(kernel, 1, [(a, block), (b, block)], [((half, wide), BF, one)] * 2, ROWS * wide)


def add_halves(a, b, u, v, width):
    wide = a.shape[1]
    half = ROWS // 2

    def kernel(a2, a4, b2, b4, u_ref, v_ref, to_2, to_4):
        low, high = slice(0, half), slice(half, ROWS)
        for out, rows, terms in (
            (to_2, low, (a2[low], b2[low])),
            (to_2, high, (a2[high], b2[high], v_ref[...])),
            (to_4, low, (a4[low], b4[low], u_ref[...])),
            (to_4, high, (a4[high], b4[high])),
        ):
            parts = add_strips(width, *terms)
            for p, at in zip(parts, (slice(0, width), slice(width, wide))):
                out[rows, at] = p

    spec = lambda k: pl.BlockSpec((ROWS, wide), lambda i: (k, 0))
    ins = [(t, spec(k)) for t in (a, b) for k in (1, 2)] + [(u, whole_spec(u)), (v, whole_spec(v))]
    return call(kernel, 1, ins, [((ROWS, wide), BF, spec(0))] * 2, ROWS * wide)


def strip_of(column):
    lane = lax.broadcasted_iota(jnp.int32, (column[0].shape[0], EXTRA), 1)
    strip = jnp.zeros(lane.shape, F32)
    for m, rest in enumerate(column):
        for n in range(3):
            top = rest.astype(BF).astype(F32)
            strip = jnp.where(lane == 3 * m + n, top, strip)
            rest = rest - top
    return strip.astype(BF)


def mid_rows(sums, inputs, dest):
    width = inputs.shape[1]
    cut = width // 4
    block = ROWS // 2

    def kernel(a, b, c, d, x_ref, dest_ref, mid_ref, branch_ref, scale_ref, norm_ref):
        branch = square = None
        for ref in (a, b, c, d):
            part = ref[:, :width].astype(F32)
            extra = ref[:, width:].astype(F32)
            more = extra[:, 0:1] + extra[:, 1:2] + extra[:, 2:3]
            branch = part if branch is None else branch + part
            square = more if square is None else square + more
        r = lax.rsqrt(square / width + EPS)
        mid = x_ref[...].astype(F32) + r * branch
        branch_ref[...] = branch.astype(BF)
        scale_ref[...] = jnp.broadcast_to(r, (block, EXTRA))
        mid_ref[...] = mid
        norm = (mid * inverse_rms(mid)).astype(BF)
        for p in range(4):
            to = pl.ds(pl.multiple_of(dest_ref[p] * cut, cut), cut)
            norm_ref[:, to] = norm[:, p * cut : (p + 1) * cut]

    ins = [(v, block_spec((block, width + EXTRA))) for v in sums]
    ins += [(inputs, block_spec((block, width))), (dest, scalar_spec())]
    outs = [
        ((ROWS, width), F32, (block, width)),
        ((ROWS, width), BF, (block, width)),
        ((ROWS, EXTRA), F32, (block, EXTRA)),
        ((ROWS, width), BF, (block, width)),
    ]
    return call(kernel, 2, ins, outs, 20 * ROWS * width)


def mid_back_rows(sums, out_grad, mid, branch, scale, dest):
    width = mid.shape[1]
    cut = width // 4
    block = ROWS // 2

    def kernel(a, b, c, d, g_ref, mid_ref, branch_ref, scale_ref, dest_ref, grad_ref, out_ref):
        parts = []
        for p in range(4):
            at = pl.ds(pl.multiple_of(dest_ref[p] * cut, cut), cut)
            part = a[:, at].astype(F32)
            for ref in (b, c, d):
                part = part + ref[:, at].astype(F32)
            parts.append(part)
        grad = g_ref[...].astype(F32) + srms_back(mid_ref[...], jnp.concatenate(parts, axis=1))
        grad_ref[...] = grad
        low = grad.astype(BF)
        out_ref[:, :width] = low
        inward = low.astype(F32) * branch_ref[...].astype(F32)
        inward = jnp.mean(inward, axis=1, keepdims=True)
        r = scale_ref[:, 0:1]
        out_ref[:, width:] = strip_of([r, r * r * r * inward])

    ins = [(v, block_spec((block, width))) for v in (*sums, out_grad, mid, branch)]
    ins += [(scale, block_spec((block, EXTRA))), (dest, scalar_spec())]
    outs = [
        ((ROWS, width), F32, (block, width)),
        ((ROWS, width + EXTRA), BF, (block, width + EXTRA)),
    ]
    return call(kernel, 2, ins, outs, 20 * ROWS * width)


def renew_turned(grad, weight, moment, average, fan, tokens):
    few, total = weight.shape
    block = 16

    def kernel(g_ref, w_ref, m_ref, a_ref, m_new, w_new, a_new):
        for p in range(8):
            for t in range(4):
                for j in range(2):
                    col = t * (total // 4) + (8 * (p % 2) + 4 * j + p // 2) * HD
                    to = slice(col, col + HD)
                    at = slice((2 * t + j) * HD, (2 * t + j + 1) * HD)
                    new = renew(
                        w_ref[:, to], m_ref[:, to], a_ref[:, to], g_ref[p, :, at].astype(F32),
                        fan, tokens,
                    )
                    m_new[:, to], w_new[:, to], a_new[:, to] = new

    ins = [(grad, pl.BlockSpec((8, block, grad.shape[2]), lambda i: (0, i, 0)))]
    ins += [(v, block_spec((block, total))) for v in (weight, moment, average)]
    outs = [((few, total), F32, (block, total))] * 3
    return call(kernel, few // block, ins, outs, 10 * weight.size)


def cut4(v, axis):
    n = v.shape[axis] // 4
    return [lax.slice_in_dim(v, k * n, (k + 1) * n, axis=axis) for k in range(4)]


def strip_sum(v):
    strip = v[:, v.shape[1] - EXTRA :].astype(F32)
    return strip[:, 0:1] + strip[:, 1:2] + strip[:, 2:3]


def pieces(v):
    out = []
    for _ in range(3):
        top = lax.reduce_precision(v, 8, 7)
        out.append(top.astype(BF))
        v = v - top
    return out


class Places:
    def __init__(self, plan, seq_lengths, decay_rate, rows):
        size = plan.size
        group_rows = size * rows
        tokens = group_rows * plan.groups
        ends = jnp.cumsum(seq_lengths)

        def seg_at(place):
            mark = jnp.sum((place[..., None] >= ends).astype(jnp.int32), axis=-1)
            return jnp.where(place < 0, -1, mark)

        first_block = plan.group * size
        blocks = first_block + plan.slot_ids
        seg = seg_at(blocks[:, None] * rows + jnp.arange(rows, dtype=jnp.int32)[None, :])
        prev = seg_at(blocks * rows - 1)
        last = seg[:, rows - 1]
        head_ids = plan.head_ids if hasattr(plan, "head_ids") else plan.own * plan.p + jnp.arange(plan.own)
        rate = jnp.take(decay_rate, head_ids)

        def reach(gap, same):
            return jnp.where(
                same & (gap >= 0), jnp.exp(-rate[:, None, None] * (rows * jnp.maximum(gap, 0))), 0.0
            )

        inner = reach(
            (blocks[:, None] - blocks[None, :] - 1).astype(F32)[None],
            (prev[:, None] == last[None, :])[None],
        )
        border = seg_at((first_block + size) * rows - 1)
        out_reach = reach(
            (first_block + size - 1 - blocks).astype(F32)[None, None], (last == border)[None, None]
        )[:, 0]
        entry = seg_at(first_block * rows - 1)
        in_reach = reach((blocks - first_block).astype(F32)[None, None], (prev == entry)[None, None])[
            :, 0
        ]
        longest = tokens // 4
        hops = min(-(-longest // group_rows), plan.groups - 1)

        def hop_factor(j, ahead):
            if ahead:
                here, there = border, seg_at((first_block + j * size) * rows - 1)
            else:
                here, there = entry, seg_at((first_block - (j - 1) * size) * rows - 1)
            return jnp.where(here == there, jnp.exp(-rate * ((j - 1) * group_rows)), 0.0)

        def bring(total, ahead):
            n = plan.groups
            got = jnp.zeros_like(total)
            for j in range(1, hops + 1):
                pairs = [(i + j, i) if ahead else (i, i + j) for i in range(n - j)]
                part = lax.ppermute(total, plan.fs, pairs)
                got = got + hop_factor(j, ahead)[:, None, None] * part
            return got

        self.bring, self.hop = bring, hop_factor
        self.inner = inner.reshape(inner.shape[0], -1)
        self.out_reach, self.in_reach = out_reach, in_reach
        self.own = plan.own
        self.cols, self.rows = seg[:, :, None], seg[:, None, :]
        self.prev, self.last = prev, last
        step = jnp.arange(rows).astype(F32)
        spread = step[:, None] - step[None, :]
        fade = jnp.exp(-rate[:, None, None] * jnp.maximum(spread, 0.0)[None])
        self.fade = jnp.where((spread >= 0)[None], fade, 0.0)
        ramps = [jnp.exp(-rate[None] * step[:, None]), jnp.exp(-rate[None] * (rows - step)[:, None])]
        blank = jnp.zeros((rows, EXTRA - 2 * plan.own), F32)
        self.ramps = jnp.concatenate(ramps + [blank], axis=1)


class Square:
    def __init__(self):
        self.tp = ("y", "x", "c")
        self.fs = ("z",)
        self.size = 8
        self.groups = 4

    def begin(self):
        self.z = lax.axis_index("z")
        self.y = lax.axis_index("y")
        self.c = lax.axis_index("c")
        self.p = lax.axis_index(self.tp)
        self.q = self.p // 2
        self.group = self.z
        self.slot_ids = self.p ^ jnp.array(XORS, jnp.int32)
        self.head_ids = 8 * self.c + 4 * jnp.arange(2) + self.q
        self.order = jnp.array(MEETS, jnp.int32)[self.z]
        self.dest = jnp.array(PLACES, jnp.int32)[self.z]

    def turn(self, v, places):
        wide = v.shape[1] // 4
        return jnp.concatenate(
            [lax.dynamic_slice_in_dim(v, places[k] * wide, wide, axis=1) for k in range(4)], axis=1
        )

    def slots(self, own, one, two, three):
        outer = (self.z == 0) | (self.z == 3)
        return [
            own,
            one[0],
            pin(jnp.where(outer, two[0], one[1])),
            pin(jnp.where(outer, three, two[1])),
        ]

    def by_y(self, mine, got, axis):
        first = self.y == 0
        parts = [jnp.where(first, mine, got), jnp.where(first, got, mine)]
        return pin(jnp.concatenate(parts, axis=axis))

    def of_y(self, one, two):
        first = self.y == 0
        return pin(jnp.where(first, one, two)), pin(jnp.where(first, two, one))


def over(axis, pairs=SWAP):
    return lambda v: pin(lax.ppermute(pin(v), axis, pairs))


to_x, to_y, to_core = over("x"), over("y"), over("c")


to_pair = over("z", [(0, 1), (1, 0), (2, 3), (3, 2)])
to_middle = over("z", [(1, 2), (2, 1)])
outward = over("z", [(1, 0), (2, 3)])
inward_z = over("z", [(0, 1), (3, 2)])


def spread0(own):
    return to_pair(own), to_middle(own)


def spread1(one):
    return outward(one[1]), to_middle(one[0])


def spread2(two):
    return outward(two[1])


def gather1(g):
    return inward_z(g[3])


def gather2(g2, third):
    return inward_z(g2), to_middle(third)


def gather3(first, second):
    return to_pair(first), to_middle(second)


def plus(a, b):
    return (a.astype(F32) + b.astype(F32)).astype(BF)


def square_layer(plan, places, lengths, inputs, out_grad, attn_in, attn_out, sglu_in, sglu_out):
    rows, width = inputs.shape
    h2 = rows // 2
    cut = width // 4
    clock = Clock()
    now, end = clock.now, clock.end

    order, dest = plan.order, plan.dest

    def pick(stack, place):
        return lax.dynamic_index_in_dim(stack, place, 0, False)

    xf = inputs.astype(F32)
    n1 = pin(plan.turn((xf * inverse_rms(xf)).astype(BF), order))
    og = pin(plan.turn(out_grad, order))
    few = attn_in.shape[0]
    view = attn_in.astype(BF).reshape(few, 4, 2, 2, 4, HD).transpose(4, 2, 0, 1, 3, 5)
    own_in = lax.all_to_all(view.reshape(8, few, -1), plan.tp, 0, 0, tiled=True)
    own_in = own_in.reshape(8 * few, -1)
    deep, across = own_in.shape
    own_out = attn_out.astype(BF)
    own_w = pin(jnp.concatenate([own_in, own_out[:, :across], own_out[:, across:]]))
    end(own_w, n1, og)

    a_w, a_n1 = now(own_w, n1)
    w1 = spread0(a_w)
    nx, ny = to_x(a_n1), to_y(a_n1)
    at = places(now(lengths))
    hid = sglu_in.shape[2] // 2
    three = pin(now(sglu_in).astype(BF)).swapaxes(1, 2)
    three = jnp.concatenate([three, sglu_out.astype(BF)[None]])
    my_three, to_three = plan.of_y(three[:, :hid], three[:, hid:])
    tables = [at.cols, at.rows, at.prev, at.last, at.fade, at.ramps]
    tables += [at.inner, at.out_reach, at.in_reach, at.hop(1, False), at.hop(1, True)]
    end(*w1, nx, ny, my_three, to_three, *tables)

    w2 = spread1(now(*w1))
    ax, ay = now(nx, ny)
    nd = to_x(ay[:h2]), to_y(ax[h2:])
    end(*w2, *nd)

    w3 = spread2(now(*w2))
    a_og, a_three = now(og, to_three)
    gx = to_x(a_og)
    got = to_y(a_three)
    n1_a = pin(jnp.concatenate([n1, nx, ny, *now(*nd)]))
    norm1 = n1_a, to_core(n1_a)
    own_three = plan.by_y(my_three, got, 2)
    own_pair, own_third = pin(own_three[:2]), pin(own_three[2])
    end(w3, gx, *norm1, own_pair, own_third)

    pair1 = spread0(now(own_pair))
    gy = to_y(now(og))
    w_in = plan.slots(own_w, now(*w1), now(*w2), now(w3))
    outs = jnp.stack([w[deep:] for w in w_in])
    w_mine = [pick(outs, dest[2 * plan.c + j]) for j in (0, 1)]
    w_got = to_core(jnp.concatenate([pick(outs, dest[2 * (1 - plan.c) + j]) for j in (0, 1)]))
    core0 = plan.c == 0
    raw, gate, qkv, term, leaving = project((now(norm1[0]), norm1[1]), w_in, at)
    end(*pair1, gy, w_got, leaving)

    w_rows = []
    for j in (0, 1):
        got = w_got[j * 2 * few : (j + 1) * 2 * few]
        for half in (jnp.where(core0, w_mine[j], got), jnp.where(core0, got, w_mine[j])):
            w_rows.append(jnp.concatenate([half[:few], half[few:]], axis=1))
    w_out = pin(jnp.concatenate(w_rows))
    entering = at.bring(now(leaving), False)
    attn_b, give, state_b = attend(1, qkv, gate, term, entering, w_out, at)
    end(give)

    third1 = spread0(now(own_third))
    a_qkv, give = now(qkv, give)
    attn_a, keep, state_a = attend(0, a_qkv, gate, term, entering, w_out, at)
    got = to_core(give)
    a_gx, a_gy = now(gx, gy)
    gd = to_x(a_gy[:h2]), to_y(a_gx[h2:])
    end(*third1, got, keep, *gd)

    def first_step(keep, got):
        low, high = add_last(keep, got, width)
        return to_x(low), to_y(high)

    def total(*parts):
        out = parts[0].astype(F32)
        for p in parts[1:]:
            out = out + p.astype(F32)
        return out

    keep, got = now(keep, got)
    u, v = first_step(keep, got)
    third2 = spread1(now(*third1))
    g_a = pin(jnp.concatenate([og, gx, gy, *now(*gd)]))
    end(u, v, *third2, g_a)

    to_2, to_4 = add_halves(keep, got, *now(u, v), width)
    sx, sy = to_x(to_2), to_y(to_4)
    pair2 = spread1(now(*pair1))
    g_b = to_core(now(g_a))
    end(sx, sy, *pair2, g_b)

    pair3 = spread2(now(*pair2))
    mid, branch, r_attn, n2 = mid_rows((keep, got, *now(sx, sy)), inputs, dest)
    mx, my, mc = to_x(n2), to_y(n2), to_core(n2)
    end(mx, my, mc, pair3)

    third3 = spread2(now(*third2))
    ax, ay = now(mx, my)
    md = to_x(ay[:h2]), to_y(ax[h2:])
    mxyc = to_core(jnp.concatenate([ax, ay]))
    mdc = to_core(jnp.concatenate(md))
    n2_a = pin(jnp.concatenate([n2, mx, my, *md]))
    n2_b = pin(jnp.concatenate([mc, mxyc, mdc]))
    w_pair = plan.slots(own_pair, now(*pair1), now(*pair2), now(pair3))
    end(third3, n2_a, n2_b, *w_pair)

    w_third = plan.slots(own_third, now(*third1), now(*third2), now(third3))
    prod_b, turned_b, gf_b, gs_b, give = sglu_rows(n2_b, g_b, w_pair, w_third)
    end(give)

    give, a_n2 = now(give, n2_a)
    got = to_core(give)
    prod_a, turned_a, gf_a, gs_a, keep = sglu_rows(a_n2, g_a, w_pair, w_third)
    end(keep, got)

    keep, got = now(keep, got)
    u, v = first_step(keep, got)
    lefts = [(now(gf_a), gf_b), (gs_a, gs_b)]
    d_late = grads_by_right(lefts, (n2_a, n2_b), cut, 2, 2)
    end(u, v, *d_late)

    d_late = now(*d_late)
    pair1 = inward_z(d_late[1])
    lefts = [(now(gf_a), gf_b), (gs_a, gs_b)]
    d_pair = [*grads_by_right(lefts, (n2_a, n2_b), cut, 0, 2), *d_late]
    to_2, to_4 = add_halves(keep, got, *now(u, v), width)
    sx, sy = to_x(to_2), to_y(to_4)
    d_third = grads_by_right([(now(turned_a), turned_b)], (g_a, g_b), cut, 0, 4)

    def join(part, more):
        return pin(plus(part, now(more)))

    end(sx, sy, pair1, *d_third, *d_pair)

    d_third = [d[0] for d in now(*d_third)]
    d_pair = now(*d_pair)
    pair2 = gather2(d_pair[2], pin(plus(d_pair[3], now(pair1))))
    grad_mid, gb = mid_back_rows((keep, got, *now(sx, sy)), out_grad, mid, branch, r_attn, dest)
    bx, by, bc = to_x(gb), to_y(gb), to_core(gb)
    o_give = sglu_last(now(prod_b), w_third)
    o_keep = sglu_last(now(prod_a), w_third)

    end(bx, by, bc, *pair2, o_keep, o_give)

    third1 = gather1(now(*d_third))
    o_got = to_core(now(o_give))
    ax, ay = now(bx, by)
    bd = to_x(ay[:h2]), to_y(ax[h2:])
    bxyc = to_core(jnp.concatenate([ax, ay]))
    bdc = to_core(jnp.concatenate(bd))
    gb_a = pin(jnp.concatenate([gb, bx, by, *bd]))
    gb_b = pin(jnp.concatenate([bc, bxyc, bdc]))
    end(third1, gb_a, gb_b, o_got)

    third2 = gather2(now(d_third[2]), join(d_third[3], third1))
    ou, ov = first_step(*now(o_keep, o_got))
    ga, gg, mixed, d_term, d_leaving = attend_back_rows(
        (now(gb_a), gb_b), w_out, (attn_a, attn_b), gate, qkv, at
    )
    a_pair = now(*pair2)
    ready = [
        (pin(plus(d_pair[1][m], a_pair[1][m])), pin(plus(d_pair[2][m], a_pair[0][m])))
        for m in (0, 1)
    ]
    end(*third2, d_leaving, ou, ov, *ready[0], *ready[1])

    first3 = gather3(*now(*ready[0]))
    d_out = grads_out(now(mixed), (gb_a, gb_b), width)
    d_entering = at.bring(now(d_leaving), True)

    def back_half(h, first, state):
        return project_back(
            h, first, raw, ga, gg, state, d_term, d_entering, w_in, width, at
        )

    gp_b, give = back_half(1, after(qkv, d_out), state_b)
    end(*first3, give, d_out)

    second3 = gather3(*now(*ready[1]))
    parts = now(d_out).reshape(2, 2, few, width)
    w_keep = jnp.where(core0, parts[:, 0], parts[:, 1])
    w_got = to_core(jnp.where(core0, parts[:, 1], parts[:, 0]))
    a_qkv, give = now(qkv, give)
    gp_a, keep = back_half(0, a_qkv, state_a)
    got = to_core(give)
    ready = join(d_third[1], third2[1]), join(d_third[2], third2[0])
    end(*second3, keep, got, w_keep, w_got, *ready)

    third3 = gather3(*now(*ready))
    keep, got = now(keep, got)
    u, v = first_step(keep, got)
    mine = (order // 2 == plan.c).astype(jnp.int32)
    d_w = grads_by_left(norm1, (now(gp_a), gp_b), 4, (*now(w_keep, w_got), mine, order % 2))
    end(u, v, *third3, *d_w)

    d_w = now(*d_w)
    w1 = gather1(d_w)
    to_2, to_4 = add_halves(keep, got, *now(u, v), width)
    sx, sy = to_x(to_2), to_y(to_4)
    sum_three = [
        total(d_pair[0][0], *now(*first3)),
        total(d_pair[0][1], *now(*second3)),
        total(d_third[0], *now(*third3)),
    ]
    sum_three = jnp.stack([v.astype(BF) for v in sum_three])
    my_three, to_three = plan.of_y(sum_three[:, :, :rows], sum_three[:, :, rows:])
    end(sx, sy, w1, my_three, to_three)

    w2 = gather2(d_w[2], join(d_w[3], w1))
    three_got = to_y(now(to_three))
    grad_norm1 = total(keep[:rows], got[:rows], *now(sx, sy))
    input_grad = grad_mid + srms_back(xf, plan.turn(grad_norm1, dest))
    end(*w2, three_got)

    ready = join(d_w[1], w2[1]), join(d_w[2], w2[0])
    w3 = gather3(*ready)
    to_2, to_4 = add_halves(after(o_keep, *ready), o_got, *now(ou, ov), width)
    ox, oy = to_x(to_2), to_y(to_4)
    sum_three = plan.by_y(my_three, now(three_got), 1)
    sum_pair = pin(sum_three[:2].swapaxes(1, 2)).astype(F32)
    sum_third = sum_three[2].astype(F32)
    end(*w3, ox, oy)

    sum_w = pin(total(d_w[0], *now(*w3)))
    sum_in = pin(sum_w[:deep].astype(BF)).reshape(8, few, across)
    sum_in = lax.all_to_all(sum_in, plan.tp, 0, 0, tiled=True)
    sum_out = jnp.concatenate([sum_w[deep : deep + few], sum_w[deep + few :]], axis=1)
    output = mid + plan.turn(total(o_keep[:rows], o_got[:rows], *now(ox, oy)), dest)
    return output, input_grad, sum_in, sum_out, sum_pair, sum_third


class Plain:
    def __init__(self, wide, narrow):
        self.tp = ("narrow",)
        self.fs = ("wide",)
        self.size = narrow
        self.groups = wide

    def begin(self):
        self.p = lax.axis_index("narrow")
        self.group = lax.axis_index("wide")
        self.slot_ids = jnp.arange(self.size, dtype=jnp.int32)

    def turn(self, v):
        return v

    def rows_all(self, a):
        whole = lax.all_gather(a, "narrow", axis=0, tiled=True)
        return whole[: whole.shape[0] // 2], whole[whole.shape[0] // 2 :]

    def rows_sum(self, keep, give, kind=BF):
        total = lax.psum_scatter(
            jnp.concatenate([keep, give]), "narrow", scatter_dimension=0, tiled=True
        )
        return total.astype(F32)

    def attn_in(self, w):
        rows, cols = w.shape
        each = cols // 4 // self.size
        view = w.reshape(rows, 4, self.size, each).transpose(2, 0, 1, 3)
        view = view.reshape(self.size, rows, 4 * each)
        mine = lax.all_to_all(view, "narrow", 0, 0, tiled=True)
        mine = mine.reshape(self.size * rows, 4 * each)
        return cut4(lax.all_gather(mine, "wide", axis=0, tiled=True), 0)

    def attn_in_back(self, g):
        cols = g.shape[1]
        total = lax.psum_scatter(g.astype(BF), "wide", scatter_dimension=0, tiled=True)
        rows = total.shape[0] // self.size
        view = total.reshape(self.size, rows, cols)
        mine = lax.all_to_all(view, "narrow", 0, 0, tiled=True)
        mine = mine.reshape(self.size, rows, 4, cols // 4).transpose(1, 2, 0, 3)
        return mine.reshape(rows, cols * self.size).astype(F32)

    def attn_out(self, w):
        whole = lax.all_gather(w, ("wide", "narrow"), axis=0, tiled=True)
        each = whole.shape[0] // self.size
        return lax.dynamic_slice_in_dim(whole, self.p * each, each)

    def attn_out_back(self, g):
        each = g.shape[0]
        whole = jnp.zeros((each * self.size, g.shape[1]), BF)
        whole = lax.dynamic_update_slice_in_dim(whole, g.astype(BF), self.p * each, 0)
        total = lax.psum_scatter(whole, ("wide", "narrow"), scatter_dimension=0, tiled=True)
        return total.astype(F32)

    def sglu(self, pair, third):
        return pair, third

    def sglu_all(self, both, back):
        pair = lax.all_gather(both.swapaxes(1, 2), "wide", axis=2, tiled=True)
        third = lax.all_gather(back, "wide", axis=1, tiled=True)
        return cut4(pair, 2), cut4(third, 1)

    def pair_back(self, g):
        g = jnp.concatenate([g[k] for k in range(4)], axis=2)
        total = lax.psum_scatter(g, "wide", scatter_dimension=2, tiled=True)
        return total.swapaxes(1, 2).astype(F32)

    def third_back(self, g):
        g = jnp.concatenate([g[k] for k in range(4)], axis=1)
        total = lax.psum_scatter(g, "wide", scatter_dimension=1, tiled=True)
        return total.astype(F32)


def plain_layer(plan, places, lengths, inputs, out_grad, attn_in, attn_out, sglu_in, sglu_out):
    rows, width = inputs.shape
    at = places(lengths)
    w_out = plan.attn_out(attn_out.astype(BF))
    w_in = plan.attn_in(attn_in.astype(BF))
    w_pair, w_third = plan.sglu_all(sglu_in.astype(BF), sglu_out.astype(BF))
    xf = inputs.astype(F32)
    norm1 = plan.rows_all(plan.turn((xf * inverse_rms(xf)).astype(BF)))
    grad_rows = plan.rows_all(plan.turn(out_grad))
    raw, gate, qkv, term, leaving = project(norm1, w_in, at)
    entering = at.bring(leaving, False)
    attn, branch, state = [None] * 2, [None] * 2, [None] * 2
    for h in (1, 0):
        attn[h], branch[h], state[h] = attend(h, qkv, gate, term, entering, w_out, at)
    square = plan.rows_sum(*[strip_sum(v) for v in branch], F32)
    branch = plan.rows_sum(*[v[:, :width] for v in branch])
    r_attn = lax.rsqrt(square / width + EPS)
    mid = xf + r_attn * branch
    r_mid = inverse_rms(mid)
    norm2 = plan.rows_all(plan.turn((mid * r_mid).astype(BF)))

    product, turned, grad_first, grad_second, back = [[None] * 2 for _ in range(5)]
    for h in (1, 0):
        product[h], turned[h], grad_first[h], grad_second[h], back[h] = sglu_rows(
            norm2[h], grad_rows[h], w_pair, w_third
        )
    cut = width // 4
    sum_third = plan.third_back([g[0] for g in grads_by_right([turned], grad_rows, cut, 0, 4)])
    grad_norm2 = plan.rows_sum(*back)
    sum_pair = plan.pair_back(grads_by_right([grad_first, grad_second], norm2, cut, 0, 4))

    grad_mid = out_grad.astype(F32) + srms_back(mid, plan.turn(grad_norm2))
    grad_branch = grad_mid.astype(BF)
    inward = jnp.mean(grad_branch.astype(F32) * branch, axis=1, keepdims=True)
    extra = pieces(r_attn) + pieces(r_attn * r_attn * r_attn * inward)
    extra.append(jnp.zeros((rows, 128 - len(extra)), BF))
    grad_branch = jnp.concatenate([grad_branch] + extra, axis=1)
    grad_branch = plan.rows_all(grad_branch)
    branch_out = plan.rows_sum(*[sglu_last(v, w_third) for v in product])
    output = mid + plan.turn(branch_out)
    grad_attn, grad_gate, mixed, d_term, d_leaving = attend_back_rows(
        grad_branch, w_out, attn, gate, qkv, at
    )
    d_entering = at.bring(d_leaving, True)
    grad_pre, back = [None] * 2, [None] * 2
    for h in (1, 0):
        grad_pre[h], back[h] = project_back(
            h, qkv, raw, grad_attn, grad_gate, state[h], d_term, d_entering, w_in, width, at
        )
    grad_win = jnp.concatenate(grads_by_left(norm1, grad_pre, 4))
    sum_in = plan.attn_in_back(grad_win)
    sum_out = plan.attn_out_back(grads_out(mixed, grad_branch, width))
    grad_norm1 = plan.rows_sum(*back)
    input_grad = grad_mid + srms_back(xf, plan.turn(grad_norm1))
    return output, input_grad, sum_in, sum_out, sum_pair, sum_third


def per_device(plan, layer, *args):
    inputs, out_grad, seq_lengths, decay_rate = args[:4]
    weights, moments, averages = args[4:8], args[8:12], args[12:16]
    plan.begin()
    rows, width = inputs.shape
    plan.own = decay_rate.shape[0] // plan.size

    def places(lengths):
        return Places(plan, lengths, decay_rate, rows)

    output, input_grad, *grads = layer(plan, places, seq_lengths, inputs, out_grad, *weights)
    tokens = plan.size * rows * plan.groups
    fans = (width, width, width, weights[3].shape[0] * lax.axis_size(plan.narrow))
    new = []
    for w, m, a, grad, fan in zip(weights, moments, averages, grads, fans):
        if grad.shape == w.shape:
            new.append(renew(w, m, a, grad, fan, tokens))
        else:
            new.append(renew_turned(grad, w, m, a, fan, tokens))
    return (output, input_grad) + tuple(n[i] for i in range(3) for n in new)


def solution(mesh):
    wide, narrow = mesh.shape["wide"], mesh.shape["narrow"]
    if (wide, narrow) == (8, 4):
        mesh = Mesh(mesh.devices.reshape(4, 2, 2, 2), ("z", "y", "x", "c"))
        plan, layer, w, n = Square(), square_layer, ("z", "y"), ("x", "c")
    else:
        plan, layer, w, n = Plain(wide, narrow), plain_layer, ("wide",), ("narrow",)
    plan.narrow = n
    by_rows = P(w + n, None)
    pair, third = P(None, w, n), P(n, w)
    weights = (by_rows, by_rows, pair, third)

    def run(*args):
        return per_device(plan, layer, *args)

    return jax.shard_map(
        run,
        mesh=mesh,
        in_specs=(by_rows, by_rows, P(), P()) + weights * 3,
        out_specs=(by_rows, by_rows) + weights * 3,
        check_vma=False,
    )
```

```python
import math

import jax
import jax.numpy as jnp
from jax import lax
from jax.experimental import pallas as pl
from jax.experimental.layout import Layout, with_layout_constraint
from jax.experimental.pallas import tpu as pltpu
from jax.sharding import Mesh
from jax.sharding import PartitionSpec as P

BLOCK = 256
EPS = 1e-06
MU = 0.9
BETA = 0.8
HIGH = lax.Precision.HIGHEST
BF = jnp.bfloat16
F32 = jnp.float32
SWAP = [(0, 1), (1, 0)]
XORS = (0, 2, 4, 6, 1, 3, 5, 7)
MEETS = ((0, 1, 2, 3), (1, 0, 2, 3), (2, 3, 1, 0), (3, 2, 1, 0))
PLACES = ((0, 1, 2, 3), (1, 0, 2, 3), (3, 2, 0, 1), (3, 2, 1, 0))


def dot(a, b, dims=((1,), (0,))):
    return lax.dot_general(a, b, (dims, ((), ())), preferred_element_type=F32)


def inverse_rms(v):
    return lax.rsqrt(jnp.mean(v * v, axis=-1, keepdims=True) + EPS)


def srms_back(v, grad):
    r = inverse_rms(v)
    return r * grad - v * (r * r * r) * jnp.mean(grad * v, axis=-1, keepdims=True)


def renew(weight, moment, average, grad, fan, tokens):
    step = 0.4 / math.sqrt(fan * tokens)
    moment_new = MU * moment + grad
    weight_new = weight - step * (grad + MU * moment_new)
    average_new = BETA * average + (1.0 - BETA) * weight_new
    return (moment_new, weight_new, average_new)


ROWS = 256
HALF = 4
SUB = 2
STEPS = HALF // SUB
TALL = SUB * ROWS
HD = 128
VMEM = 56 * 1024 * 1024
EXTRA = 128


def pin(v):
    return with_layout_constraint(v, Layout(major_to_minor=tuple(range(v.ndim))))


def after(value, *done):
    return lax.optimization_barrier((value,) + done)[0]


class Clock:
    def __init__(self):
        self.token = jnp.zeros((8, 128), F32)

    def now(self, *values):
        out = [lax.optimization_barrier((v, self.token))[0] for v in values]
        return out if len(out) > 1 else out[0]

    def end(self, *done):
        self.token = lax.optimization_barrier((self.token,) + done)[0]


def block_spec(shape):
    return pl.BlockSpec(shape, lambda i: (i,) + (0,) * (len(shape) - 1))


def whole_spec(a):
    return pl.BlockSpec(a.shape, lambda i: (0,) * a.ndim, pipeline_mode=pl.Buffered(1))


def scalar_spec():
    return pl.BlockSpec(memory_space=pltpu.SMEM)


def call(kernel, steps, ins, outs, flops):
    moved = sum(a.size * a.dtype.itemsize for a, _ in ins)
    moved += sum(math.prod(s) * jnp.dtype(d).itemsize for s, d, _ in outs)
    return pl.pallas_call(
        kernel,
        grid=(steps,),
        in_specs=[s for _, s in ins],
        out_specs=[b if isinstance(b, pl.BlockSpec) else block_spec(b) for _, _, b in outs],
        out_shape=[jax.ShapeDtypeStruct(s, d) for s, d, _ in outs],
        compiler_params=pltpu.CompilerParams(
            vmem_limit_bytes=VMEM, dimension_semantics=("arbitrary",)
        ),
        cost_estimate=pl.CostEstimate(
            flops=int(flops), bytes_accessed=int(moved), transcendentals=0
        ),
    )(*[a for a, _ in ins])


NT = ((1,), (1,))
TN = ((0,), (0,))


def mask_of(fade, seg_c, seg_r):
    return jnp.where(seg_c == seg_r, fade, 0.0)


def pair_spec(shape, late):
    if late:
        return pl.BlockSpec(shape, lambda i: (jnp.maximum(i - STEPS, 0),) + (0,) * (len(shape) - 1))
    return pl.BlockSpec(shape, lambda i: (jnp.minimum(i, STEPS - 1),) + (0,) * (len(shape) - 1))


def half_spec(shape, h):
    return pl.BlockSpec(shape, lambda i: (i + h * STEPS,) + (0,) * (len(shape) - 1))


def project(n1, w_in, at):
    own = at.own
    cols = own * HD
    parts = len(w_in)
    width = n1[0].shape[1]
    deep = width // parts

    def kernel(*refs):
        a_ref, b_ref, w_refs = refs[0], refs[1], refs[2 : 2 + parts]
        seg_ref, ramp_ref, last_ref, reach_ref = refs[2 + parts : 6 + parts]
        raw_ref, gate_ref, qkv_ref, term_ref, leaving_ref = refs[6 + parts :]
        i = pl.program_id(0)
        pre = None
        for k in range(parts):
            some = slice(k * deep, (k + 1) * deep)
            x = jnp.where(i < STEPS, a_ref[:, some], b_ref[:, some])
            new = dot(x, w_refs[k][...])
            pre = new if pre is None else pre + new
        pq, pk, pv = pre[:, :cols], pre[:, cols : 2 * cols], pre[:, 2 * cols : 3 * cols]
        raw_ref[...] = pre[:, : 2 * cols]
        gate_ref[...] = pre[:, 3 * cols :]
        key = (pk * jax.nn.sigmoid(pk)).astype(BF)
        value = pv.astype(BF)
        qkv_ref[:, :cols] = (pq * jax.nn.sigmoid(pq)).astype(BF)
        qkv_ref[:, cols : 2 * cols] = key
        qkv_ref[:, 2 * cols :] = value

        @pl.when(i == 0)
        def _():
            leaving_ref[...] = jnp.zeros_like(leaving_ref)

        for s in range(SUB):
            b = i * SUB + s
            block = slice(s * ROWS, (s + 1) * ROWS)
            for j in range(own):
                ramp = ramp_ref[:, own + j : own + j + 1]
                leave = jnp.where(seg_ref[s] == last_ref[b], ramp, 0.0)
                head = slice(j * HD, (j + 1) * HD)
                scaled = (key[block, head].astype(F32) * leave).astype(BF)
                term = dot(scaled, value[block, head], TN)
                term_ref[s, j] = term
                leaving_ref[j] += reach_ref[j, b] * term

    some = pl.BlockSpec((deep, 4 * cols), lambda i: (0, 0), pipeline_mode=pl.Buffered(1))
    ins = [(v, pair_spec((TALL, width), late)) for late, v in enumerate(n1)]
    ins += [(w, some) for w in w_in]
    ins += [(at.cols, block_spec((SUB, ROWS, 1))), (at.ramps, whole_spec(at.ramps))]
    ins += [(v, scalar_spec()) for v in (at.last, at.out_reach)]
    n = 2 * HALF
    outs = [
        ((n * ROWS, 2 * cols), F32, (TALL, 2 * cols)),
        ((n * ROWS, cols), F32, (TALL, cols)),
        ((n * ROWS, 3 * cols), BF, (TALL, 3 * cols)),
        ((n, own, HD, HD), F32, (SUB, own, HD, HD)),
        ((own, HD, HD), F32, pl.BlockSpec((own, HD, HD), lambda i: (0, 0, 0))),
    ]
    return call(kernel, 2 * STEPS, ins, outs, 4 * n1[0].size * 4 * cols)


def combine(weights, terms, more, reach):
    state = reach * more
    for c in range(2 * HALF):
        state = state + weights(c) * terms(c)
    return state


def attend(h, qkv, gate, term, entering, w_out, at):
    own = at.own
    cols = own * HD
    width = w_out.shape[1]

    def kernel(
        qkv_ref, gate_ref, term_ref, more_ref, w_ref, sc_ref, sr_ref, fade_ref, ramp_ref,
        prev_ref, inner_ref, reach_ref, attn_ref, branch_ref, state_ref,
    ):
        for s, j in ((s, j) for s in range(SUB) for j in range(own)):
            i = (pl.program_id(0) + h * STEPS) * SUB + s
            block = slice(s * ROWS, (s + 1) * ROWS)
            head = slice(j * HD, (j + 1) * HD)
            q = qkv_ref[block, j * HD : (j + 1) * HD]
            k = qkv_ref[block, cols + j * HD : cols + (j + 1) * HD]
            v = qkv_ref[block, 2 * cols + j * HD : 2 * cols + (j + 1) * HD]
            state = combine(
                lambda c: inner_ref[j, i * 2 * HALF + c],
                lambda c: term_ref[c, j],
                more_ref[j],
                reach_ref[j, i],
            ).astype(BF)
            state_ref[s, j] = state
            enter = jnp.where(sc_ref[s] == prev_ref[i], ramp_ref[:, j : j + 1], 0.0)
            weights = (dot(q, k, NT) * mask_of(fade_ref[j], sc_ref[s], sr_ref[s])).astype(BF)
            attn_ref[block, head] = dot(weights, v) + enter * dot(q, state)
        attn = attn_ref[...]
        branch_ref[:, :width] = dot((attn * gate_ref[...]).astype(BF), w_ref[...]).astype(BF)
        rest = jnp.sum(attn * attn, axis=1, keepdims=True)
        branch_ref[:, width:] = strip_of([rest])

    n = HALF
    ins = [
        (qkv, half_spec((TALL, 3 * cols), h)),
        (gate, half_spec((TALL, cols), h)),
        (term, whole_spec(term)),
        (entering, whole_spec(entering)),
        (w_out, whole_spec(w_out)),
        (at.cols, half_spec((SUB, ROWS, 1), h)),
        (at.rows, half_spec((SUB, 1, ROWS), h)),
        (at.fade, whole_spec(at.fade)),
        (at.ramps, whole_spec(at.ramps)),
    ] + [(v, scalar_spec()) for v in (at.prev, at.inner, at.in_reach)]
    outs = [
        ((n * ROWS, cols), F32, (TALL, cols)),
        ((n * ROWS, width + EXTRA), BF, (TALL, width + EXTRA)),
        ((n, own, HD, HD), BF, (SUB, own, HD, HD)),
    ]
    return call(kernel, STEPS, ins, outs, 2 * n * ROWS * cols * (width + 2 * ROWS))


def sglu_rows(n2, g, w_pair, w_third):
    parts = len(w_pair)
    _, hidden, deep = w_pair[0].shape
    block = 2 * ROWS

    def kernel(*refs):
        x_ref, g_ref = refs[:2]
        both, three = (refs[2 + k * parts : 2 + (k + 1) * parts] for k in range(2))
        prod_ref, prod_t, gf_t, gs_t, back_ref = refs[2 + 2 * parts :]
        first = second = grad = None
        for k in range(parts):
            at = slice(k * deep, (k + 1) * deep)
            x, gk = x_ref[:, at], g_ref[:, at]
            a, b, c = dot(x, both[k][0], NT), dot(x, both[k][1], NT), dot(gk, three[k][...], NT)
            first = a if first is None else first + a
            second = b if second is None else second + b
            grad = c if grad is None else grad + c
        prod = (first * second).astype(BF)
        gf = (grad * second).astype(BF)
        gs = (grad * first).astype(BF)
        prod_ref[...] = prod
        prod_t[...] = prod.T
        gf_t[...] = gf.T
        gs_t[...] = gs.T
        for k in range(parts):
            at = slice(k * deep, (k + 1) * deep)
            back_ref[:, at] = (dot(gf, both[k][0]) + dot(gs, both[k][1])).astype(BF)

    n = n2.shape[0] // block
    width = n2.shape[1]
    ins = [(n2, block_spec((block, width))), (g, block_spec((block, width)))]
    ins += [(w, whole_spec(w)) for w in w_pair + w_third]
    outs = [((n * block, hidden), BF, (block, hidden))]
    turned = pl.BlockSpec((hidden, block), lambda i: (0, i))
    outs += [((hidden, n * block), BF, turned)] * 3
    outs += [((n * block, width), BF, (block, width))]
    return call(kernel, n, ins, outs, 10 * n2.size * hidden)


def sglu_last(product, w_third):
    parts = len(w_third)
    deep = w_third[0].shape[1]
    block = 2 * ROWS

    def kernel(*refs):
        for k in range(parts):
            refs[-1][:, k * deep : (k + 1) * deep] = dot(refs[0][...], refs[1 + k][...]).astype(BF)

    n, width = product.shape[0] // block, parts * deep
    ins = [(product, block_spec((block, product.shape[1])))]
    ins += [(w, whole_spec(w)) for w in w_third]
    return call(
        kernel, n, ins, [((n * block, width), BF, (block, width))], 2 * product.size * width
    )[0]


def attend_back_rows(gb, w_out, attn, gate, qkv, at):
    own = at.own
    cols = own * HD
    width = w_out.shape[1]

    def kernel(
        gb_a, gb_b, w_ref, attn_a, attn_b, gate_ref, qkv_ref, sc_ref, ramp_ref, prev_ref, reach_ref,
        ga_ref, gg_ref, mixed_ref, term_ref, leaving_ref,
    ):
        i = pl.program_id(0)
        early = i < STEPS
        extra = jnp.where(early, gb_a[:, width:], gb_b[:, width:]).astype(F32)
        r = extra[:, 0:1] + extra[:, 1:2] + extra[:, 2:3]
        pull = extra[:, 3:4] + extra[:, 4:5] + extra[:, 5:6]
        gm = dot(jnp.where(early, gb_a[:, :width], gb_b[:, :width]), w_ref[...], NT)
        attn, gate = jnp.where(early, attn_a[...], attn_b[...]), gate_ref[...]
        normed = r * attn
        gg_ref[...] = (gm * normed).astype(BF)
        mixed_ref[...] = (normed * gate).astype(BF)
        ga = (r * (gm * gate) - attn * pull).astype(BF)
        ga_ref[...] = ga

        @pl.when(i == 0)
        def _():
            leaving_ref[...] = jnp.zeros_like(leaving_ref)

        for s, j in ((s, j) for s in range(SUB) for j in range(own)):
            b = i * SUB + s
            block = slice(s * ROWS, (s + 1) * ROWS)
            enter = jnp.where(sc_ref[s] == prev_ref[b], ramp_ref[:, j : j + 1], 0.0)
            q = qkv_ref[block, j * HD : (j + 1) * HD].astype(F32)
            term = dot((q * enter).astype(BF), ga[block, j * HD : (j + 1) * HD], TN)
            term_ref[s, j] = term
            leaving_ref[j] += reach_ref[j, b] * term

    n = 2 * HALF
    ins = [(v, pair_spec((TALL, v.shape[1]), late)) for late, v in enumerate(gb)]
    ins += [(w_out, whole_spec(w_out))]
    ins += [(v, pair_spec((TALL, cols), late)) for late, v in enumerate(attn)]
    ins += [
        (gate, block_spec((TALL, cols))),
        (qkv, block_spec((TALL, 3 * cols))),
        (at.cols, block_spec((SUB, ROWS, 1))),
        (at.ramps, whole_spec(at.ramps)),
    ] + [(v, scalar_spec()) for v in (at.prev, at.in_reach)]
    outs = [((n * ROWS, cols), BF, (TALL, cols))] * 3
    outs += [((n, own, HD, HD), F32, (SUB, own, HD, HD))]
    outs += [((own, HD, HD), F32, pl.BlockSpec((own, HD, HD), lambda i: (0, 0, 0)))]
    return call(kernel, 2 * STEPS, ins, outs, 2 * n * ROWS * cols * width)


def project_back(h, qkv, raw, ga, gg, state, term, entering, w_in, width, at):
    own = at.own
    cols = own * HD
    parts = len(w_in)
    deep = width // parts

    def kernel(*refs):
        qkv_ref, raw_ref, ga_ref, gg_ref, state_ref, term_ref, more_ref = refs[:7]
        w_refs = refs[7 : 7 + parts]
        sc_ref, sr_ref, fade_ref, ramp_ref = refs[7 + parts : 11 + parts]
        prev_ref, last_ref, inner_ref, reach_ref, gp_ref, back_ref = refs[11 + parts :]
        for s, j in ((s, j) for s in range(SUB) for j in range(own)):
            i = (pl.program_id(0) + h * STEPS) * SUB + s
            block = slice(s * ROWS, (s + 1) * ROWS)
            head = slice(j * HD, (j + 1) * HD)
            kt = slice(cols + j * HD, cols + (j + 1) * HD)
            vt = slice(2 * cols + j * HD, 2 * cols + (j + 1) * HD)
            q, k, v = qkv_ref[block, head], qkv_ref[block, kt], qkv_ref[block, vt]
            g = ga_ref[block, head]
            mask = mask_of(fade_ref[j], sc_ref[s], sr_ref[s])
            enter = jnp.where(sc_ref[s] == prev_ref[i], ramp_ref[:, j : j + 1], 0.0)
            leave = jnp.where(sc_ref[s] == last_ref[i], ramp_ref[:, own + j : own + j + 1], 0.0)
            later = combine(
                lambda c: inner_ref[j, c * 2 * HALF + i],
                lambda c: term_ref[c, j],
                more_ref[j],
                reach_ref[j, i],
            ).astype(BF)
            weights = (dot(q, k, NT) * mask).astype(BF)
            gs = (dot(g, v, NT) * mask).astype(BF)
            gq = dot(gs, k) + enter * dot(g, state_ref[s, j], NT)
            gk = dot(gs, q, TN) + leave * dot(v, later, NT)
            gv = dot(weights, g, TN) + leave * dot(k, later)
            rq, rk = raw_ref[block, head], raw_ref[block, kt]
            sq, sk = jax.nn.sigmoid(rq), jax.nn.sigmoid(rk)
            gp_ref[block, head] = (gq * (sq * (1.0 + rq * (1.0 - sq)))).astype(BF)
            gp_ref[block, kt] = (gk * (sk * (1.0 + rk * (1.0 - sk)))).astype(BF)
            gp_ref[block, vt] = gv.astype(BF)
        gp_ref[:, 3 * cols :] = gg_ref[...]
        for k in range(parts):
            some = slice(k * deep, (k + 1) * deep)
            back_ref[:, some] = dot(gp_ref[...], w_refs[k][...], NT).astype(BF)

    n = HALF
    some = pl.BlockSpec((deep, 4 * cols), lambda i: (0, 0), pipeline_mode=pl.Buffered(1))
    ins = [
        (qkv, half_spec((TALL, 3 * cols), h)),
        (raw, half_spec((TALL, 2 * cols), h)),
        (ga, half_spec((TALL, cols), h)),
        (gg, half_spec((TALL, cols), h)),
        (state, block_spec((SUB, own, HD, HD))),
        (term, whole_spec(term)),
        (entering, whole_spec(entering)),
    ] + [(w, some) for w in w_in]
    ins += [
        (at.cols, half_spec((SUB, ROWS, 1), h)),
        (at.rows, half_spec((SUB, 1, ROWS), h)),
        (at.fade, whole_spec(at.fade)),
        (at.ramps, whole_spec(at.ramps)),
    ]
    ins += [(v, scalar_spec()) for v in (at.prev, at.last, at.inner, at.out_reach)]
    outs = [
        ((n * ROWS, 4 * cols), BF, (TALL, 4 * cols)),
        ((n * ROWS, width), BF, (TALL, width)),
    ]
    return call(kernel, STEPS, ins, outs, 2 * n * ROWS * 4 * cols * width)


def one_by_one(count, shape):
    spec = pl.BlockSpec(shape, lambda i: (0,) * len(shape), pipeline_mode=pl.Buffered(1))
    return [(shape, BF, spec) for _ in range(count)]


def grads_by_left(left, right, n, below=None):
    cut, cols = left[0].shape[1] // n, right[0].shape[1]
    more = 0 if below is None else 2 * below[0].shape[1]

    def kernel(*refs):
        l0, l1, r0, r1 = refs[:4]
        outs = refs[len(refs) - n :]
        grad = (dot(l0[...], r0[...], TN) + dot(l1[...], r1[...], TN)).astype(BF)
        for k in range(n):

            @pl.when(pl.program_id(0) == k)
            def _():
                outs[k][:cut] = grad
                if more:
                    a_ref, b_ref, from_a, row = refs[4:8]
                    part = jnp.where(from_a[k] == 1, a_ref[row[k]], b_ref[row[k]])
                    outs[k][cut : cut + more // 2] = part[:, :cols]
                    outs[k][cut + more // 2 :] = part[:, cols:]

    ins = [(a, pl.BlockSpec((a.shape[0], cut), lambda i: (0, i))) for a in left]
    ins += [(a, whole_spec(a)) for a in right]
    if more:
        ins += [(a, whole_spec(a)) for a in below[:2]] + [(a, scalar_spec()) for a in below[2:]]
    outs = one_by_one(n, (cut + more, cols))
    return call(kernel, n, ins, outs, 4 * left[0].size * cols)


def grads_by_right(lefts, right, cut, first, n, step=1):
    count = len(lefts)
    tall = lefts[0][0].shape[0]

    def kernel(*refs):
        r0, r1 = refs[2 * count : 2 * count + 2]
        outs = refs[2 * count + 2 :]
        for m in range(count):
            l0, l1 = refs[2 * m : 2 * m + 2]
            grad = (dot(l0[...], r0[...]) + dot(l1[...], r1[...])).astype(BF)
            for k in range(n):

                @pl.when(pl.program_id(0) == k)
                def _():
                    outs[k][m] = grad

    ins = [(a, whole_spec(a)) for left in lefts for a in left]
    ins += [(a, pl.BlockSpec((a.shape[0], cut), lambda i: (0, first + step * i))) for a in right]
    outs = one_by_one(n, (count, tall, cut))
    return call(kernel, n, ins, outs, 4 * count * right[0].size * tall)


def grads_out(left, right, width):
    def kernel(l0, l1, r0, r1, out):
        out[...] = (dot(l0[...], r0[...], TN) + dot(l1[...], r1[...], TN)).astype(BF)

    cut, (rows, tall) = width // 4, left.shape
    spec = lambda rows: pl.BlockSpec((rows, cut), lambda i: (0, i))
    half = lambda k: pl.BlockSpec((rows // 2, tall), lambda i: (k, 0))
    ins = [(left, half(k)) for k in (0, 1)] + [(a, spec(a.shape[0])) for a in right]
    return call(kernel, 4, ins, [((tall, width), BF, spec(tall))], 2 * left.size * width)[0]


def add_strips(width, *parts):
    total = parts[0][:, :width].astype(F32)
    for p in parts[1:]:
        total = total + p[:, :width].astype(F32)
    out = [total.astype(BF)]
    if parts[0].shape[1] > width:
        rest = 0.0
        for p in parts:
            for n in range(3):
                rest = rest + p[:, width + n : width + n + 1].astype(F32)
        lane = lax.broadcasted_iota(jnp.int32, (total.shape[0], EXTRA), 1)
        strip = jnp.zeros((total.shape[0], EXTRA), F32)
        for n in range(3):
            top = rest.astype(BF).astype(F32)
            strip = jnp.where(lane == n, top, strip)
            rest = rest - top
        out.append(strip.astype(BF))
    return out


def add_last(a, b, width):
    n, wide = a.shape[0] // ROWS, a.shape[1]
    half = ROWS // 2

    def kernel(a_ref, b_ref, low_ref, high_ref):
        parts = add_strips(width, a_ref[...], b_ref[...])
        for v, at in zip(parts, (slice(0, width), slice(width, wide))):
            low_ref[:, at] = v[:half]
            high_ref[:, at] = v[half:]

    block = pl.BlockSpec((ROWS, wide), lambda i: (n - 1, 0))
    one = pl.BlockSpec((half, wide), lambda i: (0, 0))
    return call(kernel, 1, [(a, block), (b, block)], [((half, wide), BF, one)] * 2, ROWS * wide)


def add_halves(a, b, u, v, width):
    wide = a.shape[1]
    half = ROWS // 2

    def kernel(a2, a4, b2, b4, u_ref, v_ref, to_2, to_4):
        low, high = slice(0, half), slice(half, ROWS)
        for out, rows, terms in (
            (to_2, low, (a2[low], b2[low])),
            (to_2, high, (a2[high], b2[high], v_ref[...])),
            (to_4, low, (a4[low], b4[low], u_ref[...])),
            (to_4, high, (a4[high], b4[high])),
        ):
            parts = add_strips(width, *terms)
            for p, at in zip(parts, (slice(0, width), slice(width, wide))):
                out[rows, at] = p

    spec = lambda k: pl.BlockSpec((ROWS, wide), lambda i: (k, 0))
    ins = [(t, spec(k)) for t in (a, b) for k in (1, 2)] + [(u, whole_spec(u)), (v, whole_spec(v))]
    return call(kernel, 1, ins, [((ROWS, wide), BF, spec(0))] * 2, ROWS * wide)


def strip_of(column):
    lane = lax.broadcasted_iota(jnp.int32, (column[0].shape[0], EXTRA), 1)
    strip = jnp.zeros(lane.shape, F32)
    for m, rest in enumerate(column):
        for n in range(3):
            top = rest.astype(BF).astype(F32)
            strip = jnp.where(lane == 3 * m + n, top, strip)
            rest = rest - top
    return strip.astype(BF)


def mid_rows(sums, inputs, dest):
    width = inputs.shape[1]
    cut = width // 4
    block = ROWS // 2

    def kernel(a, b, c, d, x_ref, dest_ref, mid_ref, branch_ref, scale_ref, norm_ref):
        branch = square = None
        for ref in (a, b, c, d):
            part = ref[:, :width].astype(F32)
            extra = ref[:, width:].astype(F32)
            more = extra[:, 0:1] + extra[:, 1:2] + extra[:, 2:3]
            branch = part if branch is None else branch + part
            square = more if square is None else square + more
        r = lax.rsqrt(square / width + EPS)
        mid = x_ref[...].astype(F32) + r * branch
        branch_ref[...] = branch.astype(BF)
        scale_ref[...] = jnp.broadcast_to(r, (block, EXTRA))
        mid_ref[...] = mid
        norm = (mid * inverse_rms(mid)).astype(BF)
        for p in range(4):
            to = pl.ds(pl.multiple_of(dest_ref[p] * cut, cut), cut)
            norm_ref[:, to] = norm[:, p * cut : (p + 1) * cut]

    ins = [(v, block_spec((block, width + EXTRA))) for v in sums]
    ins += [(inputs, block_spec((block, width))), (dest, scalar_spec())]
    outs = [
        ((ROWS, width), F32, (block, width)),
        ((ROWS, width), BF, (block, width)),
        ((ROWS, EXTRA), F32, (block, EXTRA)),
        ((ROWS, width), BF, (block, width)),
    ]
    return call(kernel, 2, ins, outs, 20 * ROWS * width)


def mid_back_rows(sums, out_grad, mid, branch, scale, dest):
    width = mid.shape[1]
    cut = width // 4
    block = ROWS // 2

    def kernel(a, b, c, d, g_ref, mid_ref, branch_ref, scale_ref, dest_ref, grad_ref, out_ref):
        parts = []
        for p in range(4):
            at = pl.ds(pl.multiple_of(dest_ref[p] * cut, cut), cut)
            part = a[:, at].astype(F32)
            for ref in (b, c, d):
                part = part + ref[:, at].astype(F32)
            parts.append(part)
        grad = g_ref[...].astype(F32) + srms_back(mid_ref[...], jnp.concatenate(parts, axis=1))
        grad_ref[...] = grad
        low = grad.astype(BF)
        out_ref[:, :width] = low
        inward = low.astype(F32) * branch_ref[...].astype(F32)
        inward = jnp.mean(inward, axis=1, keepdims=True)
        r = scale_ref[:, 0:1]
        out_ref[:, width:] = strip_of([r, r * r * r * inward])

    ins = [(v, block_spec((block, width))) for v in (*sums, out_grad, mid, branch)]
    ins += [(scale, block_spec((block, EXTRA))), (dest, scalar_spec())]
    outs = [
        ((ROWS, width), F32, (block, width)),
        ((ROWS, width + EXTRA), BF, (block, width + EXTRA)),
    ]
    return call(kernel, 2, ins, outs, 20 * ROWS * width)


def renew_turned(grad, weight, moment, average, fan, tokens):
    few, total = weight.shape
    block = 16

    def kernel(g_ref, w_ref, m_ref, a_ref, m_new, w_new, a_new):
        for p in range(8):
            for t in range(4):
                for j in range(2):
                    col = t * (total // 4) + (8 * (p % 2) + 4 * j + p // 2) * HD
                    to = slice(col, col + HD)
                    at = slice((2 * t + j) * HD, (2 * t + j + 1) * HD)
                    new = renew(
                        w_ref[:, to], m_ref[:, to], a_ref[:, to], g_ref[p, :, at].astype(F32),
                        fan, tokens,
                    )
                    m_new[:, to], w_new[:, to], a_new[:, to] = new

    ins = [(grad, pl.BlockSpec((8, block, grad.shape[2]), lambda i: (0, i, 0)))]
    ins += [(v, block_spec((block, total))) for v in (weight, moment, average)]
    outs = [((few, total), F32, (block, total))] * 3
    return call(kernel, few // block, ins, outs, 10 * weight.size)


def cut4(v, axis):
    n = v.shape[axis] // 4
    return [lax.slice_in_dim(v, k * n, (k + 1) * n, axis=axis) for k in range(4)]


def strip_sum(v):
    strip = v[:, v.shape[1] - EXTRA :].astype(F32)
    return strip[:, 0:1] + strip[:, 1:2] + strip[:, 2:3]


def pieces(v):
    out = []
    for _ in range(3):
        top = lax.reduce_precision(v, 8, 7)
        out.append(top.astype(BF))
        v = v - top
    return out


class Places:
    def __init__(self, plan, seq_lengths, decay_rate, rows):
        size = plan.size
        group_rows = size * rows
        tokens = group_rows * plan.groups
        ends = jnp.cumsum(seq_lengths)

        def seg_at(place):
            mark = jnp.sum((place[..., None] >= ends).astype(jnp.int32), axis=-1)
            return jnp.where(place < 0, -1, mark)

        first_block = plan.group * size
        blocks = first_block + plan.slot_ids
        seg = seg_at(blocks[:, None] * rows + jnp.arange(rows, dtype=jnp.int32)[None, :])
        prev = seg_at(blocks * rows - 1)
        last = seg[:, rows - 1]
        head_ids = plan.head_ids if hasattr(plan, "head_ids") else plan.own * plan.p + jnp.arange(plan.own)
        rate = jnp.take(decay_rate, head_ids)

        def reach(gap, same):
            return jnp.where(
                same & (gap >= 0), jnp.exp(-rate[:, None, None] * (rows * jnp.maximum(gap, 0))), 0.0
            )

        inner = reach(
            (blocks[:, None] - blocks[None, :] - 1).astype(F32)[None],
            (prev[:, None] == last[None, :])[None],
        )
        border = seg_at((first_block + size) * rows - 1)
        out_reach = reach(
            (first_block + size - 1 - blocks).astype(F32)[None, None], (last == border)[None, None]
        )[:, 0]
        entry = seg_at(first_block * rows - 1)
        in_reach = reach((blocks - first_block).astype(F32)[None, None], (prev == entry)[None, None])[
            :, 0
        ]
        longest = tokens // 4
        hops = min(-(-longest // group_rows), plan.groups - 1)

        def hop_factor(j, ahead):
            if ahead:
                here, there = border, seg_at((first_block + j * size) * rows - 1)
            else:
                here, there = entry, seg_at((first_block - (j - 1) * size) * rows - 1)
            return jnp.where(here == there, jnp.exp(-rate * ((j - 1) * group_rows)), 0.0)

        def bring(total, ahead):
            n = plan.groups
            got = jnp.zeros_like(total)
            for j in range(1, hops + 1):
                pairs = [(i + j, i) if ahead else (i, i + j) for i in range(n - j)]
                part = lax.ppermute(total, plan.fs, pairs)
                got = got + hop_factor(j, ahead)[:, None, None] * part
            return got

        self.bring, self.hop = bring, hop_factor
        self.inner = inner.reshape(inner.shape[0], -1)
        self.out_reach, self.in_reach = out_reach, in_reach
        self.own = plan.own
        self.cols, self.rows = seg[:, :, None], seg[:, None, :]
        self.prev, self.last = prev, last
        step = jnp.arange(rows).astype(F32)
        spread = step[:, None] - step[None, :]
        fade = jnp.exp(-rate[:, None, None] * jnp.maximum(spread, 0.0)[None])
        self.fade = jnp.where((spread >= 0)[None], fade, 0.0)
        ramps = [jnp.exp(-rate[None] * step[:, None]), jnp.exp(-rate[None] * (rows - step)[:, None])]
        blank = jnp.zeros((rows, EXTRA - 2 * plan.own), F32)
        self.ramps = jnp.concatenate(ramps + [blank], axis=1)


class Square:
    def __init__(self):
        self.tp = ("y", "x", "c")
        self.fs = ("z",)
        self.size = 8
        self.groups = 4

    def begin(self):
        self.z = lax.axis_index("z")
        self.y = lax.axis_index("y")
        self.c = lax.axis_index("c")
        self.p = lax.axis_index(self.tp)
        self.q = self.p // 2
        self.group = self.z
        self.slot_ids = self.p ^ jnp.array(XORS, jnp.int32)
        self.head_ids = 8 * self.c + 4 * jnp.arange(2) + self.q
        self.order = jnp.array(MEETS, jnp.int32)[self.z]
        self.dest = jnp.array(PLACES, jnp.int32)[self.z]

    def turn(self, v, places):
        wide = v.shape[1] // 4
        return jnp.concatenate(
            [lax.dynamic_slice_in_dim(v, places[k] * wide, wide, axis=1) for k in range(4)], axis=1
        )

    def slots(self, own, one, two, three):
        outer = (self.z == 0) | (self.z == 3)
        return [
            own,
            one[0],
            pin(jnp.where(outer, two[0], one[1])),
            pin(jnp.where(outer, three, two[1])),
        ]

    def by_y(self, mine, got, axis):
        first = self.y == 0
        parts = [jnp.where(first, mine, got), jnp.where(first, got, mine)]
        return pin(jnp.concatenate(parts, axis=axis))

    def of_y(self, one, two):
        first = self.y == 0
        return pin(jnp.where(first, one, two)), pin(jnp.where(first, two, one))


def over(axis, pairs=SWAP):
    return lambda v: pin(lax.ppermute(pin(v), axis, pairs))


to_x, to_y, to_core = over("x"), over("y"), over("c")


to_pair = over("z", [(0, 1), (1, 0), (2, 3), (3, 2)])
to_middle = over("z", [(1, 2), (2, 1)])
outward = over("z", [(1, 0), (2, 3)])
inward_z = over("z", [(0, 1), (3, 2)])


def spread0(own):
    return to_pair(own), to_middle(own)


def spread1(one):
    return outward(one[1]), to_middle(one[0])


def spread2(two):
    return outward(two[1])


def gather1(g):
    return inward_z(g[3])


def gather2(g2, third):
    return inward_z(g2), to_middle(third)


def gather3(first, second):
    return to_pair(first), to_middle(second)


def plus(a, b):
    return (a.astype(F32) + b.astype(F32)).astype(BF)


def square_layer(plan, places, lengths, inputs, out_grad, attn_in, attn_out, sglu_in, sglu_out):
    rows, width = inputs.shape
    h2 = rows // 2
    cut = width // 4
    clock = Clock()
    now, end = clock.now, clock.end

    order, dest = plan.order, plan.dest

    def pick(stack, place):
        return lax.dynamic_index_in_dim(stack, place, 0, False)

    xf = inputs.astype(F32)
    n1 = pin(plan.turn((xf * inverse_rms(xf)).astype(BF), order))
    og = pin(plan.turn(out_grad, order))
    few = attn_in.shape[0]
    view = attn_in.astype(BF).reshape(few, 4, 2, 2, 4, HD).transpose(4, 2, 0, 1, 3, 5)
    own_in = lax.all_to_all(view.reshape(8, few, -1), plan.tp, 0, 0, tiled=True)
    own_in = own_in.reshape(8 * few, -1)
    deep, across = own_in.shape
    own_out = attn_out.astype(BF)
    own_w = pin(jnp.concatenate([own_in, own_out[:, :across], own_out[:, across:]]))
    end(own_w, n1, og)

    a_w, a_n1 = now(own_w, n1)
    w1 = spread0(a_w)
    nx, ny = to_x(a_n1), to_y(a_n1)
    at = places(now(lengths))
    hid = sglu_in.shape[2] // 2
    three = pin(now(sglu_in).astype(BF)).swapaxes(1, 2)
    three = jnp.concatenate([three, sglu_out.astype(BF)[None]])
    my_three, to_three = plan.of_y(three[:, :hid], three[:, hid:])
    tables = [at.cols, at.rows, at.prev, at.last, at.fade, at.ramps]
    tables += [at.inner, at.out_reach, at.in_reach, at.hop(1, False), at.hop(1, True)]
    end(*w1, nx, ny, my_three, to_three, *tables)

    w2 = spread1(now(*w1))
    ax, ay = now(nx, ny)
    nd = to_x(ay[:h2]), to_y(ax[h2:])
    end(*w2, *nd)

    w3 = spread2(now(*w2))
    a_og, a_three = now(og, to_three)
    gx = to_x(a_og)
    got = to_y(a_three)
    n1_a = pin(jnp.concatenate([n1, nx, ny, *now(*nd)]))
    norm1 = n1_a, to_core(n1_a)
    own_three = plan.by_y(my_three, got, 2)
    own_pair, own_third = pin(own_three[:2]), pin(own_three[2])
    end(w3, gx, *norm1, own_pair, own_third)

    pair1 = spread0(now(own_pair))
    gy = to_y(now(og))
    w_in = plan.slots(own_w, now(*w1), now(*w2), now(w3))
    outs = jnp.stack([w[deep:] for w in w_in])
    w_mine = [pick(outs, dest[2 * plan.c + j]) for j in (0, 1)]
    w_got = to_core(jnp.concatenate([pick(outs, dest[2 * (1 - plan.c) + j]) for j in (0, 1)]))
    core0 = plan.c == 0
    raw, gate, qkv, term, leaving = project((now(norm1[0]), norm1[1]), w_in, at)
    end(*pair1, gy, w_got, leaving)

    w_rows = []
    for j in (0, 1):
        got = w_got[j * 2 * few : (j + 1) * 2 * few]
        for half in (jnp.where(core0, w_mine[j], got), jnp.where(core0, got, w_mine[j])):
            w_rows.append(jnp.concatenate([half[:few], half[few:]], axis=1))
    w_out = pin(jnp.concatenate(w_rows))
    entering = at.bring(now(leaving), False)
    attn_b, give, state_b = attend(1, qkv, gate, term, entering, w_out, at)
    end(give)

    third1 = spread0(now(own_third))
    a_qkv, give = now(qkv, give)
    attn_a, keep, state_a = attend(0, a_qkv, gate, term, entering, w_out, at)
    got = to_core(give)
    a_gx, a_gy = now(gx, gy)
    gd = to_x(a_gy[:h2]), to_y(a_gx[h2:])
    end(*third1, got, keep, *gd)

    def first_step(keep, got):
        low, high = add_last(keep, got, width)
        return to_x(low), to_y(high)

    def total(*parts):
        out = parts[0].astype(F32)
        for p in parts[1:]:
            out = out + p.astype(F32)
        return out

    keep, got = now(keep, got)
    u, v = first_step(keep, got)
    third2 = spread1(now(*third1))
    g_a = pin(jnp.concatenate([og, gx, gy, *now(*gd)]))
    end(u, v, *third2, g_a)

    to_2, to_4 = add_halves(keep, got, *now(u, v), width)
    sx, sy = to_x(to_2), to_y(to_4)
    pair2 = spread1(now(*pair1))
    g_b = to_core(now(g_a))
    end(sx, sy, *pair2, g_b)

    pair3 = spread2(now(*pair2))
    mid, branch, r_attn, n2 = mid_rows((keep, got, *now(sx, sy)), inputs, dest)
    mx, my, mc = to_x(n2), to_y(n2), to_core(n2)
    end(mx, my, mc, pair3)

    third3 = spread2(now(*third2))
    ax, ay = now(mx, my)
    md = to_x(ay[:h2]), to_y(ax[h2:])
    mxyc = to_core(jnp.concatenate([ax, ay]))
    mdc = to_core(jnp.concatenate(md))
    n2_a = pin(jnp.concatenate([n2, mx, my, *md]))
    n2_b = pin(jnp.concatenate([mc, mxyc, mdc]))
    w_pair = plan.slots(own_pair, now(*pair1), now(*pair2), now(pair3))
    end(third3, n2_a, n2_b, *w_pair)

    w_third = plan.slots(own_third, now(*third1), now(*third2), now(third3))
    prod_b, turned_b, gf_b, gs_b, give = sglu_rows(n2_b, g_b, w_pair, w_third)
    end(give)

    give, a_n2 = now(give, n2_a)
    got = to_core(give)
    prod_a, turned_a, gf_a, gs_a, keep = sglu_rows(a_n2, g_a, w_pair, w_third)
    end(keep, got)

    keep, got = now(keep, got)
    u, v = first_step(keep, got)
    lefts = [(now(gf_a), gf_b), (gs_a, gs_b)]
    d_late = grads_by_right(lefts, (n2_a, n2_b), cut, 2, 2)
    end(u, v, *d_late)

    d_late = now(*d_late)
    pair1 = inward_z(d_late[1])
    lefts = [(now(gf_a), gf_b), (gs_a, gs_b)]
    d_pair = [*grads_by_right(lefts, (n2_a, n2_b), cut, 0, 2), *d_late]
    to_2, to_4 = add_halves(keep, got, *now(u, v), width)
    sx, sy = to_x(to_2), to_y(to_4)
    d_third = grads_by_right([(now(turned_a), turned_b)], (g_a, g_b), cut, 0, 4)

    def join(part, more):
        return pin(plus(part, now(more)))

    end(sx, sy, pair1, *d_third, *d_pair)

    d_third = [d[0] for d in now(*d_third)]
    d_pair = now(*d_pair)
    pair2 = gather2(d_pair[2], pin(plus(d_pair[3], now(pair1))))
    grad_mid, gb = mid_back_rows((keep, got, *now(sx, sy)), out_grad, mid, branch, r_attn, dest)
    bx, by, bc = to_x(gb), to_y(gb), to_core(gb)
    o_give = sglu_last(now(prod_b), w_third)
    o_keep = sglu_last(now(prod_a), w_third)

    end(bx, by, bc, *pair2, o_keep, o_give)

    third1 = gather1(now(*d_third))
    o_got = to_core(now(o_give))
    ax, ay = now(bx, by)
    bd = to_x(ay[:h2]), to_y(ax[h2:])
    bxyc = to_core(jnp.concatenate([ax, ay]))
    bdc = to_core(jnp.concatenate(bd))
    gb_a = pin(jnp.concatenate([gb, bx, by, *bd]))
    gb_b = pin(jnp.concatenate([bc, bxyc, bdc]))
    a_pair = now(*pair2)
    ready = [
        (pin(plus(d_pair[1][m], a_pair[1][m])), pin(plus(d_pair[2][m], a_pair[0][m])))
        for m in (0, 1)
    ]
    end(third1, gb_a, gb_b, o_got, *ready[0], *ready[1])

    third2 = gather2(now(d_third[2]), join(d_third[3], third1))
    ou, ov = first_step(*now(o_keep, o_got))
    ga, gg, mixed, d_term, d_leaving = attend_back_rows(
        (now(gb_a), gb_b), w_out, (attn_a, attn_b), gate, qkv, at
    )
    end(*third2, d_leaving, ou, ov)

    first3 = gather3(*now(*ready[0]))
    d_out = grads_out(now(mixed), (gb_a, gb_b), width)
    d_entering = at.bring(now(d_leaving), True)

    def back_half(h, first, state):
        return project_back(
            h, first, raw, ga, gg, state, d_term, d_entering, w_in, width, at
        )

    gp_b, give = back_half(1, after(qkv, d_out), state_b)
    end(*first3, give, d_out)

    second3 = gather3(*now(*ready[1]))
    parts = now(d_out).reshape(2, 2, few, width)
    w_keep = jnp.where(core0, parts[:, 0], parts[:, 1])
    w_got = to_core(jnp.where(core0, parts[:, 1], parts[:, 0]))
    a_qkv, give = now(qkv, give)
    gp_a, keep = back_half(0, a_qkv, state_a)
    got = to_core(give)
    ready = join(d_third[1], third2[1]), join(d_third[2], third2[0])
    end(*second3, keep, got, w_keep, w_got, *ready)

    third3 = gather3(*now(*ready))
    keep, got = now(keep, got)
    u, v = first_step(keep, got)
    mine = (order // 2 == plan.c).astype(jnp.int32)
    d_w = grads_by_left(norm1, (now(gp_a), gp_b), 4, (*now(w_keep, w_got), mine, order % 2))
    end(u, v, *third3, *d_w)

    d_w = now(*d_w)
    w1 = gather1(d_w)
    to_2, to_4 = add_halves(keep, got, *now(u, v), width)
    sx, sy = to_x(to_2), to_y(to_4)
    sum_three = [
        total(d_pair[0][0], *now(*first3)),
        total(d_pair[0][1], *now(*second3)),
        total(d_third[0], *now(*third3)),
    ]
    sum_three = jnp.stack([v.astype(BF) for v in sum_three])
    my_three, to_three = plan.of_y(sum_three[:, :, :rows], sum_three[:, :, rows:])
    end(sx, sy, w1, my_three, to_three)

    w2 = gather2(d_w[2], join(d_w[3], w1))
    three_got = to_y(now(to_three))
    grad_norm1 = total(keep[:rows], got[:rows], *now(sx, sy))
    input_grad = grad_mid + srms_back(xf, plan.turn(grad_norm1, dest))
    summed = pin(plus(d_w[2], w2[0]))
    end(*w2, three_got, summed)

    ready = join(d_w[1], w2[1]), now(summed)
    w3 = gather3(*ready)
    to_2, to_4 = add_halves(after(o_keep, *ready), o_got, *now(ou, ov), width)
    ox, oy = to_x(to_2), to_y(to_4)
    sum_three = plan.by_y(my_three, now(three_got), 1)
    sum_pair = pin(sum_three[:2].swapaxes(1, 2)).astype(F32)
    sum_third = sum_three[2].astype(F32)
    end(*w3, ox, oy)

    sum_w = pin(total(d_w[0], *now(*w3)))
    sum_in = pin(sum_w[:deep].astype(BF)).reshape(8, few, across)
    sum_in = lax.all_to_all(sum_in, plan.tp, 0, 0, tiled=True)
    sum_out = jnp.concatenate([sum_w[deep : deep + few], sum_w[deep + few :]], axis=1)
    output = mid + plan.turn(total(o_keep[:rows], o_got[:rows], *now(ox, oy)), dest)
    return output, input_grad, sum_in, sum_out, sum_pair, sum_third


class Plain:
    def __init__(self, wide, narrow):
        self.tp = ("narrow",)
        self.fs = ("wide",)
        self.size = narrow
        self.groups = wide

    def begin(self):
        self.p = lax.axis_index("narrow")
        self.group = lax.axis_index("wide")
        self.slot_ids = jnp.arange(self.size, dtype=jnp.int32)

    def turn(self, v):
        return v

    def rows_all(self, a):
        whole = lax.all_gather(a, "narrow", axis=0, tiled=True)
        return whole[: whole.shape[0] // 2], whole[whole.shape[0] // 2 :]

    def rows_sum(self, keep, give, kind=BF):
        total = lax.psum_scatter(
            jnp.concatenate([keep, give]), "narrow", scatter_dimension=0, tiled=True
        )
        return total.astype(F32)

    def attn_in(self, w):
        rows, cols = w.shape
        each = cols // 4 // self.size
        view = w.reshape(rows, 4, self.size, each).transpose(2, 0, 1, 3)
        view = view.reshape(self.size, rows, 4 * each)
        mine = lax.all_to_all(view, "narrow", 0, 0, tiled=True)
        mine = mine.reshape(self.size * rows, 4 * each)
        return cut4(lax.all_gather(mine, "wide", axis=0, tiled=True), 0)

    def attn_in_back(self, g):
        cols = g.shape[1]
        total = lax.psum_scatter(g.astype(BF), "wide", scatter_dimension=0, tiled=True)
        rows = total.shape[0] // self.size
        view = total.reshape(self.size, rows, cols)
        mine = lax.all_to_all(view, "narrow", 0, 0, tiled=True)
        mine = mine.reshape(self.size, rows, 4, cols // 4).transpose(1, 2, 0, 3)
        return mine.reshape(rows, cols * self.size).astype(F32)

    def attn_out(self, w):
        whole = lax.all_gather(w, ("wide", "narrow"), axis=0, tiled=True)
        each = whole.shape[0] // self.size
        return lax.dynamic_slice_in_dim(whole, self.p * each, each)

    def attn_out_back(self, g):
        each = g.shape[0]
        whole = jnp.zeros((each * self.size, g.shape[1]), BF)
        whole = lax.dynamic_update_slice_in_dim(whole, g.astype(BF), self.p * each, 0)
        total = lax.psum_scatter(whole, ("wide", "narrow"), scatter_dimension=0, tiled=True)
        return total.astype(F32)

    def sglu(self, pair, third):
        return pair, third

    def sglu_all(self, both, back):
        pair = lax.all_gather(both.swapaxes(1, 2), "wide", axis=2, tiled=True)
        third = lax.all_gather(back, "wide", axis=1, tiled=True)
        return cut4(pair, 2), cut4(third, 1)

    def pair_back(self, g):
        g = jnp.concatenate([g[k] for k in range(4)], axis=2)
        total = lax.psum_scatter(g, "wide", scatter_dimension=2, tiled=True)
        return total.swapaxes(1, 2).astype(F32)

    def third_back(self, g):
        g = jnp.concatenate([g[k] for k in range(4)], axis=1)
        total = lax.psum_scatter(g, "wide", scatter_dimension=1, tiled=True)
        return total.astype(F32)


def plain_layer(plan, places, lengths, inputs, out_grad, attn_in, attn_out, sglu_in, sglu_out):
    rows, width = inputs.shape
    at = places(lengths)
    w_out = plan.attn_out(attn_out.astype(BF))
    w_in = plan.attn_in(attn_in.astype(BF))
    w_pair, w_third = plan.sglu_all(sglu_in.astype(BF), sglu_out.astype(BF))
    xf = inputs.astype(F32)
    norm1 = plan.rows_all(plan.turn((xf * inverse_rms(xf)).astype(BF)))
    grad_rows = plan.rows_all(plan.turn(out_grad))
    raw, gate, qkv, term, leaving = project(norm1, w_in, at)
    entering = at.bring(leaving, False)
    attn, branch, state = [None] * 2, [None] * 2, [None] * 2
    for h in (1, 0):
        attn[h], branch[h], state[h] = attend(h, qkv, gate, term, entering, w_out, at)
    square = plan.rows_sum(*[strip_sum(v) for v in branch], F32)
    branch = plan.rows_sum(*[v[:, :width] for v in branch])
    r_attn = lax.rsqrt(square / width + EPS)
    mid = xf + r_attn * branch
    r_mid = inverse_rms(mid)
    norm2 = plan.rows_all(plan.turn((mid * r_mid).astype(BF)))

    product, turned, grad_first, grad_second, back = [[None] * 2 for _ in range(5)]
    for h in (1, 0):
        product[h], turned[h], grad_first[h], grad_second[h], back[h] = sglu_rows(
            norm2[h], grad_rows[h], w_pair, w_third
        )
    cut = width // 4
    sum_third = plan.third_back([g[0] for g in grads_by_right([turned], grad_rows, cut, 0, 4)])
    grad_norm2 = plan.rows_sum(*back)
    sum_pair = plan.pair_back(grads_by_right([grad_first, grad_second], norm2, cut, 0, 4))

    grad_mid = out_grad.astype(F32) + srms_back(mid, plan.turn(grad_norm2))
    grad_branch = grad_mid.astype(BF)
    inward = jnp.mean(grad_branch.astype(F32) * branch, axis=1, keepdims=True)
    extra = pieces(r_attn) + pieces(r_attn * r_attn * r_attn * inward)
    extra.append(jnp.zeros((rows, 128 - len(extra)), BF))
    grad_branch = jnp.concatenate([grad_branch] + extra, axis=1)
    grad_branch = plan.rows_all(grad_branch)
    branch_out = plan.rows_sum(*[sglu_last(v, w_third) for v in product])
    output = mid + plan.turn(branch_out)
    grad_attn, grad_gate, mixed, d_term, d_leaving = attend_back_rows(
        grad_branch, w_out, attn, gate, qkv, at
    )
    d_entering = at.bring(d_leaving, True)
    grad_pre, back = [None] * 2, [None] * 2
    for h in (1, 0):
        grad_pre[h], back[h] = project_back(
            h, qkv, raw, grad_attn, grad_gate, state[h], d_term, d_entering, w_in, width, at
        )
    grad_win = jnp.concatenate(grads_by_left(norm1, grad_pre, 4))
    sum_in = plan.attn_in_back(grad_win)
    sum_out = plan.attn_out_back(grads_out(mixed, grad_branch, width))
    grad_norm1 = plan.rows_sum(*back)
    input_grad = grad_mid + srms_back(xf, plan.turn(grad_norm1))
    return output, input_grad, sum_in, sum_out, sum_pair, sum_third


def per_device(plan, layer, *args):
    inputs, out_grad, seq_lengths, decay_rate = args[:4]
    weights, moments, averages = args[4:8], args[8:12], args[12:16]
    plan.begin()
    rows, width = inputs.shape
    plan.own = decay_rate.shape[0] // plan.size

    def places(lengths):
        return Places(plan, lengths, decay_rate, rows)

    output, input_grad, *grads = layer(plan, places, seq_lengths, inputs, out_grad, *weights)
    tokens = plan.size * rows * plan.groups
    fans = (width, width, width, weights[3].shape[0] * lax.axis_size(plan.narrow))
    new = []
    for w, m, a, grad, fan in zip(weights, moments, averages, grads, fans):
        if grad.shape == w.shape:
            new.append(renew(w, m, a, grad, fan, tokens))
        else:
            new.append(renew_turned(grad, w, m, a, fan, tokens))
    return (output, input_grad) + tuple(n[i] for i in range(3) for n in new)


def solution(mesh):
    wide, narrow = mesh.shape["wide"], mesh.shape["narrow"]
    if (wide, narrow) == (8, 4):
        mesh = Mesh(mesh.devices.reshape(4, 2, 2, 2), ("z", "y", "x", "c"))
        plan, layer, w, n = Square(), square_layer, ("z", "y"), ("x", "c")
    else:
        plan, layer, w, n = Plain(wide, narrow), plain_layer, ("wide",), ("narrow",)
    plan.narrow = n
    by_rows = P(w + n, None)
    pair, third = P(None, w, n), P(n, w)
    weights = (by_rows, by_rows, pair, third)

    def run(*args):
        return per_device(plan, layer, *args)

    return jax.shard_map(
        run,
        mesh=mesh,
        in_specs=(by_rows, by_rows, P(), P()) + weights * 3,
        out_specs=(by_rows, by_rows) + weights * 3,
        check_vma=False,
    )
```

```python
import math

import jax
import jax.numpy as jnp
from jax import lax
from jax.experimental import pallas as pl
from jax.experimental.layout import Layout, with_layout_constraint
from jax.experimental.pallas import tpu as pltpu
from jax.sharding import Mesh
from jax.sharding import PartitionSpec as P

BLOCK = 256
EPS = 1e-06
MU = 0.9
BETA = 0.8
HIGH = lax.Precision.HIGHEST
BF = jnp.bfloat16
F32 = jnp.float32
SWAP = [(0, 1), (1, 0)]
XORS = (0, 2, 4, 6, 1, 3, 5, 7)
MEETS = ((0, 1, 2, 3), (1, 0, 2, 3), (2, 3, 1, 0), (3, 2, 1, 0))
PLACES = ((0, 1, 2, 3), (1, 0, 2, 3), (3, 2, 0, 1), (3, 2, 1, 0))


def dot(a, b, dims=((1,), (0,))):
    return lax.dot_general(a, b, (dims, ((), ())), preferred_element_type=F32)


def inverse_rms(v):
    return lax.rsqrt(jnp.mean(v * v, axis=-1, keepdims=True) + EPS)


def srms_back(v, grad):
    r = inverse_rms(v)
    return r * grad - v * (r * r * r) * jnp.mean(grad * v, axis=-1, keepdims=True)


def renew(weight, moment, average, grad, fan, tokens):
    step = 0.4 / math.sqrt(fan * tokens)
    moment_new = MU * moment + grad
    weight_new = weight - step * (grad + MU * moment_new)
    average_new = BETA * average + (1.0 - BETA) * weight_new
    return (moment_new, weight_new, average_new)


ROWS = 256
HALF = 4
SUB = 2
STEPS = HALF // SUB
TALL = SUB * ROWS
HD = 128
VMEM = 56 * 1024 * 1024
EXTRA = 128


def pin(v):
    return with_layout_constraint(v, Layout(major_to_minor=tuple(range(v.ndim))))


def after(value, *done):
    return lax.optimization_barrier((value,) + done)[0]


class Clock:
    def __init__(self):
        self.token = jnp.zeros((8, 128), F32)

    def now(self, *values):
        out = [lax.optimization_barrier((v, self.token))[0] for v in values]
        return out if len(out) > 1 else out[0]

    def end(self, *done):
        self.token = lax.optimization_barrier((self.token,) + done)[0]


def block_spec(shape):
    return pl.BlockSpec(shape, lambda i: (i,) + (0,) * (len(shape) - 1))


def whole_spec(a):
    return pl.BlockSpec(a.shape, lambda i: (0,) * a.ndim, pipeline_mode=pl.Buffered(1))


def scalar_spec():
    return pl.BlockSpec(memory_space=pltpu.SMEM)


def call(kernel, steps, ins, outs, flops):
    moved = sum(a.size * a.dtype.itemsize for a, _ in ins)
    moved += sum(math.prod(s) * jnp.dtype(d).itemsize for s, d, _ in outs)
    return pl.pallas_call(
        kernel,
        grid=(steps,),
        in_specs=[s for _, s in ins],
        out_specs=[b if isinstance(b, pl.BlockSpec) else block_spec(b) for _, _, b in outs],
        out_shape=[jax.ShapeDtypeStruct(s, d) for s, d, _ in outs],
        compiler_params=pltpu.CompilerParams(
            vmem_limit_bytes=VMEM, dimension_semantics=("arbitrary",)
        ),
        cost_estimate=pl.CostEstimate(
            flops=int(flops), bytes_accessed=int(moved), transcendentals=0
        ),
    )(*[a for a, _ in ins])


NT = ((1,), (1,))
TN = ((0,), (0,))


def mask_of(fade, seg_c, seg_r):
    return jnp.where(seg_c == seg_r, fade, 0.0)


def pair_spec(shape, late):
    if late:
        return pl.BlockSpec(shape, lambda i: (jnp.maximum(i - STEPS, 0),) + (0,) * (len(shape) - 1))
    return pl.BlockSpec(shape, lambda i: (jnp.minimum(i, STEPS - 1),) + (0,) * (len(shape) - 1))


def half_spec(shape, h):
    return pl.BlockSpec(shape, lambda i: (i + h * STEPS,) + (0,) * (len(shape) - 1))


def project(n1, w_in, at):
    own = at.own
    cols = own * HD
    parts = len(w_in)
    width = n1[0].shape[1]
    deep = width // parts

    def kernel(*refs):
        a_ref, b_ref, w_refs = refs[0], refs[1], refs[2 : 2 + parts]
        seg_ref, ramp_ref, last_ref, reach_ref = refs[2 + parts : 6 + parts]
        raw_ref, gate_ref, qkv_ref, term_ref, leaving_ref = refs[6 + parts :]
        i = pl.program_id(0)
        pre = None
        for k in range(parts):
            some = slice(k * deep, (k + 1) * deep)
            x = jnp.where(i < STEPS, a_ref[:, some], b_ref[:, some])
            new = dot(x, w_refs[k][...])
            pre = new if pre is None else pre + new
        pq, pk, pv = pre[:, :cols], pre[:, cols : 2 * cols], pre[:, 2 * cols : 3 * cols]
        raw_ref[...] = pre[:, : 2 * cols]
        gate_ref[...] = pre[:, 3 * cols :]
        key = (pk * jax.nn.sigmoid(pk)).astype(BF)
        value = pv.astype(BF)
        qkv_ref[:, :cols] = (pq * jax.nn.sigmoid(pq)).astype(BF)
        qkv_ref[:, cols : 2 * cols] = key
        qkv_ref[:, 2 * cols :] = value

        @pl.when(i == 0)
        def _():
            leaving_ref[...] = jnp.zeros_like(leaving_ref)

        for s in range(SUB):
            b = i * SUB + s
            block = slice(s * ROWS, (s + 1) * ROWS)
            for j in range(own):
                ramp = ramp_ref[:, own + j : own + j + 1]
                leave = jnp.where(seg_ref[s] == last_ref[b], ramp, 0.0)
                head = slice(j * HD, (j + 1) * HD)
                scaled = (key[block, head].astype(F32) * leave).astype(BF)
                term = dot(scaled, value[block, head], TN)
                term_ref[s, j] = term
                leaving_ref[j] += reach_ref[j, b] * term

    some = pl.BlockSpec((deep, 4 * cols), lambda i: (0, 0), pipeline_mode=pl.Buffered(1))
    ins = [(v, pair_spec((TALL, width), late)) for late, v in enumerate(n1)]
    ins += [(w, some) for w in w_in]
    ins += [(at.cols, block_spec((SUB, ROWS, 1))), (at.ramps, whole_spec(at.ramps))]
    ins += [(v, scalar_spec()) for v in (at.last, at.out_reach)]
    n = 2 * HALF
    outs = [
        ((n * ROWS, 2 * cols), F32, (TALL, 2 * cols)),
        ((n * ROWS, cols), F32, (TALL, cols)),
        ((n * ROWS, 3 * cols), BF, (TALL, 3 * cols)),
        ((n, own, HD, HD), F32, (SUB, own, HD, HD)),
        ((own, HD, HD), F32, pl.BlockSpec((own, HD, HD), lambda i: (0, 0, 0))),
    ]
    return call(kernel, 2 * STEPS, ins, outs, 4 * n1[0].size * 4 * cols)


def combine(weights, terms, more, reach):
    state = reach * more
    for c in range(2 * HALF):
        state = state + weights(c) * terms(c)
    return state


def attend(h, qkv, gate, term, entering, w_out, at):
    own = at.own
    cols = own * HD
    width = w_out.shape[1]

    def kernel(
        qkv_ref, gate_ref, term_ref, more_ref, w_ref, sc_ref, sr_ref, fade_ref, ramp_ref,
        prev_ref, inner_ref, reach_ref, attn_ref, branch_ref, state_ref,
    ):
        for s, j in ((s, j) for s in range(SUB) for j in range(own)):
            i = (pl.program_id(0) + h * STEPS) * SUB + s
            block = slice(s * ROWS, (s + 1) * ROWS)
            head = slice(j * HD, (j + 1) * HD)
            q = qkv_ref[block, j * HD : (j + 1) * HD]
            k = qkv_ref[block, cols + j * HD : cols + (j + 1) * HD]
            v = qkv_ref[block, 2 * cols + j * HD : 2 * cols + (j + 1) * HD]
            state = combine(
                lambda c: inner_ref[j, i * 2 * HALF + c],
                lambda c: term_ref[c, j],
                more_ref[j],
                reach_ref[j, i],
            ).astype(BF)
            state_ref[s, j] = state
            enter = jnp.where(sc_ref[s] == prev_ref[i], ramp_ref[:, j : j + 1], 0.0)
            weights = (dot(q, k, NT) * mask_of(fade_ref[j], sc_ref[s], sr_ref[s])).astype(BF)
            attn_ref[block, head] = dot(weights, v) + enter * dot(q, state)
        attn = attn_ref[...]
        branch_ref[:, :width] = dot((attn * gate_ref[...]).astype(BF), w_ref[...]).astype(BF)
        rest = jnp.sum(attn * attn, axis=1, keepdims=True)
        branch_ref[:, width:] = strip_of([rest])

    n = HALF
    ins = [
        (qkv, half_spec((TALL, 3 * cols), h)),
        (gate, half_spec((TALL, cols), h)),
        (term, whole_spec(term)),
        (entering, whole_spec(entering)),
        (w_out, whole_spec(w_out)),
        (at.cols, half_spec((SUB, ROWS, 1), h)),
        (at.rows, half_spec((SUB, 1, ROWS), h)),
        (at.fade, whole_spec(at.fade)),
        (at.ramps, whole_spec(at.ramps)),
    ] + [(v, scalar_spec()) for v in (at.prev, at.inner, at.in_reach)]
    outs = [
        ((n * ROWS, cols), F32, (TALL, cols)),
        ((n * ROWS, width + EXTRA), BF, (TALL, width + EXTRA)),
        ((n, own, HD, HD), BF, (SUB, own, HD, HD)),
    ]
    return call(kernel, STEPS, ins, outs, 2 * n * ROWS * cols * (width + 2 * ROWS))


def sglu_rows(n2, g, w_pair, w_third):
    parts = len(w_pair)
    _, hidden, deep = w_pair[0].shape
    block = 2 * ROWS

    def kernel(*refs):
        x_ref, g_ref = refs[:2]
        both, three = (refs[2 + k * parts : 2 + (k + 1) * parts] for k in range(2))
        prod_ref, prod_t, gf_t, gs_t, back_ref = refs[2 + 2 * parts :]
        first = second = grad = None
        for k in range(parts):
            at = slice(k * deep, (k + 1) * deep)
            x, gk = x_ref[:, at], g_ref[:, at]
            a, b, c = dot(x, both[k][0], NT), dot(x, both[k][1], NT), dot(gk, three[k][...], NT)
            first = a if first is None else first + a
            second = b if second is None else second + b
            grad = c if grad is None else grad + c
        prod = (first * second).astype(BF)
        gf = (grad * second).astype(BF)
        gs = (grad * first).astype(BF)
        prod_ref[...] = prod
        prod_t[...] = prod.T
        gf_t[...] = gf.T
        gs_t[...] = gs.T
        for k in range(parts):
            at = slice(k * deep, (k + 1) * deep)
            back_ref[:, at] = (dot(gf, both[k][0]) + dot(gs, both[k][1])).astype(BF)

    n = n2.shape[0] // block
    width = n2.shape[1]
    ins = [(n2, block_spec((block, width))), (g, block_spec((block, width)))]
    ins += [(w, whole_spec(w)) for w in w_pair + w_third]
    outs = [((n * block, hidden), BF, (block, hidden))]
    turned = pl.BlockSpec((hidden, block), lambda i: (0, i))
    outs += [((hidden, n * block), BF, turned)] * 3
    outs += [((n * block, width), BF, (block, width))]
    return call(kernel, n, ins, outs, 10 * n2.size * hidden)


def sglu_last(product, w_third):
    parts = len(w_third)
    deep = w_third[0].shape[1]
    block = 2 * ROWS

    def kernel(*refs):
        for k in range(parts):
            refs[-1][:, k * deep : (k + 1) * deep] = dot(refs[0][...], refs[1 + k][...]).astype(BF)

    n, width = product.shape[0] // block, parts * deep
    ins = [(product, block_spec((block, product.shape[1])))]
    ins += [(w, whole_spec(w)) for w in w_third]
    return call(
        kernel, n, ins, [((n * block, width), BF, (block, width))], 2 * product.size * width
    )[0]


def attend_back_rows(gb, w_out, attn, gate, qkv, at):
    own = at.own
    cols = own * HD
    width = w_out.shape[1]

    def kernel(
        gb_a, gb_b, w_ref, attn_a, attn_b, gate_ref, qkv_ref, sc_ref, ramp_ref, prev_ref, reach_ref,
        ga_ref, gg_ref, mixed_ref, term_ref, leaving_ref,
    ):
        i = pl.program_id(0)
        early = i < STEPS
        extra = jnp.where(early, gb_a[:, width:], gb_b[:, width:]).astype(F32)
        r = extra[:, 0:1] + extra[:, 1:2] + extra[:, 2:3]
        pull = extra[:, 3:4] + extra[:, 4:5] + extra[:, 5:6]
        gm = dot(jnp.where(early, gb_a[:, :width], gb_b[:, :width]), w_ref[...], NT)
        attn, gate = jnp.where(early, attn_a[...], attn_b[...]), gate_ref[...]
        normed = r * attn
        gg_ref[...] = (gm * normed).astype(BF)
        mixed_ref[...] = (normed * gate).astype(BF)
        ga = (r * (gm * gate) - attn * pull).astype(BF)
        ga_ref[...] = ga

        @pl.when(i == 0)
        def _():
            leaving_ref[...] = jnp.zeros_like(leaving_ref)

        for s, j in ((s, j) for s in range(SUB) for j in range(own)):
            b = i * SUB + s
            block = slice(s * ROWS, (s + 1) * ROWS)
            enter = jnp.where(sc_ref[s] == prev_ref[b], ramp_ref[:, j : j + 1], 0.0)
            q = qkv_ref[block, j * HD : (j + 1) * HD].astype(F32)
            term = dot((q * enter).astype(BF), ga[block, j * HD : (j + 1) * HD], TN)
            term_ref[s, j] = term
            leaving_ref[j] += reach_ref[j, b] * term

    n = 2 * HALF
    ins = [(v, pair_spec((TALL, v.shape[1]), late)) for late, v in enumerate(gb)]
    ins += [(w_out, whole_spec(w_out))]
    ins += [(v, pair_spec((TALL, cols), late)) for late, v in enumerate(attn)]
    ins += [
        (gate, block_spec((TALL, cols))),
        (qkv, block_spec((TALL, 3 * cols))),
        (at.cols, block_spec((SUB, ROWS, 1))),
        (at.ramps, whole_spec(at.ramps)),
    ] + [(v, scalar_spec()) for v in (at.prev, at.in_reach)]
    outs = [((n * ROWS, cols), BF, (TALL, cols))] * 3
    outs += [((n, own, HD, HD), F32, (SUB, own, HD, HD))]
    outs += [((own, HD, HD), F32, pl.BlockSpec((own, HD, HD), lambda i: (0, 0, 0)))]
    return call(kernel, 2 * STEPS, ins, outs, 2 * n * ROWS * cols * width)


def project_back(h, qkv, raw, ga, gg, state, term, entering, w_in, width, at):
    own = at.own
    cols = own * HD
    parts = len(w_in)
    deep = width // parts

    def kernel(*refs):
        qkv_ref, raw_ref, ga_ref, gg_ref, state_ref, term_ref, more_ref = refs[:7]
        w_refs = refs[7 : 7 + parts]
        sc_ref, sr_ref, fade_ref, ramp_ref = refs[7 + parts : 11 + parts]
        prev_ref, last_ref, inner_ref, reach_ref, gp_ref, back_ref = refs[11 + parts :]
        for s, j in ((s, j) for s in range(SUB) for j in range(own)):
            i = (pl.program_id(0) + h * STEPS) * SUB + s
            block = slice(s * ROWS, (s + 1) * ROWS)
            head = slice(j * HD, (j + 1) * HD)
            kt = slice(cols + j * HD, cols + (j + 1) * HD)
            vt = slice(2 * cols + j * HD, 2 * cols + (j + 1) * HD)
            q, k, v = qkv_ref[block, head], qkv_ref[block, kt], qkv_ref[block, vt]
            g = ga_ref[block, head]
            mask = mask_of(fade_ref[j], sc_ref[s], sr_ref[s])
            enter = jnp.where(sc_ref[s] == prev_ref[i], ramp_ref[:, j : j + 1], 0.0)
            leave = jnp.where(sc_ref[s] == last_ref[i], ramp_ref[:, own + j : own + j + 1], 0.0)
            later = combine(
                lambda c: inner_ref[j, c * 2 * HALF + i],
                lambda c: term_ref[c, j],
                more_ref[j],
                reach_ref[j, i],
            ).astype(BF)
            weights = (dot(q, k, NT) * mask).astype(BF)
            gs = (dot(g, v, NT) * mask).astype(BF)
            gq = dot(gs, k) + enter * dot(g, state_ref[s, j], NT)
            gk = dot(gs, q, TN) + leave * dot(v, later, NT)
            gv = dot(weights, g, TN) + leave * dot(k, later)
            rq, rk = raw_ref[block, head], raw_ref[block, kt]
            sq, sk = jax.nn.sigmoid(rq), jax.nn.sigmoid(rk)
            gp_ref[block, head] = (gq * (sq * (1.0 + rq * (1.0 - sq)))).astype(BF)
            gp_ref[block, kt] = (gk * (sk * (1.0 + rk * (1.0 - sk)))).astype(BF)
            gp_ref[block, vt] = gv.astype(BF)
        gp_ref[:, 3 * cols :] = gg_ref[...]
        for k in range(parts):
            some = slice(k * deep, (k + 1) * deep)
            back_ref[:, some] = dot(gp_ref[...], w_refs[k][...], NT).astype(BF)

    n = HALF
    some = pl.BlockSpec((deep, 4 * cols), lambda i: (0, 0), pipeline_mode=pl.Buffered(1))
    ins = [
        (qkv, half_spec((TALL, 3 * cols), h)),
        (raw, half_spec((TALL, 2 * cols), h)),
        (ga, half_spec((TALL, cols), h)),
        (gg, half_spec((TALL, cols), h)),
        (state, block_spec((SUB, own, HD, HD))),
        (term, whole_spec(term)),
        (entering, whole_spec(entering)),
    ] + [(w, some) for w in w_in]
    ins += [
        (at.cols, half_spec((SUB, ROWS, 1), h)),
        (at.rows, half_spec((SUB, 1, ROWS), h)),
        (at.fade, whole_spec(at.fade)),
        (at.ramps, whole_spec(at.ramps)),
    ]
    ins += [(v, scalar_spec()) for v in (at.prev, at.last, at.inner, at.out_reach)]
    outs = [
        ((n * ROWS, 4 * cols), BF, (TALL, 4 * cols)),
        ((n * ROWS, width), BF, (TALL, width)),
    ]
    return call(kernel, STEPS, ins, outs, 2 * n * ROWS * 4 * cols * width)


def one_by_one(count, shape):
    spec = pl.BlockSpec(shape, lambda i: (0,) * len(shape), pipeline_mode=pl.Buffered(1))
    return [(shape, BF, spec) for _ in range(count)]


def grads_by_left(left, right, n, below=None):
    cut, cols = left[0].shape[1] // n, right[0].shape[1]
    more = 0 if below is None else 2 * below[0].shape[1]

    def kernel(*refs):
        l0, l1, r0, r1 = refs[:4]
        outs = refs[len(refs) - n :]
        grad = (dot(l0[...], r0[...], TN) + dot(l1[...], r1[...], TN)).astype(BF)
        for k in range(n):

            @pl.when(pl.program_id(0) == k)
            def _():
                outs[k][:cut] = grad
                if more:
                    a_ref, b_ref, from_a, row = refs[4:8]
                    part = jnp.where(from_a[k] == 1, a_ref[row[k]], b_ref[row[k]])
                    outs[k][cut : cut + more // 2] = part[:, :cols]
                    outs[k][cut + more // 2 :] = part[:, cols:]

    ins = [(a, pl.BlockSpec((a.shape[0], cut), lambda i: (0, i))) for a in left]
    ins += [(a, whole_spec(a)) for a in right]
    if more:
        ins += [(a, whole_spec(a)) for a in below[:2]] + [(a, scalar_spec()) for a in below[2:]]
    outs = one_by_one(n, (cut + more, cols))
    return call(kernel, n, ins, outs, 4 * left[0].size * cols)


def grads_by_right(lefts, right, cut, first, n, step=1):
    count = len(lefts)
    tall = lefts[0][0].shape[0]

    def kernel(*refs):
        r0, r1 = refs[2 * count : 2 * count + 2]
        outs = refs[2 * count + 2 :]
        for m in range(count):
            l0, l1 = refs[2 * m : 2 * m + 2]
            grad = (dot(l0[...], r0[...]) + dot(l1[...], r1[...])).astype(BF)
            for k in range(n):

                @pl.when(pl.program_id(0) == k)
                def _():
                    outs[k][m] = grad

    ins = [(a, whole_spec(a)) for left in lefts for a in left]
    ins += [(a, pl.BlockSpec((a.shape[0], cut), lambda i: (0, first + step * i))) for a in right]
    outs = one_by_one(n, (count, tall, cut))
    return call(kernel, n, ins, outs, 4 * count * right[0].size * tall)


def grads_out(left, right, width):
    def kernel(l0, l1, r0, r1, out):
        out[...] = (dot(l0[...], r0[...], TN) + dot(l1[...], r1[...], TN)).astype(BF)

    cut, (rows, tall) = width // 4, left.shape
    spec = lambda rows: pl.BlockSpec((rows, cut), lambda i: (0, i))
    half = lambda k: pl.BlockSpec((rows // 2, tall), lambda i: (k, 0))
    ins = [(left, half(k)) for k in (0, 1)] + [(a, spec(a.shape[0])) for a in right]
    return call(kernel, 4, ins, [((tall, width), BF, spec(tall))], 2 * left.size * width)[0]


def add_strips(width, *parts):
    total = parts[0][:, :width].astype(F32)
    for p in parts[1:]:
        total = total + p[:, :width].astype(F32)
    out = [total.astype(BF)]
    if parts[0].shape[1] > width:
        rest = 0.0
        for p in parts:
            for n in range(3):
                rest = rest + p[:, width + n : width + n + 1].astype(F32)
        lane = lax.broadcasted_iota(jnp.int32, (total.shape[0], EXTRA), 1)
        strip = jnp.zeros((total.shape[0], EXTRA), F32)
        for n in range(3):
            top = rest.astype(BF).astype(F32)
            strip = jnp.where(lane == n, top, strip)
            rest = rest - top
        out.append(strip.astype(BF))
    return out


def add_last(a, b, width):
    n, wide = a.shape[0] // ROWS, a.shape[1]
    half = ROWS // 2

    def kernel(a_ref, b_ref, low_ref, high_ref):
        parts = add_strips(width, a_ref[...], b_ref[...])
        for v, at in zip(parts, (slice(0, width), slice(width, wide))):
            low_ref[:, at] = v[:half]
            high_ref[:, at] = v[half:]

    block = pl.BlockSpec((ROWS, wide), lambda i: (n - 1, 0))
    one = pl.BlockSpec((half, wide), lambda i: (0, 0))
    return call(kernel, 1, [(a, block), (b, block)], [((half, wide), BF, one)] * 2, ROWS * wide)


def add_halves(a, b, u, v, width):
    wide = a.shape[1]
    half = ROWS // 2

    def kernel(a2, a4, b2, b4, u_ref, v_ref, to_2, to_4):
        low, high = slice(0, half), slice(half, ROWS)
        for out, rows, terms in (
            (to_2, low, (a2[low], b2[low])),
            (to_2, high, (a2[high], b2[high], v_ref[...])),
            (to_4, low, (a4[low], b4[low], u_ref[...])),
            (to_4, high, (a4[high], b4[high])),
        ):
            parts = add_strips(width, *terms)
            for p, at in zip(parts, (slice(0, width), slice(width, wide))):
                out[rows, at] = p

    spec = lambda k: pl.BlockSpec((ROWS, wide), lambda i: (k, 0))
    ins = [(t, spec(k)) for t in (a, b) for k in (1, 2)] + [(u, whole_spec(u)), (v, whole_spec(v))]
    return call(kernel, 1, ins, [((ROWS, wide), BF, spec(0))] * 2, ROWS * wide)


def strip_of(column):
    lane = lax.broadcasted_iota(jnp.int32, (column[0].shape[0], EXTRA), 1)
    strip = jnp.zeros(lane.shape, F32)
    for m, rest in enumerate(column):
        for n in range(3):
            top = rest.astype(BF).astype(F32)
            strip = jnp.where(lane == 3 * m + n, top, strip)
            rest = rest - top
    return strip.astype(BF)


def mid_rows(sums, inputs, dest):
    width = inputs.shape[1]
    cut = width // 4
    block = ROWS // 2

    def kernel(a, b, c, d, x_ref, dest_ref, mid_ref, branch_ref, scale_ref, norm_ref):
        branch = square = None
        for ref in (a, b, c, d):
            part = ref[:, :width].astype(F32)
            extra = ref[:, width:].astype(F32)
            more = extra[:, 0:1] + extra[:, 1:2] + extra[:, 2:3]
            branch = part if branch is None else branch + part
            square = more if square is None else square + more
        r = lax.rsqrt(square / width + EPS)
        mid = x_ref[...].astype(F32) + r * branch
        branch_ref[...] = branch.astype(BF)
        scale_ref[...] = jnp.broadcast_to(r, (block, EXTRA))
        mid_ref[...] = mid
        norm = (mid * inverse_rms(mid)).astype(BF)
        for p in range(4):
            to = pl.ds(pl.multiple_of(dest_ref[p] * cut, cut), cut)
            norm_ref[:, to] = norm[:, p * cut : (p + 1) * cut]

    ins = [(v, block_spec((block, width + EXTRA))) for v in sums]
    ins += [(inputs, block_spec((block, width))), (dest, scalar_spec())]
    outs = [
        ((ROWS, width), F32, (block, width)),
        ((ROWS, width), BF, (block, width)),
        ((ROWS, EXTRA), F32, (block, EXTRA)),
        ((ROWS, width), BF, (block, width)),
    ]
    return call(kernel, 2, ins, outs, 20 * ROWS * width)


def mid_back_rows(sums, out_grad, mid, branch, scale, dest):
    width = mid.shape[1]
    cut = width // 4
    block = ROWS // 2

    def kernel(a, b, c, d, g_ref, mid_ref, branch_ref, scale_ref, dest_ref, grad_ref, out_ref):
        parts = []
        for p in range(4):
            at = pl.ds(pl.multiple_of(dest_ref[p] * cut, cut), cut)
            part = a[:, at].astype(F32)
            for ref in (b, c, d):
                part = part + ref[:, at].astype(F32)
            parts.append(part)
        grad = g_ref[...].astype(F32) + srms_back(mid_ref[...], jnp.concatenate(parts, axis=1))
        grad_ref[...] = grad
        low = grad.astype(BF)
        out_ref[:, :width] = low
        inward = low.astype(F32) * branch_ref[...].astype(F32)
        inward = jnp.mean(inward, axis=1, keepdims=True)
        r = scale_ref[:, 0:1]
        out_ref[:, width:] = strip_of([r, r * r * r * inward])

    ins = [(v, block_spec((block, width))) for v in (*sums, out_grad, mid, branch)]
    ins += [(scale, block_spec((block, EXTRA))), (dest, scalar_spec())]
    outs = [
        ((ROWS, width), F32, (block, width)),
        ((ROWS, width + EXTRA), BF, (block, width + EXTRA)),
    ]
    return call(kernel, 2, ins, outs, 20 * ROWS * width)


def renew_turned(grad, weight, moment, average, fan, tokens):
    few, total = weight.shape
    block = 16

    def kernel(g_ref, w_ref, m_ref, a_ref, m_new, w_new, a_new):
        for p in range(8):
            for t in range(4):
                for j in range(2):
                    col = t * (total // 4) + (8 * (p % 2) + 4 * j + p // 2) * HD
                    to = slice(col, col + HD)
                    at = slice((2 * t + j) * HD, (2 * t + j + 1) * HD)
                    new = renew(
                        w_ref[:, to], m_ref[:, to], a_ref[:, to], g_ref[p, :, at].astype(F32),
                        fan, tokens,
                    )
                    m_new[:, to], w_new[:, to], a_new[:, to] = new

    ins = [(grad, pl.BlockSpec((8, block, grad.shape[2]), lambda i: (0, i, 0)))]
    ins += [(v, block_spec((block, total))) for v in (weight, moment, average)]
    outs = [((few, total), F32, (block, total))] * 3
    return call(kernel, few // block, ins, outs, 10 * weight.size)


def cut4(v, axis):
    n = v.shape[axis] // 4
    return [lax.slice_in_dim(v, k * n, (k + 1) * n, axis=axis) for k in range(4)]


def strip_sum(v):
    strip = v[:, v.shape[1] - EXTRA :].astype(F32)
    return strip[:, 0:1] + strip[:, 1:2] + strip[:, 2:3]


def pieces(v):
    out = []
    for _ in range(3):
        top = lax.reduce_precision(v, 8, 7)
        out.append(top.astype(BF))
        v = v - top
    return out


class Places:
    def __init__(self, plan, seq_lengths, decay_rate, rows):
        size = plan.size
        group_rows = size * rows
        tokens = group_rows * plan.groups
        ends = jnp.cumsum(seq_lengths)

        def seg_at(place):
            mark = jnp.sum((place[..., None] >= ends).astype(jnp.int32), axis=-1)
            return jnp.where(place < 0, -1, mark)

        first_block = plan.group * size
        blocks = first_block + plan.slot_ids
        seg = seg_at(blocks[:, None] * rows + jnp.arange(rows, dtype=jnp.int32)[None, :])
        prev = seg_at(blocks * rows - 1)
        last = seg[:, rows - 1]
        head_ids = plan.head_ids if hasattr(plan, "head_ids") else plan.own * plan.p + jnp.arange(plan.own)
        rate = jnp.take(decay_rate, head_ids)

        def reach(gap, same):
            return jnp.where(
                same & (gap >= 0), jnp.exp(-rate[:, None, None] * (rows * jnp.maximum(gap, 0))), 0.0
            )

        inner = reach(
            (blocks[:, None] - blocks[None, :] - 1).astype(F32)[None],
            (prev[:, None] == last[None, :])[None],
        )
        border = seg_at((first_block + size) * rows - 1)
        out_reach = reach(
            (first_block + size - 1 - blocks).astype(F32)[None, None], (last == border)[None, None]
        )[:, 0]
        entry = seg_at(first_block * rows - 1)
        in_reach = reach((blocks - first_block).astype(F32)[None, None], (prev == entry)[None, None])[
            :, 0
        ]
        longest = tokens // 4
        hops = min(-(-longest // group_rows), plan.groups - 1)

        def hop_factor(j, ahead):
            if ahead:
                here, there = border, seg_at((first_block + j * size) * rows - 1)
            else:
                here, there = entry, seg_at((first_block - (j - 1) * size) * rows - 1)
            return jnp.where(here == there, jnp.exp(-rate * ((j - 1) * group_rows)), 0.0)

        def bring(total, ahead):
            n = plan.groups
            got = jnp.zeros_like(total)
            for j in range(1, hops + 1):
                pairs = [(i + j, i) if ahead else (i, i + j) for i in range(n - j)]
                part = lax.ppermute(total, plan.fs, pairs)
                got = got + hop_factor(j, ahead)[:, None, None] * part
            return got

        self.bring, self.hop = bring, hop_factor
        self.inner = inner.reshape(inner.shape[0], -1)
        self.out_reach, self.in_reach = out_reach, in_reach
        self.own = plan.own
        self.cols, self.rows = seg[:, :, None], seg[:, None, :]
        self.prev, self.last = prev, last
        step = jnp.arange(rows).astype(F32)
        spread = step[:, None] - step[None, :]
        fade = jnp.exp(-rate[:, None, None] * jnp.maximum(spread, 0.0)[None])
        self.fade = jnp.where((spread >= 0)[None], fade, 0.0)
        ramps = [jnp.exp(-rate[None] * step[:, None]), jnp.exp(-rate[None] * (rows - step)[:, None])]
        blank = jnp.zeros((rows, EXTRA - 2 * plan.own), F32)
        self.ramps = jnp.concatenate(ramps + [blank], axis=1)


class Square:
    def __init__(self):
        self.tp = ("y", "x", "c")
        self.fs = ("z",)
        self.size = 8
        self.groups = 4

    def begin(self):
        self.z = lax.axis_index("z")
        self.y = lax.axis_index("y")
        self.c = lax.axis_index("c")
        self.p = lax.axis_index(self.tp)
        self.q = self.p // 2
        self.group = self.z
        self.slot_ids = self.p ^ jnp.array(XORS, jnp.int32)
        self.head_ids = 8 * self.c + 4 * jnp.arange(2) + self.q
        self.order = jnp.array(MEETS, jnp.int32)[self.z]
        self.dest = jnp.array(PLACES, jnp.int32)[self.z]

    def turn(self, v, places):
        wide = v.shape[1] // 4
        return jnp.concatenate(
            [lax.dynamic_slice_in_dim(v, places[k] * wide, wide, axis=1) for k in range(4)], axis=1
        )

    def slots(self, own, one, two, three):
        outer = (self.z == 0) | (self.z == 3)
        return [
            own,
            one[0],
            pin(jnp.where(outer, two[0], one[1])),
            pin(jnp.where(outer, three, two[1])),
        ]

    def by_y(self, mine, got, axis):
        first = self.y == 0
        parts = [jnp.where(first, mine, got), jnp.where(first, got, mine)]
        return pin(jnp.concatenate(parts, axis=axis))

    def of_y(self, one, two):
        first = self.y == 0
        return pin(jnp.where(first, one, two)), pin(jnp.where(first, two, one))


def over(axis, pairs=SWAP):
    return lambda v: pin(lax.ppermute(pin(v), axis, pairs))


to_x, to_y, to_core = over("x"), over("y"), over("c")


to_pair = over("z", [(0, 1), (1, 0), (2, 3), (3, 2)])
to_middle = over("z", [(1, 2), (2, 1)])
outward = over("z", [(1, 0), (2, 3)])
inward_z = over("z", [(0, 1), (3, 2)])


def spread0(own):
    return to_pair(own), to_middle(own)


def spread1(one):
    return outward(one[1]), to_middle(one[0])


def spread2(two):
    return outward(two[1])


def gather1(g):
    return inward_z(g[3])


def gather2(g2, third):
    return inward_z(g2), to_middle(third)


def gather3(first, second):
    return to_pair(first), to_middle(second)


def plus(a, b):
    return (a.astype(F32) + b.astype(F32)).astype(BF)


def square_layer(plan, places, lengths, inputs, out_grad, attn_in, attn_out, sglu_in, sglu_out):
    rows, width = inputs.shape
    h2 = rows // 2
    cut = width // 4
    clock = Clock()
    now, end = clock.now, clock.end

    order, dest = plan.order, plan.dest

    def pick(stack, place):
        return lax.dynamic_index_in_dim(stack, place, 0, False)

    xf = inputs.astype(F32)
    n1 = pin(plan.turn((xf * inverse_rms(xf)).astype(BF), order))
    og = pin(plan.turn(out_grad, order))
    few = attn_in.shape[0]
    view = attn_in.astype(BF).reshape(few, 4, 2, 2, 4, HD).transpose(4, 2, 0, 1, 3, 5)
    own_in = lax.all_to_all(view.reshape(8, few, -1), plan.tp, 0, 0, tiled=True)
    own_in = own_in.reshape(8 * few, -1)
    deep, across = own_in.shape
    own_out = attn_out.astype(BF)
    own_w = pin(jnp.concatenate([own_in, own_out[:, :across], own_out[:, across:]]))
    end(own_w, n1, og)

    a_w, a_n1 = now(own_w, n1)
    w1 = spread0(a_w)
    nx, ny = to_x(a_n1), to_y(a_n1)
    at = places(now(lengths))
    hid = sglu_in.shape[2] // 2
    three = pin(now(sglu_in).astype(BF)).swapaxes(1, 2)
    three = jnp.concatenate([three, sglu_out.astype(BF)[None]])
    my_three, to_three = plan.of_y(three[:, :hid], three[:, hid:])
    tables = [at.cols, at.rows, at.prev, at.last, at.fade, at.ramps]
    tables += [at.inner, at.out_reach, at.in_reach, at.hop(1, False), at.hop(1, True)]
    end(*w1, nx, ny, my_three, to_three, *tables)

    w2 = spread1(now(*w1))
    ax, ay = now(nx, ny)
    nd = to_x(ay[:h2]), to_y(ax[h2:])
    end(*w2, *nd)

    w3 = spread2(now(*w2))
    a_og, a_three = now(og, to_three)
    gx = to_x(a_og)
    got = to_y(a_three)
    n1_a = pin(jnp.concatenate([n1, nx, ny, *now(*nd)]))
    norm1 = n1_a, to_core(n1_a)
    own_three = plan.by_y(my_three, got, 2)
    own_pair, own_third = pin(own_three[:2]), pin(own_three[2])
    end(w3, gx, *norm1, own_pair, own_third)

    pair1 = spread0(now(own_pair))
    gy = to_y(now(og))
    w_in = plan.slots(own_w, now(*w1), now(*w2), now(w3))
    outs = jnp.stack([w[deep:] for w in w_in])
    w_mine = [pick(outs, dest[2 * plan.c + j]) for j in (0, 1)]
    w_got = to_core(jnp.concatenate([pick(outs, dest[2 * (1 - plan.c) + j]) for j in (0, 1)]))
    core0 = plan.c == 0
    raw, gate, qkv, term, leaving = project((now(norm1[0]), norm1[1]), w_in, at)
    end(*pair1, gy, w_got, leaving)

    w_rows = []
    for j in (0, 1):
        got = w_got[j * 2 * few : (j + 1) * 2 * few]
        for half in (jnp.where(core0, w_mine[j], got), jnp.where(core0, got, w_mine[j])):
            w_rows.append(jnp.concatenate([half[:few], half[few:]], axis=1))
    w_out = pin(jnp.concatenate(w_rows))
    entering = at.bring(now(leaving), False)
    attn_b, give, state_b = attend(1, qkv, gate, term, entering, w_out, at)
    end(give)

    third1 = spread0(after(own_third, entering))
    a_qkv, give = now(qkv, give)
    attn_a, keep, state_a = attend(0, a_qkv, gate, term, entering, w_out, at)
    got = to_core(give)
    a_gx, a_gy = after(gx, entering), after(gy, entering)
    gd = to_x(a_gy[:h2]), to_y(a_gx[h2:])
    end(*third1, got, keep, *gd)

    def first_step(keep, got):
        low, high = add_last(keep, got, width)
        return to_x(low), to_y(high)

    def total(*parts):
        out = parts[0].astype(F32)
        for p in parts[1:]:
            out = out + p.astype(F32)
        return out

    keep, got = now(keep, got)
    u, v = first_step(keep, got)
    third2 = spread1(now(*third1))
    g_a = pin(jnp.concatenate([og, gx, gy, *now(*gd)]))
    end(u, v, *third2, g_a)

    to_2, to_4 = add_halves(keep, got, *now(u, v), width)
    sx, sy = to_x(to_2), to_y(to_4)
    pair2 = spread1(now(*pair1))
    g_b = to_core(now(g_a))
    end(sx, sy, *pair2, g_b)

    pair3 = spread2(now(*pair2))
    mid, branch, r_attn, n2 = mid_rows((keep, got, *now(sx, sy)), inputs, dest)
    mx, my, mc = to_x(n2), to_y(n2), to_core(n2)
    end(mx, my, mc, pair3)

    third3 = spread2(now(*third2))
    ax, ay = now(mx, my)
    md = to_x(ay[:h2]), to_y(ax[h2:])
    mxyc = to_core(jnp.concatenate([ax, ay]))
    mdc = to_core(jnp.concatenate(md))
    n2_a = pin(jnp.concatenate([n2, mx, my, *md]))
    n2_b = pin(jnp.concatenate([mc, mxyc, mdc]))
    w_pair = plan.slots(own_pair, now(*pair1), now(*pair2), now(pair3))
    end(third3, n2_a, n2_b, *w_pair)

    w_third = plan.slots(own_third, now(*third1), now(*third2), now(third3))
    prod_b, turned_b, gf_b, gs_b, give = sglu_rows(n2_b, g_b, w_pair, w_third)
    end(give)

    give, a_n2 = now(give, n2_a)
    got = to_core(give)
    prod_a, turned_a, gf_a, gs_a, keep = sglu_rows(a_n2, g_a, w_pair, w_third)
    end(keep, got)

    keep, got = now(keep, got)
    u, v = first_step(keep, got)
    lefts = [(now(gf_a), gf_b), (gs_a, gs_b)]
    d_late = grads_by_right(lefts, (n2_a, n2_b), cut, 2, 2)
    end(u, v, *d_late)

    d_late = now(*d_late)
    pair1 = inward_z(d_late[1])
    lefts = [(now(gf_a), gf_b), (gs_a, gs_b)]
    d_pair = [*grads_by_right(lefts, (n2_a, n2_b), cut, 0, 2), *d_late]
    to_2, to_4 = add_halves(keep, got, *now(u, v), width)
    sx, sy = to_x(to_2), to_y(to_4)
    d_third = grads_by_right([(now(turned_a), turned_b)], (g_a, g_b), cut, 0, 4)

    def join(part, more):
        return pin(plus(part, now(more)))

    end(sx, sy, pair1, *d_third, *d_pair)

    d_third = [d[0] for d in now(*d_third)]
    d_pair = now(*d_pair)
    pair2 = gather2(d_pair[2], pin(plus(d_pair[3], now(pair1))))
    grad_mid, gb = mid_back_rows((keep, got, *now(sx, sy)), out_grad, mid, branch, r_attn, dest)
    bx, by, bc = to_x(gb), to_y(gb), to_core(gb)
    o_give = sglu_last(now(prod_b), w_third)
    o_keep = sglu_last(now(prod_a), w_third)

    end(bx, by, bc, *pair2, o_keep, o_give)

    third1 = gather1(now(*d_third))
    o_got = to_core(now(o_give))
    ax, ay = now(bx, by)
    bd = to_x(ay[:h2]), to_y(ax[h2:])
    bxyc = to_core(jnp.concatenate([ax, ay]))
    bdc = to_core(jnp.concatenate(bd))
    gb_a = pin(jnp.concatenate([gb, bx, by, *bd]))
    gb_b = pin(jnp.concatenate([bc, bxyc, bdc]))
    a_pair = now(*pair2)
    ready = [
        (pin(plus(d_pair[1][m], a_pair[1][m])), pin(plus(d_pair[2][m], a_pair[0][m])))
        for m in (0, 1)
    ]
    end(third1, gb_a, gb_b, o_got, *ready[0], *ready[1])

    third2 = gather2(now(d_third[2]), join(d_third[3], third1))
    ou, ov = first_step(*now(o_keep, o_got))
    ga, gg, mixed, d_term, d_leaving = attend_back_rows(
        (now(gb_a), gb_b), w_out, (attn_a, attn_b), gate, qkv, at
    )
    end(*third2, d_leaving, ou, ov)

    first3 = gather3(*now(*ready[0]))
    d_out = grads_out(now(mixed), (gb_a, gb_b), width)
    d_entering = at.bring(now(d_leaving), True)

    def back_half(h, first, state):
        return project_back(
            h, first, raw, ga, gg, state, d_term, d_entering, w_in, width, at
        )

    gp_b, give = back_half(1, after(qkv, d_out), state_b)
    end(*first3, give, d_out)

    second3 = gather3(*now(*ready[1]))
    parts = now(d_out).reshape(2, 2, few, width)
    w_keep = jnp.where(core0, parts[:, 0], parts[:, 1])
    w_got = to_core(jnp.where(core0, parts[:, 1], parts[:, 0]))
    a_qkv, give = now(qkv, give)
    gp_a, keep = back_half(0, a_qkv, state_a)
    got = to_core(give)
    ready = join(d_third[1], third2[1]), join(d_third[2], third2[0])
    end(*second3, keep, got, w_keep, w_got, *ready)

    third3 = gather3(*now(*ready))
    keep, got = now(keep, got)
    u, v = first_step(keep, got)
    mine = (order // 2 == plan.c).astype(jnp.int32)
    d_w = grads_by_left(norm1, (now(gp_a), gp_b), 4, (*now(w_keep, w_got), mine, order % 2))
    end(u, v, *third3, *d_w)

    d_w = now(*d_w)
    w1 = gather1(d_w)
    to_2, to_4 = add_halves(keep, got, *now(u, v), width)
    sx, sy = to_x(to_2), to_y(to_4)
    sum_three = [
        total(d_pair[0][0], *now(*first3)),
        total(d_pair[0][1], *now(*second3)),
        total(d_third[0], *now(*third3)),
    ]
    sum_three = jnp.stack([v.astype(BF) for v in sum_three])
    my_three, to_three = plan.of_y(sum_three[:, :, :rows], sum_three[:, :, rows:])
    end(sx, sy, w1, my_three, to_three)

    w2 = gather2(d_w[2], join(d_w[3], w1))
    three_got = to_y(now(to_three))
    grad_norm1 = total(keep[:rows], got[:rows], *now(sx, sy))
    input_grad = grad_mid + srms_back(xf, plan.turn(grad_norm1, dest))
    summed = pin(plus(d_w[2], w2[0]))
    end(*w2, three_got, summed)

    ready = join(d_w[1], w2[1]), now(summed)
    w3 = gather3(*ready)
    to_2, to_4 = add_halves(after(o_keep, *ready), o_got, *now(ou, ov), width)
    ox, oy = to_x(to_2), to_y(to_4)
    sum_three = plan.by_y(my_three, now(three_got), 1)
    sum_pair = pin(sum_three[:2].swapaxes(1, 2)).astype(F32)
    sum_third = sum_three[2].astype(F32)
    end(*w3, ox, oy)

    w3 = now(*w3)
    sum_in = total(*[v[:deep] for v in (d_w[0], *w3)])
    sum_in = pin(sum_in.astype(BF)).reshape(8, few, across)
    sum_in = lax.all_to_all(sum_in, plan.tp, 0, 0, tiled=True)
    sum_out = pin(total(*[v[deep:] for v in (d_w[0], *w3)]))
    sum_out = jnp.concatenate([sum_out[:few], sum_out[few:]], axis=1)
    output = mid + plan.turn(total(o_keep[:rows], o_got[:rows], *now(ox, oy)), dest)
    return output, input_grad, sum_in, sum_out, sum_pair, sum_third


class Plain:
    def __init__(self, wide, narrow):
        self.tp = ("narrow",)
        self.fs = ("wide",)
        self.size = narrow
        self.groups = wide

    def begin(self):
        self.p = lax.axis_index("narrow")
        self.group = lax.axis_index("wide")
        self.slot_ids = jnp.arange(self.size, dtype=jnp.int32)

    def turn(self, v):
        return v

    def rows_all(self, a):
        whole = lax.all_gather(a, "narrow", axis=0, tiled=True)
        return whole[: whole.shape[0] // 2], whole[whole.shape[0] // 2 :]

    def rows_sum(self, keep, give, kind=BF):
        total = lax.psum_scatter(
            jnp.concatenate([keep, give]), "narrow", scatter_dimension=0, tiled=True
        )
        return total.astype(F32)

    def attn_in(self, w):
        rows, cols = w.shape
        each = cols // 4 // self.size
        view = w.reshape(rows, 4, self.size, each).transpose(2, 0, 1, 3)
        view = view.reshape(self.size, rows, 4 * each)
        mine = lax.all_to_all(view, "narrow", 0, 0, tiled=True)
        mine = mine.reshape(self.size * rows, 4 * each)
        return cut4(lax.all_gather(mine, "wide", axis=0, tiled=True), 0)

    def attn_in_back(self, g):
        cols = g.shape[1]
        total = lax.psum_scatter(g.astype(BF), "wide", scatter_dimension=0, tiled=True)
        rows = total.shape[0] // self.size
        view = total.reshape(self.size, rows, cols)
        mine = lax.all_to_all(view, "narrow", 0, 0, tiled=True)
        mine = mine.reshape(self.size, rows, 4, cols // 4).transpose(1, 2, 0, 3)
        return mine.reshape(rows, cols * self.size).astype(F32)

    def attn_out(self, w):
        whole = lax.all_gather(w, ("wide", "narrow"), axis=0, tiled=True)
        each = whole.shape[0] // self.size
        return lax.dynamic_slice_in_dim(whole, self.p * each, each)

    def attn_out_back(self, g):
        each = g.shape[0]
        whole = jnp.zeros((each * self.size, g.shape[1]), BF)
        whole = lax.dynamic_update_slice_in_dim(whole, g.astype(BF), self.p * each, 0)
        total = lax.psum_scatter(whole, ("wide", "narrow"), scatter_dimension=0, tiled=True)
        return total.astype(F32)

    def sglu(self, pair, third):
        return pair, third

    def sglu_all(self, both, back):
        pair = lax.all_gather(both.swapaxes(1, 2), "wide", axis=2, tiled=True)
        third = lax.all_gather(back, "wide", axis=1, tiled=True)
        return cut4(pair, 2), cut4(third, 1)

    def pair_back(self, g):
        g = jnp.concatenate([g[k] for k in range(4)], axis=2)
        total = lax.psum_scatter(g, "wide", scatter_dimension=2, tiled=True)
        return total.swapaxes(1, 2).astype(F32)

    def third_back(self, g):
        g = jnp.concatenate([g[k] for k in range(4)], axis=1)
        total = lax.psum_scatter(g, "wide", scatter_dimension=1, tiled=True)
        return total.astype(F32)


def plain_layer(plan, places, lengths, inputs, out_grad, attn_in, attn_out, sglu_in, sglu_out):
    rows, width = inputs.shape
    at = places(lengths)
    w_out = plan.attn_out(attn_out.astype(BF))
    w_in = plan.attn_in(attn_in.astype(BF))
    w_pair, w_third = plan.sglu_all(sglu_in.astype(BF), sglu_out.astype(BF))
    xf = inputs.astype(F32)
    norm1 = plan.rows_all(plan.turn((xf * inverse_rms(xf)).astype(BF)))
    grad_rows = plan.rows_all(plan.turn(out_grad))
    raw, gate, qkv, term, leaving = project(norm1, w_in, at)
    entering = at.bring(leaving, False)
    attn, branch, state = [None] * 2, [None] * 2, [None] * 2
    for h in (1, 0):
        attn[h], branch[h], state[h] = attend(h, qkv, gate, term, entering, w_out, at)
    square = plan.rows_sum(*[strip_sum(v) for v in branch], F32)
    branch = plan.rows_sum(*[v[:, :width] for v in branch])
    r_attn = lax.rsqrt(square / width + EPS)
    mid = xf + r_attn * branch
    r_mid = inverse_rms(mid)
    norm2 = plan.rows_all(plan.turn((mid * r_mid).astype(BF)))

    product, turned, grad_first, grad_second, back = [[None] * 2 for _ in range(5)]
    for h in (1, 0):
        product[h], turned[h], grad_first[h], grad_second[h], back[h] = sglu_rows(
            norm2[h], grad_rows[h], w_pair, w_third
        )
    cut = width // 4
    sum_third = plan.third_back([g[0] for g in grads_by_right([turned], grad_rows, cut, 0, 4)])
    grad_norm2 = plan.rows_sum(*back)
    sum_pair = plan.pair_back(grads_by_right([grad_first, grad_second], norm2, cut, 0, 4))

    grad_mid = out_grad.astype(F32) + srms_back(mid, plan.turn(grad_norm2))
    grad_branch = grad_mid.astype(BF)
    inward = jnp.mean(grad_branch.astype(F32) * branch, axis=1, keepdims=True)
    extra = pieces(r_attn) + pieces(r_attn * r_attn * r_attn * inward)
    extra.append(jnp.zeros((rows, 128 - len(extra)), BF))
    grad_branch = jnp.concatenate([grad_branch] + extra, axis=1)
    grad_branch = plan.rows_all(grad_branch)
    branch_out = plan.rows_sum(*[sglu_last(v, w_third) for v in product])
    output = mid + plan.turn(branch_out)
    grad_attn, grad_gate, mixed, d_term, d_leaving = attend_back_rows(
        grad_branch, w_out, attn, gate, qkv, at
    )
    d_entering = at.bring(d_leaving, True)
    grad_pre, back = [None] * 2, [None] * 2
    for h in (1, 0):
        grad_pre[h], back[h] = project_back(
            h, qkv, raw, grad_attn, grad_gate, state[h], d_term, d_entering, w_in, width, at
        )
    grad_win = jnp.concatenate(grads_by_left(norm1, grad_pre, 4))
    sum_in = plan.attn_in_back(grad_win)
    sum_out = plan.attn_out_back(grads_out(mixed, grad_branch, width))
    grad_norm1 = plan.rows_sum(*back)
    input_grad = grad_mid + srms_back(xf, plan.turn(grad_norm1))
    return output, input_grad, sum_in, sum_out, sum_pair, sum_third


def per_device(plan, layer, *args):
    inputs, out_grad, seq_lengths, decay_rate = args[:4]
    weights, moments, averages = args[4:8], args[8:12], args[12:16]
    plan.begin()
    rows, width = inputs.shape
    plan.own = decay_rate.shape[0] // plan.size

    def places(lengths):
        return Places(plan, lengths, decay_rate, rows)

    output, input_grad, *grads = layer(plan, places, seq_lengths, inputs, out_grad, *weights)
    tokens = plan.size * rows * plan.groups
    fans = (width, width, width, weights[3].shape[0] * lax.axis_size(plan.narrow))
    new = []
    for w, m, a, grad, fan in zip(weights, moments, averages, grads, fans):
        if grad.shape == w.shape:
            new.append(renew(w, m, a, grad, fan, tokens))
        else:
            new.append(renew_turned(grad, w, m, a, fan, tokens))
    return (output, input_grad) + tuple(n[i] for i in range(3) for n in new)


def solution(mesh):
    wide, narrow = mesh.shape["wide"], mesh.shape["narrow"]
    if (wide, narrow) == (8, 4):
        mesh = Mesh(mesh.devices.reshape(4, 2, 2, 2), ("z", "y", "x", "c"))
        plan, layer, w, n = Square(), square_layer, ("z", "y"), ("x", "c")
    else:
        plan, layer, w, n = Plain(wide, narrow), plain_layer, ("wide",), ("narrow",)
    plan.narrow = n
    by_rows = P(w + n, None)
    pair, third = P(None, w, n), P(n, w)
    weights = (by_rows, by_rows, pair, third)

    def run(*args):
        return per_device(plan, layer, *args)

    return jax.shard_map(
        run,
        mesh=mesh,
        in_specs=(by_rows, by_rows, P(), P()) + weights * 3,
        out_specs=(by_rows, by_rows) + weights * 3,
        check_vma=False,
    )
```

```python
import math

import jax
import jax.numpy as jnp
from jax import lax
from jax.experimental import pallas as pl
from jax.experimental.layout import Layout, with_layout_constraint
from jax.experimental.pallas import tpu as pltpu
from jax.sharding import Mesh
from jax.sharding import PartitionSpec as P

BLOCK = 256
EPS = 1e-06
MU = 0.9
BETA = 0.8
HIGH = lax.Precision.HIGHEST
BF = jnp.bfloat16
F32 = jnp.float32
SWAP = [(0, 1), (1, 0)]
XORS = (0, 2, 4, 6, 1, 3, 5, 7)
MEETS = ((0, 1, 2, 3), (1, 0, 2, 3), (2, 3, 1, 0), (3, 2, 1, 0))
PLACES = ((0, 1, 2, 3), (1, 0, 2, 3), (3, 2, 0, 1), (3, 2, 1, 0))


def dot(a, b, dims=((1,), (0,))):
    return lax.dot_general(a, b, (dims, ((), ())), preferred_element_type=F32)


def inverse_rms(v):
    return lax.rsqrt(jnp.mean(v * v, axis=-1, keepdims=True) + EPS)


def srms_back(v, grad):
    r = inverse_rms(v)
    return r * grad - v * (r * r * r) * jnp.mean(grad * v, axis=-1, keepdims=True)


def renew(weight, moment, average, grad, fan, tokens):
    step = 0.4 / math.sqrt(fan * tokens)
    moment_new = MU * moment + grad
    weight_new = weight - step * (grad + MU * moment_new)
    average_new = BETA * average + (1.0 - BETA) * weight_new
    return (moment_new, weight_new, average_new)


ROWS = 256
HALF = 4
SUB = 2
STEPS = HALF // SUB
TALL = SUB * ROWS
HD = 128
VMEM = 56 * 1024 * 1024
EXTRA = 128


def pin(v):
    return with_layout_constraint(v, Layout(major_to_minor=tuple(range(v.ndim))))


def after(value, *done):
    return lax.optimization_barrier((value,) + done)[0]


class Clock:
    def __init__(self):
        self.token = jnp.zeros((8, 128), F32)

    def now(self, *values):
        out = [lax.optimization_barrier((v, self.token))[0] for v in values]
        return out if len(out) > 1 else out[0]

    def end(self, *done):
        self.token = lax.optimization_barrier((self.token,) + done)[0]


def block_spec(shape):
    return pl.BlockSpec(shape, lambda i: (i,) + (0,) * (len(shape) - 1))


def whole_spec(a):
    return pl.BlockSpec(a.shape, lambda i: (0,) * a.ndim, pipeline_mode=pl.Buffered(1))


def scalar_spec():
    return pl.BlockSpec(memory_space=pltpu.SMEM)


def call(kernel, steps, ins, outs, flops):
    moved = sum(a.size * a.dtype.itemsize for a, _ in ins)
    moved += sum(math.prod(s) * jnp.dtype(d).itemsize for s, d, _ in outs)
    return pl.pallas_call(
        kernel,
        grid=(steps,),
        in_specs=[s for _, s in ins],
        out_specs=[b if isinstance(b, pl.BlockSpec) else block_spec(b) for _, _, b in outs],
        out_shape=[jax.ShapeDtypeStruct(s, d) for s, d, _ in outs],
        compiler_params=pltpu.CompilerParams(
            vmem_limit_bytes=VMEM, dimension_semantics=("arbitrary",)
        ),
        cost_estimate=pl.CostEstimate(
            flops=int(flops), bytes_accessed=int(moved), transcendentals=0
        ),
    )(*[a for a, _ in ins])


NT = ((1,), (1,))
TN = ((0,), (0,))


def mask_of(fade, seg_c, seg_r):
    return jnp.where(seg_c == seg_r, fade, 0.0)


def pair_spec(shape, late):
    if late:
        return pl.BlockSpec(shape, lambda i: (jnp.maximum(i - STEPS, 0),) + (0,) * (len(shape) - 1))
    return pl.BlockSpec(shape, lambda i: (jnp.minimum(i, STEPS - 1),) + (0,) * (len(shape) - 1))


def half_spec(shape, h):
    return pl.BlockSpec(shape, lambda i: (i + h * STEPS,) + (0,) * (len(shape) - 1))


def project(n1, w_in, at):
    own = at.own
    cols = own * HD
    parts = len(w_in)
    width = n1[0].shape[1]
    deep = width // parts

    def kernel(*refs):
        a_ref, b_ref, w_refs = refs[0], refs[1], refs[2 : 2 + parts]
        seg_ref, ramp_ref, last_ref, reach_ref = refs[2 + parts : 6 + parts]
        raw_ref, gate_ref, qkv_ref, term_ref, leaving_ref = refs[6 + parts :]
        i = pl.program_id(0)
        pre = None
        for k in range(parts):
            some = slice(k * deep, (k + 1) * deep)
            x = jnp.where(i < STEPS, a_ref[:, some], b_ref[:, some])
            new = dot(x, w_refs[k][...])
            pre = new if pre is None else pre + new
        pq, pk, pv = pre[:, :cols], pre[:, cols : 2 * cols], pre[:, 2 * cols : 3 * cols]
        raw_ref[...] = pre[:, : 2 * cols]
        gate_ref[...] = pre[:, 3 * cols :]
        key = (pk * jax.nn.sigmoid(pk)).astype(BF)
        value = pv.astype(BF)
        qkv_ref[:, :cols] = (pq * jax.nn.sigmoid(pq)).astype(BF)
        qkv_ref[:, cols : 2 * cols] = key
        qkv_ref[:, 2 * cols :] = value

        @pl.when(i == 0)
        def _():
            leaving_ref[...] = jnp.zeros_like(leaving_ref)

        for s in range(SUB):
            b = i * SUB + s
            block = slice(s * ROWS, (s + 1) * ROWS)
            for j in range(own):
                ramp = ramp_ref[:, own + j : own + j + 1]
                leave = jnp.where(seg_ref[s] == last_ref[b], ramp, 0.0)
                head = slice(j * HD, (j + 1) * HD)
                scaled = (key[block, head].astype(F32) * leave).astype(BF)
                term = dot(scaled, value[block, head], TN)
                term_ref[s, j] = term
                leaving_ref[j] += reach_ref[j, b] * term

    some = pl.BlockSpec((deep, 4 * cols), lambda i: (0, 0), pipeline_mode=pl.Buffered(1))
    ins = [(v, pair_spec((TALL, width), late)) for late, v in enumerate(n1)]
    ins += [(w, some) for w in w_in]
    ins += [(at.cols, block_spec((SUB, ROWS, 1))), (at.ramps, whole_spec(at.ramps))]
    ins += [(v, scalar_spec()) for v in (at.last, at.out_reach)]
    n = 2 * HALF
    outs = [
        ((n * ROWS, 2 * cols), F32, (TALL, 2 * cols)),
        ((n * ROWS, cols), F32, (TALL, cols)),
        ((n * ROWS, 3 * cols), BF, (TALL, 3 * cols)),
        ((n, own, HD, HD), F32, (SUB, own, HD, HD)),
        ((own, HD, HD), F32, pl.BlockSpec((own, HD, HD), lambda i: (0, 0, 0))),
    ]
    return call(kernel, 2 * STEPS, ins, outs, 4 * n1[0].size * 4 * cols)


def combine(weights, terms, more, reach):
    state = reach * more
    for c in range(2 * HALF):
        state = state + weights(c) * terms(c)
    return state


def attend(h, qkv, gate, term, entering, w_out, at):
    own = at.own
    cols = own * HD
    width = w_out.shape[1]

    def kernel(
        qkv_ref, gate_ref, term_ref, more_ref, w_ref, sc_ref, sr_ref, fade_ref, ramp_ref,
        prev_ref, inner_ref, reach_ref, attn_ref, branch_ref, state_ref,
    ):
        for s, j in ((s, j) for s in range(SUB) for j in range(own)):
            i = (pl.program_id(0) + h * STEPS) * SUB + s
            block = slice(s * ROWS, (s + 1) * ROWS)
            head = slice(j * HD, (j + 1) * HD)
            q = qkv_ref[block, j * HD : (j + 1) * HD]
            k = qkv_ref[block, cols + j * HD : cols + (j + 1) * HD]
            v = qkv_ref[block, 2 * cols + j * HD : 2 * cols + (j + 1) * HD]
            state = combine(
                lambda c: inner_ref[j, i * 2 * HALF + c],
                lambda c: term_ref[c, j],
                more_ref[j],
                reach_ref[j, i],
            ).astype(BF)
            state_ref[s, j] = state
            enter = jnp.where(sc_ref[s] == prev_ref[i], ramp_ref[:, j : j + 1], 0.0)
            weights = (dot(q, k, NT) * mask_of(fade_ref[j], sc_ref[s], sr_ref[s])).astype(BF)
            attn_ref[block, head] = dot(weights, v) + enter * dot(q, state)
        attn = attn_ref[...]
        branch_ref[:, :width] = dot((attn * gate_ref[...]).astype(BF), w_ref[...]).astype(BF)
        rest = jnp.sum(attn * attn, axis=1, keepdims=True)
        branch_ref[:, width:] = strip_of([rest])

    n = HALF
    ins = [
        (qkv, half_spec((TALL, 3 * cols), h)),
        (gate, half_spec((TALL, cols), h)),
        (term, whole_spec(term)),
        (entering, whole_spec(entering)),
        (w_out, whole_spec(w_out)),
        (at.cols, half_spec((SUB, ROWS, 1), h)),
        (at.rows, half_spec((SUB, 1, ROWS), h)),
        (at.fade, whole_spec(at.fade)),
        (at.ramps, whole_spec(at.ramps)),
    ] + [(v, scalar_spec()) for v in (at.prev, at.inner, at.in_reach)]
    outs = [
        ((n * ROWS, cols), F32, (TALL, cols)),
        ((n * ROWS, width + EXTRA), BF, (TALL, width + EXTRA)),
        ((n, own, HD, HD), BF, (SUB, own, HD, HD)),
    ]
    return call(kernel, STEPS, ins, outs, 2 * n * ROWS * cols * (width + 2 * ROWS))


def sglu_rows(n2, g, w_pair, w_third):
    parts = len(w_pair)
    _, hidden, deep = w_pair[0].shape
    block = 2 * ROWS

    def kernel(*refs):
        x_ref, g_ref = refs[:2]
        both, three = (refs[2 + k * parts : 2 + (k + 1) * parts] for k in range(2))
        prod_ref, prod_t, gf_t, gs_t, back_ref = refs[2 + 2 * parts :]
        first = second = grad = None
        for k in range(parts):
            at = slice(k * deep, (k + 1) * deep)
            x, gk = x_ref[:, at], g_ref[:, at]
            a, b, c = dot(x, both[k][0], NT), dot(x, both[k][1], NT), dot(gk, three[k][...], NT)
            first = a if first is None else first + a
            second = b if second is None else second + b
            grad = c if grad is None else grad + c
        prod = (first * second).astype(BF)
        gf = (grad * second).astype(BF)
        gs = (grad * first).astype(BF)
        prod_ref[...] = prod
        prod_t[...] = prod.T
        gf_t[...] = gf.T
        gs_t[...] = gs.T
        for k in range(parts):
            at = slice(k * deep, (k + 1) * deep)
            back_ref[:, at] = (dot(gf, both[k][0]) + dot(gs, both[k][1])).astype(BF)

    n = n2.shape[0] // block
    width = n2.shape[1]
    ins = [(n2, block_spec((block, width))), (g, block_spec((block, width)))]
    ins += [(w, whole_spec(w)) for w in w_pair + w_third]
    outs = [((n * block, hidden), BF, (block, hidden))]
    turned = pl.BlockSpec((hidden, block), lambda i: (0, i))
    outs += [((hidden, n * block), BF, turned)] * 3
    outs += [((n * block, width), BF, (block, width))]
    return call(kernel, n, ins, outs, 10 * n2.size * hidden)


def sglu_last(product, w_third):
    parts = len(w_third)
    deep = w_third[0].shape[1]
    block = 2 * ROWS

    def kernel(*refs):
        for k in range(parts):
            refs[-1][:, k * deep : (k + 1) * deep] = dot(refs[0][...], refs[1 + k][...]).astype(BF)

    n, width = product.shape[0] // block, parts * deep
    ins = [(product, block_spec((block, product.shape[1])))]
    ins += [(w, whole_spec(w)) for w in w_third]
    return call(
        kernel, n, ins, [((n * block, width), BF, (block, width))], 2 * product.size * width
    )[0]


def attend_back_rows(gb, w_out, attn, gate, qkv, at):
    own = at.own
    cols = own * HD
    width = w_out.shape[1]

    def kernel(
        gb_a, gb_b, w_ref, attn_a, attn_b, gate_ref, qkv_ref, sc_ref, ramp_ref, prev_ref, reach_ref,
        ga_ref, gg_ref, mixed_ref, term_ref, leaving_ref,
    ):
        i = pl.program_id(0)
        early = i < STEPS
        extra = jnp.where(early, gb_a[:, width:], gb_b[:, width:]).astype(F32)
        r = extra[:, 0:1] + extra[:, 1:2] + extra[:, 2:3]
        pull = extra[:, 3:4] + extra[:, 4:5] + extra[:, 5:6]
        gm = dot(jnp.where(early, gb_a[:, :width], gb_b[:, :width]), w_ref[...], NT)
        attn, gate = jnp.where(early, attn_a[...], attn_b[...]), gate_ref[...]
        normed = r * attn
        gg_ref[...] = (gm * normed).astype(BF)
        mixed_ref[...] = (normed * gate).astype(BF)
        ga = (r * (gm * gate) - attn * pull).astype(BF)
        ga_ref[...] = ga

        @pl.when(i == 0)
        def _():
            leaving_ref[...] = jnp.zeros_like(leaving_ref)

        for s, j in ((s, j) for s in range(SUB) for j in range(own)):
            b = i * SUB + s
            block = slice(s * ROWS, (s + 1) * ROWS)
            enter = jnp.where(sc_ref[s] == prev_ref[b], ramp_ref[:, j : j + 1], 0.0)
            q = qkv_ref[block, j * HD : (j + 1) * HD].astype(F32)
            term = dot((q * enter).astype(BF), ga[block, j * HD : (j + 1) * HD], TN)
            term_ref[s, j] = term
            leaving_ref[j] += reach_ref[j, b] * term

    n = 2 * HALF
    ins = [(v, pair_spec((TALL, v.shape[1]), late)) for late, v in enumerate(gb)]
    ins += [(w_out, whole_spec(w_out))]
    ins += [(v, pair_spec((TALL, cols), late)) for late, v in enumerate(attn)]
    ins += [
        (gate, block_spec((TALL, cols))),
        (qkv, block_spec((TALL, 3 * cols))),
        (at.cols, block_spec((SUB, ROWS, 1))),
        (at.ramps, whole_spec(at.ramps)),
    ] + [(v, scalar_spec()) for v in (at.prev, at.in_reach)]
    outs = [((n * ROWS, cols), BF, (TALL, cols))] * 3
    outs += [((n, own, HD, HD), F32, (SUB, own, HD, HD))]
    outs += [((own, HD, HD), F32, pl.BlockSpec((own, HD, HD), lambda i: (0, 0, 0)))]
    return call(kernel, 2 * STEPS, ins, outs, 2 * n * ROWS * cols * width)


def project_back(h, qkv, raw, ga, gg, state, term, entering, w_in, width, at):
    own = at.own
    cols = own * HD
    parts = len(w_in)
    deep = width // parts

    def kernel(*refs):
        qkv_ref, raw_ref, ga_ref, gg_ref, state_ref, term_ref, more_ref = refs[:7]
        w_refs = refs[7 : 7 + parts]
        sc_ref, sr_ref, fade_ref, ramp_ref = refs[7 + parts : 11 + parts]
        prev_ref, last_ref, inner_ref, reach_ref, gp_ref, back_ref = refs[11 + parts :]
        for s, j in ((s, j) for s in range(SUB) for j in range(own)):
            i = (pl.program_id(0) + h * STEPS) * SUB + s
            block = slice(s * ROWS, (s + 1) * ROWS)
            head = slice(j * HD, (j + 1) * HD)
            kt = slice(cols + j * HD, cols + (j + 1) * HD)
            vt = slice(2 * cols + j * HD, 2 * cols + (j + 1) * HD)
            q, k, v = qkv_ref[block, head], qkv_ref[block, kt], qkv_ref[block, vt]
            g = ga_ref[block, head]
            mask = mask_of(fade_ref[j], sc_ref[s], sr_ref[s])
            enter = jnp.where(sc_ref[s] == prev_ref[i], ramp_ref[:, j : j + 1], 0.0)
            leave = jnp.where(sc_ref[s] == last_ref[i], ramp_ref[:, own + j : own + j + 1], 0.0)
            later = combine(
                lambda c: inner_ref[j, c * 2 * HALF + i],
                lambda c: term_ref[c, j],
                more_ref[j],
                reach_ref[j, i],
            ).astype(BF)
            weights = (dot(q, k, NT) * mask).astype(BF)
            gs = (dot(g, v, NT) * mask).astype(BF)
            gq = dot(gs, k) + enter * dot(g, state_ref[s, j], NT)
            gk = dot(gs, q, TN) + leave * dot(v, later, NT)
            gv = dot(weights, g, TN) + leave * dot(k, later)
            rq, rk = raw_ref[block, head], raw_ref[block, kt]
            sq, sk = jax.nn.sigmoid(rq), jax.nn.sigmoid(rk)
            gp_ref[block, head] = (gq * (sq * (1.0 + rq * (1.0 - sq)))).astype(BF)
            gp_ref[block, kt] = (gk * (sk * (1.0 + rk * (1.0 - sk)))).astype(BF)
            gp_ref[block, vt] = gv.astype(BF)
        gp_ref[:, 3 * cols :] = gg_ref[...]
        for k in range(parts):
            some = slice(k * deep, (k + 1) * deep)
            back_ref[:, some] = dot(gp_ref[...], w_refs[k][...], NT).astype(BF)

    n = HALF
    some = pl.BlockSpec((deep, 4 * cols), lambda i: (0, 0), pipeline_mode=pl.Buffered(1))
    ins = [
        (qkv, half_spec((TALL, 3 * cols), h)),
        (raw, half_spec((TALL, 2 * cols), h)),
        (ga, half_spec((TALL, cols), h)),
        (gg, half_spec((TALL, cols), h)),
        (state, block_spec((SUB, own, HD, HD))),
        (term, whole_spec(term)),
        (entering, whole_spec(entering)),
    ] + [(w, some) for w in w_in]
    ins += [
        (at.cols, half_spec((SUB, ROWS, 1), h)),
        (at.rows, half_spec((SUB, 1, ROWS), h)),
        (at.fade, whole_spec(at.fade)),
        (at.ramps, whole_spec(at.ramps)),
    ]
    ins += [(v, scalar_spec()) for v in (at.prev, at.last, at.inner, at.out_reach)]
    outs = [
        ((n * ROWS, 4 * cols), BF, (TALL, 4 * cols)),
        ((n * ROWS, width), BF, (TALL, width)),
    ]
    return call(kernel, STEPS, ins, outs, 2 * n * ROWS * 4 * cols * width)


def one_by_one(count, shape):
    spec = pl.BlockSpec(shape, lambda i: (0,) * len(shape), pipeline_mode=pl.Buffered(1))
    return [(shape, BF, spec) for _ in range(count)]


def grads_by_left(left, right, n, below=None):
    cut, cols = left[0].shape[1] // n, right[0].shape[1]
    more = 0 if below is None else 2 * below[0].shape[1]

    def kernel(*refs):
        l0, l1, r0, r1 = refs[:4]
        outs = refs[len(refs) - n :]
        grad = (dot(l0[...], r0[...], TN) + dot(l1[...], r1[...], TN)).astype(BF)
        for k in range(n):

            @pl.when(pl.program_id(0) == k)
            def _():
                outs[k][:cut] = grad
                if more:
                    a_ref, b_ref, from_a, row = refs[4:8]
                    part = jnp.where(from_a[k] == 1, a_ref[row[k]], b_ref[row[k]])
                    outs[k][cut : cut + more // 2] = part[:, :cols]
                    outs[k][cut + more // 2 :] = part[:, cols:]

    ins = [(a, pl.BlockSpec((a.shape[0], cut), lambda i: (0, i))) for a in left]
    ins += [(a, whole_spec(a)) for a in right]
    if more:
        ins += [(a, whole_spec(a)) for a in below[:2]] + [(a, scalar_spec()) for a in below[2:]]
    outs = one_by_one(n, (cut + more, cols))
    return call(kernel, n, ins, outs, 4 * left[0].size * cols)


def grads_by_right(lefts, right, cut, first, n, step=1):
    count = len(lefts)
    tall = lefts[0][0].shape[0]

    def kernel(*refs):
        r0, r1 = refs[2 * count : 2 * count + 2]
        outs = refs[2 * count + 2 :]
        for m in range(count):
            l0, l1 = refs[2 * m : 2 * m + 2]
            grad = (dot(l0[...], r0[...]) + dot(l1[...], r1[...])).astype(BF)
            for k in range(n):

                @pl.when(pl.program_id(0) == k)
                def _():
                    outs[k][m] = grad

    ins = [(a, whole_spec(a)) for left in lefts for a in left]
    ins += [(a, pl.BlockSpec((a.shape[0], cut), lambda i: (0, first + step * i))) for a in right]
    outs = one_by_one(n, (count, tall, cut))
    return call(kernel, n, ins, outs, 4 * count * right[0].size * tall)


def grads_out(left, right, width):
    def kernel(l0, l1, r0, r1, out):
        out[...] = (dot(l0[...], r0[...], TN) + dot(l1[...], r1[...], TN)).astype(BF)

    cut, (rows, tall) = width // 4, left.shape
    spec = lambda rows: pl.BlockSpec((rows, cut), lambda i: (0, i))
    half = lambda k: pl.BlockSpec((rows // 2, tall), lambda i: (k, 0))
    ins = [(left, half(k)) for k in (0, 1)] + [(a, spec(a.shape[0])) for a in right]
    return call(kernel, 4, ins, [((tall, width), BF, spec(tall))], 2 * left.size * width)[0]


def add_strips(width, *parts):
    total = parts[0][:, :width].astype(F32)
    for p in parts[1:]:
        total = total + p[:, :width].astype(F32)
    out = [total.astype(BF)]
    if parts[0].shape[1] > width:
        rest = 0.0
        for p in parts:
            for n in range(3):
                rest = rest + p[:, width + n : width + n + 1].astype(F32)
        lane = lax.broadcasted_iota(jnp.int32, (total.shape[0], EXTRA), 1)
        strip = jnp.zeros((total.shape[0], EXTRA), F32)
        for n in range(3):
            top = rest.astype(BF).astype(F32)
            strip = jnp.where(lane == n, top, strip)
            rest = rest - top
        out.append(strip.astype(BF))
    return out


def add_last(a, b, width):
    n, wide = a.shape[0] // ROWS, a.shape[1]
    half = ROWS // 2

    def kernel(a_ref, b_ref, low_ref, high_ref):
        parts = add_strips(width, a_ref[...], b_ref[...])
        for v, at in zip(parts, (slice(0, width), slice(width, wide))):
            low_ref[:, at] = v[:half]
            high_ref[:, at] = v[half:]

    block = pl.BlockSpec((ROWS, wide), lambda i: (n - 1, 0))
    one = pl.BlockSpec((half, wide), lambda i: (0, 0))
    return call(kernel, 1, [(a, block), (b, block)], [((half, wide), BF, one)] * 2, ROWS * wide)


def add_halves(a, b, u, v, width):
    wide = a.shape[1]
    half = ROWS // 2

    def kernel(a2, a4, b2, b4, u_ref, v_ref, to_2, to_4):
        low, high = slice(0, half), slice(half, ROWS)
        for out, rows, terms in (
            (to_2, low, (a2[low], b2[low])),
            (to_2, high, (a2[high], b2[high], v_ref[...])),
            (to_4, low, (a4[low], b4[low], u_ref[...])),
            (to_4, high, (a4[high], b4[high])),
        ):
            parts = add_strips(width, *terms)
            for p, at in zip(parts, (slice(0, width), slice(width, wide))):
                out[rows, at] = p

    spec = lambda k: pl.BlockSpec((ROWS, wide), lambda i: (k, 0))
    ins = [(t, spec(k)) for t in (a, b) for k in (1, 2)] + [(u, whole_spec(u)), (v, whole_spec(v))]
    return call(kernel, 1, ins, [((ROWS, wide), BF, spec(0))] * 2, ROWS * wide)


def strip_of(column):
    lane = lax.broadcasted_iota(jnp.int32, (column[0].shape[0], EXTRA), 1)
    strip = jnp.zeros(lane.shape, F32)
    for m, rest in enumerate(column):
        for n in range(3):
            top = rest.astype(BF).astype(F32)
            strip = jnp.where(lane == 3 * m + n, top, strip)
            rest = rest - top
    return strip.astype(BF)


def mid_rows(sums, inputs, dest):
    width = inputs.shape[1]
    cut = width // 4
    block = ROWS // 2

    def kernel(a, b, c, d, x_ref, dest_ref, mid_ref, branch_ref, scale_ref, norm_ref):
        branch = square = None
        for ref in (a, b, c, d):
            part = ref[:, :width].astype(F32)
            extra = ref[:, width:].astype(F32)
            more = extra[:, 0:1] + extra[:, 1:2] + extra[:, 2:3]
            branch = part if branch is None else branch + part
            square = more if square is None else square + more
        r = lax.rsqrt(square / width + EPS)
        mid = x_ref[...].astype(F32) + r * branch
        branch_ref[...] = branch.astype(BF)
        scale_ref[...] = jnp.broadcast_to(r, (block, EXTRA))
        mid_ref[...] = mid
        norm = (mid * inverse_rms(mid)).astype(BF)
        for p in range(4):
            to = pl.ds(pl.multiple_of(dest_ref[p] * cut, cut), cut)
            norm_ref[:, to] = norm[:, p * cut : (p + 1) * cut]

    ins = [(v, block_spec((block, width + EXTRA))) for v in sums]
    ins += [(inputs, block_spec((block, width))), (dest, scalar_spec())]
    outs = [
        ((ROWS, width), F32, (block, width)),
        ((ROWS, width), BF, (block, width)),
        ((ROWS, EXTRA), F32, (block, EXTRA)),
        ((ROWS, width), BF, (block, width)),
    ]
    return call(kernel, 2, ins, outs, 20 * ROWS * width)


def mid_back_rows(sums, out_grad, mid, branch, scale, dest):
    width = mid.shape[1]
    cut = width // 4
    block = ROWS // 2

    def kernel(a, b, c, d, g_ref, mid_ref, branch_ref, scale_ref, dest_ref, grad_ref, out_ref):
        parts = []
        for p in range(4):
            at = pl.ds(pl.multiple_of(dest_ref[p] * cut, cut), cut)
            part = a[:, at].astype(F32)
            for ref in (b, c, d):
                part = part + ref[:, at].astype(F32)
            parts.append(part)
        grad = g_ref[...].astype(F32) + srms_back(mid_ref[...], jnp.concatenate(parts, axis=1))
        grad_ref[...] = grad
        low = grad.astype(BF)
        out_ref[:, :width] = low
        inward = low.astype(F32) * branch_ref[...].astype(F32)
        inward = jnp.mean(inward, axis=1, keepdims=True)
        r = scale_ref[:, 0:1]
        out_ref[:, width:] = strip_of([r, r * r * r * inward])

    ins = [(v, block_spec((block, width))) for v in (*sums, out_grad, mid, branch)]
    ins += [(scale, block_spec((block, EXTRA))), (dest, scalar_spec())]
    outs = [
        ((ROWS, width), F32, (block, width)),
        ((ROWS, width + EXTRA), BF, (block, width + EXTRA)),
    ]
    return call(kernel, 2, ins, outs, 20 * ROWS * width)


def renew_turned(grad, weight, moment, average, fan, tokens):
    few, total = weight.shape
    block = 32

    def kernel(g_ref, w_ref, m_ref, a_ref, m_new, w_new, a_new):
        for p in range(8):
            for t in range(4):
                for j in range(2):
                    col = t * (total // 4) + (8 * (p % 2) + 4 * j + p // 2) * HD
                    to = slice(col, col + HD)
                    at = slice((2 * t + j) * HD, (2 * t + j + 1) * HD)
                    new = renew(
                        w_ref[:, to], m_ref[:, to], a_ref[:, to], g_ref[p, :, at].astype(F32),
                        fan, tokens,
                    )
                    m_new[:, to], w_new[:, to], a_new[:, to] = new

    ins = [(grad, pl.BlockSpec((8, block, grad.shape[2]), lambda i: (0, i, 0)))]
    ins += [(v, block_spec((block, total))) for v in (weight, moment, average)]
    outs = [((few, total), F32, (block, total))] * 3
    return call(kernel, few // block, ins, outs, 10 * weight.size)


def cut4(v, axis):
    n = v.shape[axis] // 4
    return [lax.slice_in_dim(v, k * n, (k + 1) * n, axis=axis) for k in range(4)]


def strip_sum(v):
    strip = v[:, v.shape[1] - EXTRA :].astype(F32)
    return strip[:, 0:1] + strip[:, 1:2] + strip[:, 2:3]


def pieces(v):
    out = []
    for _ in range(3):
        top = lax.reduce_precision(v, 8, 7)
        out.append(top.astype(BF))
        v = v - top
    return out


class Places:
    def __init__(self, plan, seq_lengths, decay_rate, rows):
        size = plan.size
        group_rows = size * rows
        tokens = group_rows * plan.groups
        ends = jnp.cumsum(seq_lengths)

        def seg_at(place):
            mark = jnp.sum((place[..., None] >= ends).astype(jnp.int32), axis=-1)
            return jnp.where(place < 0, -1, mark)

        first_block = plan.group * size
        blocks = first_block + plan.slot_ids
        seg = seg_at(blocks[:, None] * rows + jnp.arange(rows, dtype=jnp.int32)[None, :])
        prev = seg_at(blocks * rows - 1)
        last = seg[:, rows - 1]
        head_ids = plan.head_ids if hasattr(plan, "head_ids") else plan.own * plan.p + jnp.arange(plan.own)
        rate = jnp.take(decay_rate, head_ids)

        def reach(gap, same):
            return jnp.where(
                same & (gap >= 0), jnp.exp(-rate[:, None, None] * (rows * jnp.maximum(gap, 0))), 0.0
            )

        inner = reach(
            (blocks[:, None] - blocks[None, :] - 1).astype(F32)[None],
            (prev[:, None] == last[None, :])[None],
        )
        border = seg_at((first_block + size) * rows - 1)
        out_reach = reach(
            (first_block + size - 1 - blocks).astype(F32)[None, None], (last == border)[None, None]
        )[:, 0]
        entry = seg_at(first_block * rows - 1)
        in_reach = reach((blocks - first_block).astype(F32)[None, None], (prev == entry)[None, None])[
            :, 0
        ]
        longest = tokens // 4
        hops = min(-(-longest // group_rows), plan.groups - 1)

        def hop_factor(j, ahead):
            if ahead:
                here, there = border, seg_at((first_block + j * size) * rows - 1)
            else:
                here, there = entry, seg_at((first_block - (j - 1) * size) * rows - 1)
            return jnp.where(here == there, jnp.exp(-rate * ((j - 1) * group_rows)), 0.0)

        def bring(total, ahead):
            n = plan.groups
            got = jnp.zeros_like(total)
            for j in range(1, hops + 1):
                pairs = [(i + j, i) if ahead else (i, i + j) for i in range(n - j)]
                part = lax.ppermute(total, plan.fs, pairs)
                got = got + hop_factor(j, ahead)[:, None, None] * part
            return got

        self.bring, self.hop = bring, hop_factor
        self.inner = inner.reshape(inner.shape[0], -1)
        self.out_reach, self.in_reach = out_reach, in_reach
        self.own = plan.own
        self.cols, self.rows = seg[:, :, None], seg[:, None, :]
        self.prev, self.last = prev, last
        step = jnp.arange(rows).astype(F32)
        spread = step[:, None] - step[None, :]
        fade = jnp.exp(-rate[:, None, None] * jnp.maximum(spread, 0.0)[None])
        self.fade = jnp.where((spread >= 0)[None], fade, 0.0)
        ramps = [jnp.exp(-rate[None] * step[:, None]), jnp.exp(-rate[None] * (rows - step)[:, None])]
        blank = jnp.zeros((rows, EXTRA - 2 * plan.own), F32)
        self.ramps = jnp.concatenate(ramps + [blank], axis=1)


class Square:
    def __init__(self):
        self.tp = ("y", "x", "c")
        self.fs = ("z",)
        self.size = 8
        self.groups = 4

    def begin(self):
        self.z = lax.axis_index("z")
        self.y = lax.axis_index("y")
        self.c = lax.axis_index("c")
        self.p = lax.axis_index(self.tp)
        self.q = self.p // 2
        self.group = self.z
        self.slot_ids = self.p ^ jnp.array(XORS, jnp.int32)
        self.head_ids = 8 * self.c + 4 * jnp.arange(2) + self.q
        self.order = jnp.array(MEETS, jnp.int32)[self.z]
        self.dest = jnp.array(PLACES, jnp.int32)[self.z]

    def turn(self, v, places):
        wide = v.shape[1] // 4
        return jnp.concatenate(
            [lax.dynamic_slice_in_dim(v, places[k] * wide, wide, axis=1) for k in range(4)], axis=1
        )

    def slots(self, own, one, two, three):
        outer = (self.z == 0) | (self.z == 3)
        return [
            own,
            one[0],
            pin(jnp.where(outer, two[0], one[1])),
            pin(jnp.where(outer, three, two[1])),
        ]

    def by_y(self, mine, got, axis):
        first = self.y == 0
        parts = [jnp.where(first, mine, got), jnp.where(first, got, mine)]
        return pin(jnp.concatenate(parts, axis=axis))

    def of_y(self, one, two):
        first = self.y == 0
        return pin(jnp.where(first, one, two)), pin(jnp.where(first, two, one))


def over(axis, pairs=SWAP):
    return lambda v: pin(lax.ppermute(pin(v), axis, pairs))


to_x, to_y, to_core = over("x"), over("y"), over("c")


to_pair = over("z", [(0, 1), (1, 0), (2, 3), (3, 2)])
to_middle = over("z", [(1, 2), (2, 1)])
outward = over("z", [(1, 0), (2, 3)])
inward_z = over("z", [(0, 1), (3, 2)])


def spread0(own):
    return to_pair(own), to_middle(own)


def spread1(one):
    return outward(one[1]), to_middle(one[0])


def spread2(two):
    return outward(two[1])


def gather1(g):
    return inward_z(g[3])


def gather2(g2, third):
    return inward_z(g2), to_middle(third)


def gather3(first, second):
    return to_pair(first), to_middle(second)


def plus(a, b):
    return (a.astype(F32) + b.astype(F32)).astype(BF)


def square_layer(plan, places, lengths, inputs, out_grad, attn_in, attn_out, sglu_in, sglu_out):
    rows, width = inputs.shape
    h2 = rows // 2
    cut = width // 4
    clock = Clock()
    now, end = clock.now, clock.end

    order, dest = plan.order, plan.dest

    def pick(stack, place):
        return lax.dynamic_index_in_dim(stack, place, 0, False)

    xf = inputs.astype(F32)
    n1 = pin(plan.turn((xf * inverse_rms(xf)).astype(BF), order))
    og = pin(plan.turn(out_grad, order))
    few = attn_in.shape[0]
    view = attn_in.astype(BF).reshape(few, 4, 2, 2, 4, HD).transpose(4, 2, 0, 1, 3, 5)
    own_in = lax.all_to_all(view.reshape(8, few, -1), plan.tp, 0, 0, tiled=True)
    own_in = own_in.reshape(8 * few, -1)
    deep, across = own_in.shape
    own_out = attn_out.astype(BF)
    own_w = pin(jnp.concatenate([own_in, own_out[:, :across], own_out[:, across:]]))
    end(own_w, n1, og)

    a_w, a_n1 = now(own_w, n1)
    w1 = spread0(a_w)
    nx, ny = to_x(a_n1), to_y(a_n1)
    at = places(now(lengths))
    hid = sglu_in.shape[2] // 2
    three = pin(now(sglu_in).astype(BF)).swapaxes(1, 2)
    three = jnp.concatenate([three, sglu_out.astype(BF)[None]])
    my_three, to_three = plan.of_y(three[:, :hid], three[:, hid:])
    tables = [at.cols, at.rows, at.prev, at.last, at.fade, at.ramps]
    tables += [at.inner, at.out_reach, at.in_reach, at.hop(1, False), at.hop(1, True)]
    end(*w1, nx, ny, my_three, to_three, *tables)

    w2 = spread1(now(*w1))
    ax, ay = now(nx, ny)
    nd = to_x(ay[:h2]), to_y(ax[h2:])
    end(*w2, *nd)

    w3 = spread2(now(*w2))
    a_og, a_three = now(og, to_three)
    gx = to_x(a_og)
    got = to_y(a_three)
    n1_a = pin(jnp.concatenate([n1, nx, ny, *now(*nd)]))
    norm1 = n1_a, to_core(n1_a)
    own_three = plan.by_y(my_three, got, 2)
    own_pair, own_third = pin(own_three[:2]), pin(own_three[2])
    end(w3, gx, *norm1, own_pair, own_third)

    pair1 = spread0(now(own_pair))
    gy = to_y(now(og))
    w_in = plan.slots(own_w, now(*w1), now(*w2), now(w3))
    outs = jnp.stack([w[deep:] for w in w_in])
    w_mine = [pick(outs, dest[2 * plan.c + j]) for j in (0, 1)]
    w_got = to_core(jnp.concatenate([pick(outs, dest[2 * (1 - plan.c) + j]) for j in (0, 1)]))
    core0 = plan.c == 0
    raw, gate, qkv, term, leaving = project((now(norm1[0]), norm1[1]), w_in, at)
    end(*pair1, gy, w_got, leaving)

    w_rows = []
    for j in (0, 1):
        got = w_got[j * 2 * few : (j + 1) * 2 * few]
        for half in (jnp.where(core0, w_mine[j], got), jnp.where(core0, got, w_mine[j])):
            w_rows.append(jnp.concatenate([half[:few], half[few:]], axis=1))
    w_out = pin(jnp.concatenate(w_rows))
    entering = at.bring(now(leaving), False)
    attn_b, give, state_b = attend(1, qkv, gate, term, entering, w_out, at)
    end(give)

    third1 = spread0(now(own_third))
    a_qkv, give = now(qkv, give)
    attn_a, keep, state_a = attend(0, a_qkv, gate, term, entering, w_out, at)
    got = to_core(give)
    a_gx, a_gy = now(gx, gy)
    gd = to_x(a_gy[:h2]), to_y(a_gx[h2:])
    end(*third1, got, keep, *gd)

    def first_step(keep, got):
        low, high = add_last(keep, got, width)
        return to_x(low), to_y(high)

    def total(*parts):
        out = parts[0].astype(F32)
        for p in parts[1:]:
            out = out + p.astype(F32)
        return out

    keep, got = now(keep, got)
    u, v = first_step(keep, got)
    third2 = spread1(now(*third1))
    g_a = pin(jnp.concatenate([og, gx, gy, *now(*gd)]))
    end(u, v, *third2, g_a)

    to_2, to_4 = add_halves(keep, got, *now(u, v), width)
    sx, sy = to_x(to_2), to_y(to_4)
    pair2 = spread1(now(*pair1))
    g_b = to_core(now(g_a))
    end(sx, sy, *pair2, g_b)

    pair3 = spread2(now(*pair2))
    mid, branch, r_attn, n2 = mid_rows((keep, got, *now(sx, sy)), inputs, dest)
    mx, my, mc = to_x(n2), to_y(n2), to_core(n2)
    end(mx, my, mc, pair3)

    third3 = spread2(now(*third2))
    ax, ay = now(mx, my)
    md = to_x(ay[:h2]), to_y(ax[h2:])
    mxyc = to_core(jnp.concatenate([ax, ay]))
    mdc = to_core(jnp.concatenate(md))
    n2_a = pin(jnp.concatenate([n2, mx, my, *md]))
    n2_b = pin(jnp.concatenate([mc, mxyc, mdc]))
    w_pair = plan.slots(own_pair, now(*pair1), now(*pair2), now(pair3))
    end(third3, n2_a, n2_b, *w_pair)

    w_third = plan.slots(own_third, now(*third1), now(*third2), now(third3))
    prod_b, turned_b, gf_b, gs_b, give = sglu_rows(n2_b, g_b, w_pair, w_third)
    end(give)

    give, a_n2 = now(give, n2_a)
    got = to_core(give)
    prod_a, turned_a, gf_a, gs_a, keep = sglu_rows(a_n2, g_a, w_pair, w_third)
    end(keep, got)

    keep, got = now(keep, got)
    u, v = first_step(keep, got)
    lefts = [(now(gf_a), gf_b), (gs_a, gs_b)]
    d_late = grads_by_right(lefts, (n2_a, n2_b), cut, 2, 2)
    end(u, v, *d_late)

    d_late = now(*d_late)
    pair1 = inward_z(d_late[1])
    lefts = [(now(gf_a), gf_b), (gs_a, gs_b)]
    d_pair = [*grads_by_right(lefts, (n2_a, n2_b), cut, 0, 2), *d_late]
    to_2, to_4 = add_halves(keep, got, *now(u, v), width)
    sx, sy = to_x(to_2), to_y(to_4)
    d_third = grads_by_right([(now(turned_a), turned_b)], (g_a, g_b), cut, 0, 4)

    def join(part, more):
        return pin(plus(part, now(more)))

    end(sx, sy, pair1, *d_third, *d_pair)

    d_third = [d[0] for d in now(*d_third)]
    d_pair = now(*d_pair)
    pair2 = gather2(d_pair[2], pin(plus(d_pair[3], now(pair1))))
    grad_mid, gb = mid_back_rows((keep, got, *now(sx, sy)), out_grad, mid, branch, r_attn, dest)
    bx, by, bc = to_x(gb), to_y(gb), to_core(gb)
    o_give = sglu_last(now(prod_b), w_third)
    o_keep = sglu_last(now(prod_a), w_third)

    end(bx, by, bc, *pair2, o_keep, o_give)

    third1 = gather1(now(*d_third))
    o_got = to_core(now(o_give))
    ax, ay = now(bx, by)
    bd = to_x(ay[:h2]), to_y(ax[h2:])
    bxyc = to_core(jnp.concatenate([ax, ay]))
    bdc = to_core(jnp.concatenate(bd))
    gb_a = pin(jnp.concatenate([gb, bx, by, *bd]))
    gb_b = pin(jnp.concatenate([bc, bxyc, bdc]))
    a_pair = now(*pair2)
    ready = [
        (pin(plus(d_pair[1][m], a_pair[1][m])), pin(plus(d_pair[2][m], a_pair[0][m])))
        for m in (0, 1)
    ]
    end(third1, gb_a, gb_b, o_got, *ready[0], *ready[1])

    third2 = gather2(now(d_third[2]), join(d_third[3], third1))
    ou, ov = first_step(*now(o_keep, o_got))
    ga, gg, mixed, d_term, d_leaving = attend_back_rows(
        (now(gb_a), gb_b), w_out, (attn_a, attn_b), gate, qkv, at
    )
    end(*third2, d_leaving, ou, ov)

    first3 = gather3(*now(*ready[0]))
    d_out = grads_out(now(mixed), (gb_a, gb_b), width)
    d_entering = at.bring(now(d_leaving), True)

    def back_half(h, first, state):
        return project_back(
            h, first, raw, ga, gg, state, d_term, d_entering, w_in, width, at
        )

    gp_b, give = back_half(1, after(qkv, d_out), state_b)
    end(*first3, give, d_out)

    second3 = gather3(*now(*ready[1]))
    parts = now(d_out).reshape(2, 2, few, width)
    w_keep = jnp.where(core0, parts[:, 0], parts[:, 1])
    w_got = to_core(jnp.where(core0, parts[:, 1], parts[:, 0]))
    a_qkv, give = now(qkv, give)
    gp_a, keep = back_half(0, a_qkv, state_a)
    got = to_core(give)
    ready = join(d_third[1], third2[1]), join(d_third[2], third2[0])
    end(*second3, keep, got, w_keep, w_got, *ready)

    third3 = gather3(*now(*ready))
    keep, got = now(keep, got)
    u, v = first_step(keep, got)
    mine = (order // 2 == plan.c).astype(jnp.int32)
    d_w = grads_by_left(norm1, (now(gp_a), gp_b), 4, (*now(w_keep, w_got), mine, order % 2))
    end(u, v, *third3, *d_w)

    d_w = now(*d_w)
    w1 = gather1(d_w)
    to_2, to_4 = add_halves(keep, got, *now(u, v), width)
    sx, sy = to_x(to_2), to_y(to_4)
    sum_three = [
        total(d_pair[0][0], *now(*first3)),
        total(d_pair[0][1], *now(*second3)),
        total(d_third[0], *now(*third3)),
    ]
    sum_three = jnp.stack([v.astype(BF) for v in sum_three])
    my_three, to_three = plan.of_y(sum_three[:, :, :rows], sum_three[:, :, rows:])
    end(sx, sy, w1, my_three, to_three)

    w2 = gather2(d_w[2], join(d_w[3], w1))
    three_got = to_y(now(to_three))
    grad_norm1 = total(keep[:rows], got[:rows], *now(sx, sy))
    input_grad = grad_mid + srms_back(xf, plan.turn(grad_norm1, dest))
    summed = pin(plus(d_w[2], w2[0]))
    end(*w2, three_got, summed)

    ready = join(d_w[1], w2[1]), now(summed)
    w3 = gather3(*ready)
    to_2, to_4 = add_halves(after(o_keep, *ready), o_got, *now(ou, ov), width)
    ox, oy = to_x(to_2), to_y(to_4)
    sum_three = plan.by_y(my_three, now(three_got), 1)
    sum_pair = pin(sum_three[:2].swapaxes(1, 2)).astype(F32)
    sum_third = sum_three[2].astype(F32)
    end(*w3, ox, oy)

    sum_w = pin(total(d_w[0], *now(*w3)))
    sum_in = pin(sum_w[:deep].astype(BF)).reshape(8, few, across)
    sum_in = lax.all_to_all(sum_in, plan.tp, 0, 0, tiled=True)
    sum_out = jnp.concatenate([sum_w[deep : deep + few], sum_w[deep + few :]], axis=1)
    output = mid + plan.turn(total(o_keep[:rows], o_got[:rows], *now(ox, oy)), dest)
    return output, input_grad, sum_in, sum_out, sum_pair, sum_third


class Plain:
    def __init__(self, wide, narrow):
        self.tp = ("narrow",)
        self.fs = ("wide",)
        self.size = narrow
        self.groups = wide

    def begin(self):
        self.p = lax.axis_index("narrow")
        self.group = lax.axis_index("wide")
        self.slot_ids = jnp.arange(self.size, dtype=jnp.int32)

    def turn(self, v):
        return v

    def rows_all(self, a):
        whole = lax.all_gather(a, "narrow", axis=0, tiled=True)
        return whole[: whole.shape[0] // 2], whole[whole.shape[0] // 2 :]

    def rows_sum(self, keep, give, kind=BF):
        total = lax.psum_scatter(
            jnp.concatenate([keep, give]), "narrow", scatter_dimension=0, tiled=True
        )
        return total.astype(F32)

    def attn_in(self, w):
        rows, cols = w.shape
        each = cols // 4 // self.size
        view = w.reshape(rows, 4, self.size, each).transpose(2, 0, 1, 3)
        view = view.reshape(self.size, rows, 4 * each)
        mine = lax.all_to_all(view, "narrow", 0, 0, tiled=True)
        mine = mine.reshape(self.size * rows, 4 * each)
        return cut4(lax.all_gather(mine, "wide", axis=0, tiled=True), 0)

    def attn_in_back(self, g):
        cols = g.shape[1]
        total = lax.psum_scatter(g.astype(BF), "wide", scatter_dimension=0, tiled=True)
        rows = total.shape[0] // self.size
        view = total.reshape(self.size, rows, cols)
        mine = lax.all_to_all(view, "narrow", 0, 0, tiled=True)
        mine = mine.reshape(self.size, rows, 4, cols // 4).transpose(1, 2, 0, 3)
        return mine.reshape(rows, cols * self.size).astype(F32)

    def attn_out(self, w):
        whole = lax.all_gather(w, ("wide", "narrow"), axis=0, tiled=True)
        each = whole.shape[0] // self.size
        return lax.dynamic_slice_in_dim(whole, self.p * each, each)

    def attn_out_back(self, g):
        each = g.shape[0]
        whole = jnp.zeros((each * self.size, g.shape[1]), BF)
        whole = lax.dynamic_update_slice_in_dim(whole, g.astype(BF), self.p * each, 0)
        total = lax.psum_scatter(whole, ("wide", "narrow"), scatter_dimension=0, tiled=True)
        return total.astype(F32)

    def sglu(self, pair, third):
        return pair, third

    def sglu_all(self, both, back):
        pair = lax.all_gather(both.swapaxes(1, 2), "wide", axis=2, tiled=True)
        third = lax.all_gather(back, "wide", axis=1, tiled=True)
        return cut4(pair, 2), cut4(third, 1)

    def pair_back(self, g):
        g = jnp.concatenate([g[k] for k in range(4)], axis=2)
        total = lax.psum_scatter(g, "wide", scatter_dimension=2, tiled=True)
        return total.swapaxes(1, 2).astype(F32)

    def third_back(self, g):
        g = jnp.concatenate([g[k] for k in range(4)], axis=1)
        total = lax.psum_scatter(g, "wide", scatter_dimension=1, tiled=True)
        return total.astype(F32)


def plain_layer(plan, places, lengths, inputs, out_grad, attn_in, attn_out, sglu_in, sglu_out):
    rows, width = inputs.shape
    at = places(lengths)
    w_out = plan.attn_out(attn_out.astype(BF))
    w_in = plan.attn_in(attn_in.astype(BF))
    w_pair, w_third = plan.sglu_all(sglu_in.astype(BF), sglu_out.astype(BF))
    xf = inputs.astype(F32)
    norm1 = plan.rows_all(plan.turn((xf * inverse_rms(xf)).astype(BF)))
    grad_rows = plan.rows_all(plan.turn(out_grad))
    raw, gate, qkv, term, leaving = project(norm1, w_in, at)
    entering = at.bring(leaving, False)
    attn, branch, state = [None] * 2, [None] * 2, [None] * 2
    for h in (1, 0):
        attn[h], branch[h], state[h] = attend(h, qkv, gate, term, entering, w_out, at)
    square = plan.rows_sum(*[strip_sum(v) for v in branch], F32)
    branch = plan.rows_sum(*[v[:, :width] for v in branch])
    r_attn = lax.rsqrt(square / width + EPS)
    mid = xf + r_attn * branch
    r_mid = inverse_rms(mid)
    norm2 = plan.rows_all(plan.turn((mid * r_mid).astype(BF)))

    product, turned, grad_first, grad_second, back = [[None] * 2 for _ in range(5)]
    for h in (1, 0):
        product[h], turned[h], grad_first[h], grad_second[h], back[h] = sglu_rows(
            norm2[h], grad_rows[h], w_pair, w_third
        )
    cut = width // 4
    sum_third = plan.third_back([g[0] for g in grads_by_right([turned], grad_rows, cut, 0, 4)])
    grad_norm2 = plan.rows_sum(*back)
    sum_pair = plan.pair_back(grads_by_right([grad_first, grad_second], norm2, cut, 0, 4))

    grad_mid = out_grad.astype(F32) + srms_back(mid, plan.turn(grad_norm2))
    grad_branch = grad_mid.astype(BF)
    inward = jnp.mean(grad_branch.astype(F32) * branch, axis=1, keepdims=True)
    extra = pieces(r_attn) + pieces(r_attn * r_attn * r_attn * inward)
    extra.append(jnp.zeros((rows, 128 - len(extra)), BF))
    grad_branch = jnp.concatenate([grad_branch] + extra, axis=1)
    grad_branch = plan.rows_all(grad_branch)
    branch_out = plan.rows_sum(*[sglu_last(v, w_third) for v in product])
    output = mid + plan.turn(branch_out)
    grad_attn, grad_gate, mixed, d_term, d_leaving = attend_back_rows(
        grad_branch, w_out, attn, gate, qkv, at
    )
    d_entering = at.bring(d_leaving, True)
    grad_pre, back = [None] * 2, [None] * 2
    for h in (1, 0):
        grad_pre[h], back[h] = project_back(
            h, qkv, raw, grad_attn, grad_gate, state[h], d_term, d_entering, w_in, width, at
        )
    grad_win = jnp.concatenate(grads_by_left(norm1, grad_pre, 4))
    sum_in = plan.attn_in_back(grad_win)
    sum_out = plan.attn_out_back(grads_out(mixed, grad_branch, width))
    grad_norm1 = plan.rows_sum(*back)
    input_grad = grad_mid + srms_back(xf, plan.turn(grad_norm1))
    return output, input_grad, sum_in, sum_out, sum_pair, sum_third


def per_device(plan, layer, *args):
    inputs, out_grad, seq_lengths, decay_rate = args[:4]
    weights, moments, averages = args[4:8], args[8:12], args[12:16]
    plan.begin()
    rows, width = inputs.shape
    plan.own = decay_rate.shape[0] // plan.size

    def places(lengths):
        return Places(plan, lengths, decay_rate, rows)

    output, input_grad, *grads = layer(plan, places, seq_lengths, inputs, out_grad, *weights)
    tokens = plan.size * rows * plan.groups
    fans = (width, width, width, weights[3].shape[0] * lax.axis_size(plan.narrow))
    new = []
    for w, m, a, grad, fan in zip(weights, moments, averages, grads, fans):
        if grad.shape == w.shape:
            new.append(renew(w, m, a, grad, fan, tokens))
        else:
            new.append(renew_turned(grad, w, m, a, fan, tokens))
    return (output, input_grad) + tuple(n[i] for i in range(3) for n in new)


def solution(mesh):
    wide, narrow = mesh.shape["wide"], mesh.shape["narrow"]
    if (wide, narrow) == (8, 4):
        mesh = Mesh(mesh.devices.reshape(4, 2, 2, 2), ("z", "y", "x", "c"))
        plan, layer, w, n = Square(), square_layer, ("z", "y"), ("x", "c")
    else:
        plan, layer, w, n = Plain(wide, narrow), plain_layer, ("wide",), ("narrow",)
    plan.narrow = n
    by_rows = P(w + n, None)
    pair, third = P(None, w, n), P(n, w)
    weights = (by_rows, by_rows, pair, third)

    def run(*args):
        return per_device(plan, layer, *args)

    return jax.shard_map(
        run,
        mesh=mesh,
        in_specs=(by_rows, by_rows, P(), P()) + weights * 3,
        out_specs=(by_rows, by_rows) + weights * 3,
        check_vma=False,
    )
```
